128 devices in a mesh: frame: 16 (over z, y_hi, core), fsdp: 8 (over x, y_lo).
Axes of the slice: x: 4, y: 4 (y_hi: 2, y_lo: 2; y = y_hi * 2 + y_lo), z: 4, core: 2. Of those that a mesh axis runs over, the one named last changes fastest.
Arguments:
- hidden_states: bfloat16 [32, 512, 3072], P('frame', 'fsdp'), may hold values from -150 to 150, as said below
- teacher: bfloat16 [32, 512, 3072], P('frame', 'fsdp'), may hold values from -160 to 160
- mod_scale: float32 [3072], replicated, may hold values from -1.2 to 1.2
- mod_shift: float32 [3072], replicated, may hold values from -2 to 2
- out_gate: float32 [3072], replicated, may hold values from 0.5 to 1.5
- w_qkv: bfloat16 [3, 3072, 3072], P(None, None, 'fsdp'), may hold values from -0.109375 to 0.109375
- w_out: bfloat16 [3072, 3072], P('fsdp'), may hold values from -0.109375 to 0.109375
Outputs:
- grad_hidden: bfloat16 [32, 512, 3072], P('frame', 'fsdp')
- grad_w_qkv: bfloat16 [3, 3072, 3072], P(None, 'frame', 'fsdp')
- grad_w_out: bfloat16 [3072, 3072], P('fsdp', 'frame')
- grad_scale: float32 [3072], replicated
- grad_shift: float32 [3072], replicated
- grad_gate: float32 [3072], replicated
The draws below stay inside these ranges and needn't reach their ends.
Inputs may be any that keep to these rules, and one draw needn't show every extreme that they name: `hidden_states`: each token and each feature carries a scale of its own.
All inputs are finite; a program needn't handle non-finite values.
Results may differ from the reference program's by a relative error of at most 0.018.
Values may be sent and summed in bfloat16 or wider, within the bound.
A program may use at most 192 MiB of HBM per device.

```python
import math
import jax
import jax.numpy as jnp
from jax import lax

D = 3072
HEAD_DIM = 128
FR_DEV = 2
HW = 3072
FRAMES = 32
PATCHES = 512
N_FRAME = 16
N_FSDP = 8


def token_field(key):
    first, second, third = jax.random.split(key, 3)
    rows = jnp.exp(math.log(10.0) * jax.random.uniform(second, (FRAMES, PATCHES, 1), jnp.float32))
    columns = jnp.exp(math.log(3.0) * jax.random.uniform(third, (D,), jnp.float32))
    normal_part = jnp.clip(jax.random.normal(first, (FRAMES, PATCHES, D), jnp.float32), -4.8, 4.8)
    base = normal_part
    return (base * rows * columns).astype(jnp.bfloat16)


def draw_hidden_states(key, part):
    field = token_field(key)
    return field


def draw_teacher(key, part):
    field = token_field(key)
    key = jax.random.fold_in(key, 23)
    offset = 0.7 * jnp.clip(jax.random.normal(key, (FRAMES, PATCHES, D), jnp.float32), -4.0, 4.0)
    return (field.astype(jnp.float32) + offset).astype(jnp.bfloat16)


def block_levels(own_key, shape, shards, least, top_value):
    factor_of = 1.0
    for axis_at, shards_of in shards:
        draws = jax.random.uniform(jax.random.fold_in(jax.random.fold_in(own_key, 6), axis_at), (shards_of,), jnp.float32, least / len(shards), top_value / len(shards))
        factor_of = factor_of * jnp.repeat(jnp.exp(draws), shape[axis_at] // shards_of).reshape((-1,) + (1,) * (len(shape) - 1 - axis_at))
    return factor_of


def centred(rng, shape, scale, most, pieces=(), kind=jnp.bfloat16):
    result = jax.random.normal(rng, shape, jnp.float32) * scale
    if len(pieces) > 0:
        result = block_levels(rng, shape, pieces, -0.22, 0.18) * result
    return jnp.clip(result, min=-most, max=most).astype(kind)


def setup_inputs(seed: int = 0) -> dict:
    streams_of = jax.random.split(jax.random.key(seed), 8)
    return {
        "hidden_states": draw_hidden_states(jax.random.fold_in(streams_of[7], 71), 0),
        "teacher": draw_teacher(jax.random.fold_in(streams_of[7], 71), 0),
        "mod_scale": centred(streams_of[2], (D,), 0.3, 1.2, (), jnp.float32),
        "mod_shift": centred(streams_of[3], (D,), 0.5, 2.0, (), jnp.float32),
        "out_gate": jnp.clip(jax.random.uniform(streams_of[4], (D,), jnp.float32, 0.5, 1.5), 0.5, 1.5),
        "w_qkv": centred(streams_of[5], (3, D, HW), D ** -0.5, 0.109375, ((2, 8),)),
        "w_out": centred(streams_of[6], (HW, D), HW ** -0.5, 0.109375, ((0, 8),)),
    }


def head_norm(values):
    factor = lax.rsqrt(lax.optimization_barrier(jnp.mean(values * values, -1, keepdims=True)) + 1e-06)
    return (values * factor, factor)

def norm_back(grad_in, normed, factor):
    return factor * (grad_in - normed * lax.optimization_barrier(jnp.mean(grad_in * normed, -1, keepdims=True)))

def rounded(values):
    return lax.optimization_barrier(values.astype(jnp.bfloat16)).astype(jnp.float32)

def reference(hidden_states, teacher, mod_scale, mod_shift, out_gate, w_qkv, w_out):
    states = hidden_states.astype(jnp.float32)
    factor = lax.rsqrt(lax.optimization_barrier(jnp.mean(states * states, -1, keepdims=True)) + 1e-06)
    normed = states * factor
    modded = (normed * (1.0 + mod_scale) + mod_shift).astype(jnp.bfloat16)
    flat = modded.reshape(FRAMES * PATCHES, D)
    blocks = modded.reshape(N_FRAME, FR_DEV * PATCHES, D).astype(jnp.float32)
    local_width = HW // N_FSDP
    heads_loc = local_width // HEAD_DIM
    inv_root = HEAD_DIM ** (-0.5)
    group_qkv = jnp.transpose(w_qkv.reshape(3, D, N_FSDP, local_width), (2, 0, 1, 3))
    group_out = w_out.reshape(N_FSDP, local_width, D)

    def forward_group(weights):
        proj = [jnp.dot(flat, weights[c], preferred_element_type=jnp.float32) for c in range(3)]
        q_norm, q_fac = head_norm(proj[0].reshape(-1, heads_loc, HEAD_DIM))
        k_norm, k_fac = head_norm(proj[1].reshape(-1, heads_loc, HEAD_DIM))
        shape4 = (FRAMES, PATCHES, heads_loc, HEAD_DIM)
        q_low = q_norm.astype(jnp.bfloat16).reshape(shape4)
        k_low = k_norm.astype(jnp.bfloat16).reshape(shape4)
        v_low = proj[2].astype(jnp.bfloat16).reshape(shape4)
        scores = jnp.einsum('fphe,gphe->phfg', q_low.astype(jnp.float32), k_low.astype(jnp.float32)) * inv_root
        expo = jnp.exp(scores)
        probs = expo / lax.optimization_barrier(jnp.sum(expo, -1, keepdims=True))
        probs_low = probs.astype(jnp.bfloat16)
        attended = jnp.einsum('phfg,gphe->fphe', probs_low.astype(jnp.float32), v_low.astype(jnp.float32)).astype(jnp.bfloat16)
        return (q_norm, q_fac, k_norm, k_fac, q_low, k_low, v_low, probs, probs_low, attended.reshape(-1, local_width))

    def step_forward(total, pair):
        attended = forward_group(pair[0])[-1]
        return (total + rounded(jnp.dot(attended, pair[1], preferred_element_type=jnp.float32)), None)
    mixed, _ = lax.scan(step_forward, jnp.zeros((FRAMES * PATCHES, D), jnp.float32), (group_qkv, group_out))
    mixed = mixed.reshape(FRAMES, PATCHES, D)
    diff = states + out_gate * mixed - teacher.astype(jnp.float32)
    upstream = (out_gate * diff).astype(jnp.bfloat16)
    up_flat = upstream.reshape(-1, D)
    up_blocks = upstream.reshape(N_FRAME, -1, D).astype(jnp.float32)

    def step_backward(total, pair):
        weights, out_rows = pair
        q_norm, q_fac, k_norm, k_fac, q_low, k_low, v_low, probs, probs_low, attended = forward_group(weights)
        out_grad = lax.optimization_barrier(jnp.sum(rounded(jnp.einsum('nth,ntd->nhd', attended.reshape(N_FRAME, -1, local_width).astype(jnp.float32), up_blocks)), 0))
        dattn = jnp.dot(up_flat, out_rows.T, preferred_element_type=jnp.float32).astype(jnp.bfloat16)
        dattn = dattn.reshape(FRAMES, PATCHES, heads_loc, HEAD_DIM).astype(jnp.float32)
        dprob = jnp.einsum('fphe,gphe->phfg', dattn, v_low.astype(jnp.float32))
        dval = jnp.einsum('phfg,fphe->gphe', probs_low.astype(jnp.float32), dattn).astype(jnp.bfloat16)
        dscore = (probs * (dprob - lax.optimization_barrier(jnp.sum(probs * dprob, -1, keepdims=True)))).astype(jnp.bfloat16).astype(jnp.float32)
        dquery = (jnp.einsum('phfg,gphe->fphe', dscore, k_low.astype(jnp.float32)) * inv_root).astype(jnp.bfloat16)
        dkey = (jnp.einsum('phfg,fphe->gphe', dscore, q_low.astype(jnp.float32)) * inv_root).astype(jnp.bfloat16)
        grad_q = norm_back(dquery.reshape(-1, heads_loc, HEAD_DIM).astype(jnp.float32), q_norm, q_fac).astype(jnp.bfloat16)
        grad_k = norm_back(dkey.reshape(-1, heads_loc, HEAD_DIM).astype(jnp.float32), k_norm, k_fac).astype(jnp.bfloat16)
        dproj = [grad_q.reshape(-1, local_width), grad_k.reshape(-1, local_width), dval.reshape(-1, local_width)]
        qkv_grad = jnp.stack([lax.optimization_barrier(jnp.sum(rounded(jnp.einsum('ntd,nth->ndh', blocks, piece.reshape(N_FRAME, -1, local_width).astype(jnp.float32))), 0)) for piece in dproj])
        term = jnp.dot(dproj[0], weights[0].T, preferred_element_type=jnp.float32)
        term = term + jnp.dot(dproj[1], weights[1].T, preferred_element_type=jnp.float32)
        term = term + jnp.dot(dproj[2], weights[2].T, preferred_element_type=jnp.float32)
        return (total + rounded(term), (qkv_grad, out_grad))
    dmod, grads = lax.scan(step_backward, jnp.zeros((FRAMES * PATCHES, D), jnp.float32), (group_qkv, group_out))
    grad_w_qkv = jnp.transpose(grads[0], (1, 2, 0, 3)).reshape(3, D, HW).astype(jnp.bfloat16)
    grad_w_out = grads[1].reshape(HW, D).astype(jnp.bfloat16)
    dmod = dmod.reshape(FRAMES, PATCHES, D)
    grad_scale = lax.optimization_barrier(jnp.sum(dmod * normed, (0, 1)))
    grad_shift = lax.optimization_barrier(jnp.sum(dmod, (0, 1)))
    grad_gate = lax.optimization_barrier(jnp.sum(diff * mixed, (0, 1)))
    dnorm = dmod * (1.0 + mod_scale)
    grad_hidden = (diff + factor * (dnorm - normed * lax.optimization_barrier(jnp.mean(dnorm * normed, -1, keepdims=True)))).astype(jnp.bfloat16)
    return (grad_hidden, grad_w_qkv, grad_w_out, grad_scale, grad_shift, grad_gate)
```

```python
import functools
import jax
import jax.numpy as jnp
from jax import lax
from jax.experimental import pallas as pl
from jax.experimental.pallas import tpu as pltpu
from jax.sharding import PartitionSpec as P

HEAD_DIM = 128
HEADS = 3
LOCAL = 384
WIDTH = 3072
HALF = 64
TILE = 512
INV_ROOT = HEAD_DIM ** (-0.5)
MESH = pl.DeviceIdType.MESH
BF = jnp.bfloat16
F32 = jnp.float32
VMEM_BYTES = 60 * 1024 * 1024


class Place:
    def __init__(self):
        fr = lax.axis_index("frame")
        fs = lax.axis_index("fsdp")
        self.fr = fr
        self.fs = fs
        self.x = lax.div(fs, 2)
        self.lo = lax.rem(fs, 2)
        self.core = lax.rem(fr, 2)
        self.group = lax.div(fr, 2)
        other = fs + 1 - 2 * self.lo
        hi = lax.rem(self.group, 2)
        self.right = (fr, lax.rem(fs + 2, 8))
        self.left = (fr, lax.rem(fs + 6, 8))
        self.side = ((fr, other), (fr + 2 - 4 * hi, other))

    def along(self, off):
        return lax.rem(self.x + off, 4)

    def meet(self):
        barrier = pltpu.get_barrier_semaphore()
        for peer in (self.right, self.left) + self.side:
            pl.semaphore_signal(barrier, inc=1, device_id=peer, device_id_type=MESH)

        def greet(step, carry):
            pl.semaphore_signal(
                barrier,
                inc=1,
                device_id=(lax.rem(self.fr + step, 16), self.fs),
                device_id_type=MESH,
            )
            return carry

        lax.fori_loop(1, 16, greet, 0)
        pl.semaphore_wait(barrier, 19)


def remote(src, dst, send_sem, recv_sem, device):
    return pltpu.make_async_remote_copy(
        src_ref=src,
        dst_ref=dst,
        send_sem=send_sem,
        recv_sem=recv_sem,
        device_id=device,
        device_id_type=MESH,
    )


def landed(ref, sem):
    pltpu.make_async_copy(ref, ref, sem).wait()


def loop(count, body):
    def step(i, carry):
        body(i)
        return carry

    lax.fori_loop(0, count, step, 0)


def near_first(p):
    return 3 * p - lax.div(5 * p * (p - 1), 2) + lax.div(4 * p * (p - 1) * (p - 2), 3)


def far_first(p):
    return 2 - p + lax.div(3 * p * (p - 1), 2) - lax.div(4 * p * (p - 1) * (p - 2), 3)


def gather_kernel(project, own, w_hbm, *refs):
    if project:
        full, sent_to, factors, weight, out, x_send, y_send, recv, o_send, o_recv, w_sem = refs
    else:
        full, sent_to, weight, out, x_send, y_send, recv, o_send, o_recv, w_sem = refs
    at = Place()
    if project:
        w_copies = [
            pltpu.make_async_copy(
                w_hbm.at[c], weight.at[:, pl.ds(c * LOCAL, LOCAL)], w_sem.at[c]
            )
            for c in range(3)
        ]
    else:
        w_copies = [pltpu.make_async_copy(w_hbm, weight, w_sem.at[0])]
    for copy in w_copies:
        copy.start()
    at.meet()

    def to_right(src, xi, h, n):
        return remote(src, full.at[0, xi, h], x_send.at[n], recv.at[0, xi, h], at.right)

    def to_left(src, xi, h, n):
        return remote(src, full.at[0, xi, h], x_send.at[n], recv.at[0, xi, h], at.left)

    def to_side(src, xi, h, n):
        return remote(src, full.at[1, xi, h], y_send.at[n], recv.at[1, xi, h], at.side[h])

    xl, xr, xf = at.along(3), at.along(1), at.along(2)
    first = [
        to_right(own.at[0], at.x, 0, 0),
        to_left(own.at[1], at.x, 1, 1),
        to_side(own.at[0], at.x, 0, 0),
        to_side(own.at[1], at.x, 1, 1),
        to_right(own.at[1], at.x, 1, 2),
        to_left(own.at[0], at.x, 0, 3),
    ]
    for copy in first:
        copy.start()
    full[0, at.x] = own[...]
    fwd = [
        to_right(full.at[0, xl, 0], xl, 0, 4),
        to_left(full.at[0, xr, 1], xr, 1, 5),
        to_side(full.at[0, xl, 0], xl, 0, 2),
        to_side(full.at[0, xl, 1], xl, 1, 3),
        to_side(full.at[0, xr, 0], xr, 0, 4),
        to_side(full.at[0, xr, 1], xr, 1, 5),
        to_side(full.at[0, xf, 0], xf, 0, 6),
        to_side(full.at[0, xf, 1], xf, 1, 7),
    ]
    for copy in w_copies:
        copy.wait()

    def arrived(slot, xi, h):
        landed(full.at[slot, xi, h], recv.at[slot, xi, h])

    def step(k):
        slot = lax.div(k, 4)
        xi = at.along(near_first(lax.rem(k, 4)))

        @pl.when(k == 1)
        def _():
            arrived(0, xl, 0)
            fwd[0].start()
            fwd[2].start()
            arrived(0, xr, 1)
            fwd[1].start()
            fwd[5].start()
            arrived(0, xl, 1)
            fwd[3].start()

        @pl.when(k == 2)
        def _():
            arrived(0, xr, 0)
            fwd[4].start()

        @pl.when(k == 3)
        def _():
            arrived(0, xf, 0)
            fwd[6].start()
            arrived(0, xf, 1)
            fwd[7].start()

        @pl.when(k >= 4)
        def _():
            arrived(1, xi, 0)
            arrived(1, xi, 1)

        tokens = full[slot, xi].reshape(2 * HALF, WIDTH)
        if project:
            both = jnp.dot(tokens, weight[...], preferred_element_type=F32)
            lane = lax.broadcasted_iota(jnp.int32, (2 * HALF, HEAD_DIM), 1)
            kept = jnp.zeros((2 * HALF, HEAD_DIM), F32)
            for j in range(3 * HEADS):
                block = both[:, j * HEAD_DIM : (j + 1) * HEAD_DIM]
                if j < 2 * HEADS:
                    factor = lax.rsqrt(jnp.mean(block * block, -1, keepdims=True) + 1e-06)
                    kept = jnp.where(lane == j, factor, kept)
                    block = block * factor
                out[k, :, :, j * HEAD_DIM : (j + 1) * HEAD_DIM] = block.astype(BF).reshape(
                    8, 16, HEAD_DIM
                )
            factors[slot, xi] = kept
        else:
            both = lax.dot_general(
                tokens, weight[...], (((1,), (1,)), ((), ())), preferred_element_type=F32
            )
            out[k] = both.astype(BF).reshape(8, 16, LOCAL)
        to_core = lax.rem(xi, 2)
        to_slot = 2 * lax.div(xi, 2) + lax.rem(at.lo + slot, 2)

        def give(g):
            target = 2 * g + to_core
            src = out.at[k, g]
            dst = sent_to.at[to_slot, at.fr]

            @pl.when(target == at.fr)
            def _():
                pltpu.make_async_copy(src, dst, o_recv.at[to_slot]).start()

            @pl.when(target != at.fr)
            def _():
                remote(src, dst, o_send.at[g], o_recv.at[to_slot], (target, at.fs)).start()

        loop(8, give)

    loop(8, step)

    for copy in first + fwd:
        copy.wait_send()

    def drain(g):
        @pl.when(g == at.group)
        def _():
            landed(out.at[pl.ds(0, 4), g], o_send.at[g])

        @pl.when(g != at.group)
        def _():
            landed(out.at[:, g], o_send.at[g])

    loop(8, drain)
    loop(4, lambda t: landed(sent_to.at[t], o_recv.at[t]))


def vmem(count):
    return [pl.BlockSpec(memory_space=pltpu.VMEM)] * count


def gather(own, weight, project):
    cols = 3 * LOCAL if project else LOCAL
    shapes = [
        jax.ShapeDtypeStruct((2, 4, 2, HALF, WIDTH), BF),
        jax.ShapeDtypeStruct((4, 16, 16, cols), BF),
    ]
    if project:
        shapes.append(jax.ShapeDtypeStruct((2, 4, 2 * HALF, HEAD_DIM), F32))
    flops = 2 * 1024 * WIDTH * cols
    return pl.pallas_call(
        functools.partial(gather_kernel, project),
        out_shape=shapes,
        in_specs=[pl.BlockSpec(memory_space=pltpu.VMEM), pl.BlockSpec(memory_space=pl.ANY)],
        out_specs=vmem(len(shapes)),
        scratch_shapes=[
            pltpu.VMEM((WIDTH, cols) if project else (LOCAL, WIDTH), BF),
            pltpu.VMEM((8, 8, 16, cols), BF),
            pltpu.SemaphoreType.DMA((6,)),
            pltpu.SemaphoreType.DMA((8,)),
            pltpu.SemaphoreType.DMA((2, 4, 2)),
            pltpu.SemaphoreType.DMA((8,)),
            pltpu.SemaphoreType.DMA((4,)),
            pltpu.SemaphoreType.DMA((3,)),
        ],
        compiler_params=pltpu.CompilerParams(
            collective_id=0 if project else 2,
            has_side_effects=True,
            vmem_limit_bytes=VMEM_BYTES,
        ),
        cost_estimate=pl.CostEstimate(flops=flops, bytes_accessed=30_000_000, transcendentals=0),
        name="gather_project" if project else "gather_back",
    )(own, weight)


def same_patch():
    rows = lax.broadcasted_iota(jnp.int32, (256, 256), 0)
    cols = lax.broadcasted_iota(jnp.int32, (256, 256), 1)
    return lax.rem(rows, 8) == lax.rem(cols, 8)


def dot_nt(a, b):
    return lax.dot_general(a, b, (((1,), (1,)), ((), ())), preferred_element_type=F32)


def dot_tn(a, b):
    return lax.dot_general(a, b, (((0,), (0,)), ((), ())), preferred_element_type=F32)


def softmax(query, key):
    scores = dot_nt(query, key) * INV_ROOT
    expo = jnp.where(same_patch(), jnp.exp(scores), 0.0)
    return expo / jnp.sum(expo, -1, keepdims=True)


def scatter_kernel(back, *refs):
    if back:
        qkv, grad, factors, w_hbm, total, tokens, dproj = refs[:7]
        refs = refs[7:]
    else:
        qkv, w_hbm, total, tokens = refs[:4]
        refs = refs[4:]
    (
        weight, out, part, mine, from_side, far, near,
        o_send, o_recv, y_send, y_recv, f_send, f_recv, n_send, n_recv, w_sem,
    ) = refs
    at = Place()
    if back:
        w_copies = [
            pltpu.make_async_copy(
                w_hbm.at[c], weight.at[:, pl.ds(c * LOCAL, LOCAL)], w_sem.at[c]
            )
            for c in range(3)
        ]
    else:
        w_copies = [pltpu.make_async_copy(w_hbm, weight, w_sem.at[0])]
    for copy in w_copies:
        copy.start()
    at.meet()

    def columns(ref, t, block):
        return ref[t, :, :, block * HEAD_DIM : (block + 1) * HEAD_DIM].reshape(256, HEAD_DIM)

    def put(i, block, value):
        out[i, :, :, block * HEAD_DIM : (block + 1) * HEAD_DIM] = value.astype(BF).reshape(
            16, 16, HEAD_DIM
        )

    def attend(i):
        slot = 1 - lax.div(i, 2)
        xh = lax.rem(i, 2)
        t = 2 * xh + lax.rem(at.lo + slot, 2)
        for h in range(HEADS):
            query, key, value = (columns(qkv, t, c * HEADS + h) for c in range(3))
            probs = softmax(query, key)
            low = probs.astype(BF)
            if not back:
                put(i, h, jnp.dot(low, value, preferred_element_type=F32))
                continue
            grad_in = columns(grad, t, h)
            dprob = dot_nt(grad_in, value)
            put(i, 2 * HEADS + h, dot_tn(low, grad_in))
            dscore = (probs * (dprob - jnp.sum(probs * dprob, -1, keepdims=True))).astype(BF)
            for c, normed, product in (
                (0, query, jnp.dot(dscore, key, preferred_element_type=F32)),
                (1, key, dot_tn(dscore, query)),
            ):
                step_in = (product * INV_ROOT).astype(BF).astype(F32)
                wide = normed.astype(F32)
                put(
                    i,
                    c * HEADS + h,
                    step_in - wide * jnp.mean(step_in * wide, -1, keepdims=True),
                )
        xi = 2 * xh + at.core

        def give(f):
            src = out.at[i, f]
            dst = tokens.at[slot, xi, at.group]

            @pl.when(f == at.fr)
            def _():
                pltpu.make_async_copy(src, dst, o_recv.at[slot, xi]).start()

            @pl.when(f != at.fr)
            def _():
                remote(src, dst, o_send.at[i], o_recv.at[slot, xi], (f, at.fs)).start()

        loop(16, give)

    loop(4, attend)
    for copy in w_copies:
        copy.wait()

    def product(slot, xi, j):
        tile = pl.ds(pl.multiple_of(j * TILE, TILE), TILE)
        if back:
            return tile, dot_nt(dproj[slot, xi], weight[tile, :])
        rows = tokens[slot, xi].reshape(2 * HALF, LOCAL)
        return tile, jnp.dot(rows, weight[:, tile], preferred_element_type=F32)

    def take(slot, xi):
        landed(tokens.at[slot, xi], o_recv.at[slot, xi])
        if back:
            for j in range(3 * HEADS):
                cols = slice(j * HEAD_DIM, (j + 1) * HEAD_DIM)
                block = tokens[slot, xi, :, :, cols].reshape(2 * HALF, HEAD_DIM)
                if j < 2 * HEADS:
                    block = (block.astype(F32) * factors[slot, xi, :, j : j + 1]).astype(BF)
                dproj[slot, xi, :, cols] = block

    def first(n):
        xi = at.along(far_first(n))
        take(1, xi)

        def tiles(j):
            tile, value = product(1, xi, j)
            part[xi, :, :, tile] = value.astype(BF).reshape(2, HALF, TILE)

        loop(WIDTH // TILE, tiles)
        for h in range(2):
            remote(
                part.at[xi, h], from_side.at[xi, h], y_send.at[xi, h], y_recv.at[xi, h], at.side[h]
            ).start()

    loop(4, first)

    xl, xr, xf = at.along(3), at.along(1), at.along(2)
    far_copies = [
        remote(mine.at[xf, 0], far.at[0], f_send.at[0], f_recv.at[0], at.right),
        remote(mine.at[xf, 1], far.at[1], f_send.at[1], f_recv.at[1], at.left),
    ]
    near_copies = [
        remote(mine.at[xr, 1], near.at[0, 1], n_send.at[0, 1], n_recv.at[0, 1], at.right),
        remote(mine.at[xl, 0], near.at[1, 0], n_send.at[1, 0], n_recv.at[1, 0], at.left),
        remote(mine.at[xr, 0], near.at[0, 0], n_send.at[0, 0], n_recv.at[0, 0], at.right),
        remote(mine.at[xl, 1], near.at[1, 1], n_send.at[1, 1], n_recv.at[1, 1], at.left),
    ]

    def second(n):
        xi = at.along(far_first(n))
        take(0, xi)
        for h in range(2):
            landed(from_side.at[xi, h], y_recv.at[xi, h])

        def tiles(j):
            tile, value = product(0, xi, j)
            other = from_side[xi, :, :, tile].astype(F32).reshape(2 * HALF, TILE)
            mine[xi, :, :, tile] = (value + other).astype(BF).reshape(2, HALF, TILE)

        loop(WIDTH // TILE, tiles)

        @pl.when(n == 0)
        def _():
            far_copies[0].start()
            far_copies[1].start()

        @pl.when(n == 1)
        def _():
            near_copies[0].start()

        @pl.when(n == 2)
        def _():
            near_copies[1].start()

    loop(4, second)
    for d, xi in ((0, xr), (1, xl)):
        landed(far.at[d], f_recv.at[d])

        def tiles(j, d=d, xi=xi):
            tile = pl.ds(pl.multiple_of(j * TILE, TILE), TILE)
            mine[xi, d, :, tile] = (
                mine[xi, d, :, tile].astype(F32) + far[d, :, tile].astype(F32)
            ).astype(BF)

        loop(WIDTH // TILE, tiles)
        near_copies[2 + d].start()
    for d, h in ((0, 1), (1, 0), (0, 0), (1, 1)):
        landed(near.at[d, h], n_recv.at[d, h])

    def finish(j):
        tile = pl.ds(pl.multiple_of(j * TILE, TILE), TILE)
        for h in range(2):
            total[h * HALF : (h + 1) * HALF, tile] = (
                mine[at.x, h, :, tile].astype(F32)
                + near[0, h, :, tile].astype(F32)
                + near[1, h, :, tile].astype(F32)
            )

    loop(WIDTH // TILE, finish)
    for copy in far_copies + near_copies:
        copy.wait_send()
    for xi in range(4):
        for h in range(2):
            landed(part.at[xi, h], y_send.at[xi, h])

    loop(4, lambda i: landed(out.at[i, pl.ds(0, 15)], o_send.at[i]))


def scatter(args, weight, back):
    cols = 3 * LOCAL if back else LOCAL
    shapes = [
        jax.ShapeDtypeStruct((2 * HALF, WIDTH), F32),
        jax.ShapeDtypeStruct((2, 4, 8, 16, cols), BF),
    ]
    if back:
        shapes.append(jax.ShapeDtypeStruct((2, 4, 2 * HALF, cols), BF))
    return pl.pallas_call(
        functools.partial(scatter_kernel, back),
        out_shape=shapes,
        in_specs=vmem(len(args)) + [pl.BlockSpec(memory_space=pl.ANY)],
        out_specs=vmem(len(shapes)),
        scratch_shapes=[
            pltpu.VMEM((WIDTH, cols) if back else (LOCAL, WIDTH), BF),
            pltpu.VMEM((4, 16, 16, cols), BF),
            pltpu.VMEM((4, 2, HALF, WIDTH), BF),
            pltpu.VMEM((4, 2, HALF, WIDTH), BF),
            pltpu.VMEM((4, 2, HALF, WIDTH), BF),
            pltpu.VMEM((2, HALF, WIDTH), BF),
            pltpu.VMEM((2, 2, HALF, WIDTH), BF),
            pltpu.SemaphoreType.DMA((4,)),
            pltpu.SemaphoreType.DMA((2, 4)),
            pltpu.SemaphoreType.DMA((4, 2)),
            pltpu.SemaphoreType.DMA((4, 2)),
            pltpu.SemaphoreType.DMA((2,)),
            pltpu.SemaphoreType.DMA((2,)),
            pltpu.SemaphoreType.DMA((2, 2)),
            pltpu.SemaphoreType.DMA((2, 2)),
            pltpu.SemaphoreType.DMA((3,)),
        ],
        compiler_params=pltpu.CompilerParams(
            collective_id=3 if back else 1,
            has_side_effects=True,
            vmem_limit_bytes=VMEM_BYTES,
        ),
        cost_estimate=pl.CostEstimate(
            flops=2 * 1024 * WIDTH * cols, bytes_accessed=30_000_000, transcendentals=0
        ),
        name="scatter_back" if back else "scatter_mixed",
    )(*args, weight)


def to_rows(block):
    frames, patches, width = block.shape
    return block.reshape(frames, 8, 8, width).transpose(1, 0, 2, 3).reshape(-1, width)


def from_rows(rows):
    return rows.reshape(8, 2, 8, -1).transpose(1, 0, 2, 3).reshape(2, 64, -1)


def shards(hidden_states, teacher, mod_scale, mod_shift, out_gate, w_qkv, w_out):
    states = to_rows(hidden_states).astype(F32)
    factor = lax.rsqrt(jnp.mean(states * states, -1, keepdims=True) + 1e-06)
    normed = states * factor
    modded = (normed * (1.0 + mod_scale) + mod_shift).astype(BF)
    flat, qkv, factors = gather(modded.reshape(2, HALF, WIDTH), w_qkv, True)
    mixed, attended = scatter([qkv], w_out, False)
    diff = states + out_gate * mixed - to_rows(teacher).astype(F32)
    upstream = (out_gate * diff).astype(BF)
    up_all, grad_att = gather(upstream.reshape(2, HALF, WIDTH), w_out, False)
    out_grad_local = lax.dot_general(
        attended.reshape(1024, LOCAL),
        up_all.reshape(1024, WIDTH),
        (((0,), (0,)), ((), ())),
        preferred_element_type=F32,
    )
    out_grad = lax.psum_scatter(
        out_grad_local.astype(BF), "frame", scatter_dimension=1, tiled=True
    )
    dmod, _, dproj = scatter([qkv, grad_att, factors], w_qkv, True)
    qkv_grad_local = jnp.einsum(
        "td,tch->cdh",
        flat.reshape(1024, WIDTH),
        dproj.reshape(1024, 3, LOCAL),
        preferred_element_type=F32,
    )
    qkv_grad = lax.psum_scatter(
        qkv_grad_local.astype(BF), "frame", scatter_dimension=1, tiled=True
    )
    sums = lax.psum(
        (jnp.sum(dmod * normed, 0), jnp.sum(dmod, 0), jnp.sum(diff * mixed, 0)),
        ("frame", "fsdp"),
    )
    dnorm = dmod * (1.0 + mod_scale)
    grad_hidden = (
        diff + factor * (dnorm - normed * jnp.mean(dnorm * normed, -1, keepdims=True))
    ).astype(BF)
    return (from_rows(grad_hidden), qkv_grad, out_grad, sums[0], sums[1], sums[2])


def solution(mesh):
    in_specs = (
        P("frame", "fsdp", None),
        P("frame", "fsdp", None),
        P(),
        P(),
        P(),
        P(None, None, "fsdp"),
        P("fsdp", None),
    )
    out_specs = (
        P("frame", "fsdp", None),
        P(None, "frame", "fsdp"),
        P("fsdp", "frame"),
        P(),
        P(),
        P(),
    )
    return jax.shard_map(shards, mesh=mesh, in_specs=in_specs, out_specs=out_specs, check_vma=False)
```

```python
import functools
import jax
import jax.numpy as jnp
from jax import lax
from jax.experimental import pallas as pl
from jax.experimental.pallas import tpu as pltpu
from jax.sharding import PartitionSpec as P

HEAD_DIM = 128
HEADS = 3
LOCAL = 384
WIDTH = 3072
HALF = 64
TILE = 512
INV_ROOT = HEAD_DIM ** (-0.5)
MESH = pl.DeviceIdType.MESH
BF = jnp.bfloat16
F32 = jnp.float32
VMEM_BYTES = 60 * 1024 * 1024


class Place:
    def __init__(self):
        fr = lax.axis_index("frame")
        fs = lax.axis_index("fsdp")
        self.fr = fr
        self.fs = fs
        self.x = lax.div(fs, 2)
        self.lo = lax.rem(fs, 2)
        self.core = lax.rem(fr, 2)
        self.group = lax.div(fr, 2)
        other = fs + 1 - 2 * self.lo
        hi = lax.rem(self.group, 2)
        self.right = (fr, lax.rem(fs + 2, 8))
        self.left = (fr, lax.rem(fs + 6, 8))
        self.side = ((fr, other), (fr + 2 - 4 * hi, other))

    def along(self, off):
        return lax.rem(self.x + off, 4)

    def meet(self):
        barrier = pltpu.get_barrier_semaphore()
        for peer in (self.right, self.left) + self.side:
            pl.semaphore_signal(barrier, inc=1, device_id=peer, device_id_type=MESH)

        def greet(step, carry):
            pl.semaphore_signal(
                barrier,
                inc=1,
                device_id=(lax.rem(self.fr + step, 16), self.fs),
                device_id_type=MESH,
            )
            return carry

        lax.fori_loop(1, 16, greet, 0)
        pl.semaphore_wait(barrier, 19)


def remote(src, dst, send_sem, recv_sem, device):
    return pltpu.make_async_remote_copy(
        src_ref=src,
        dst_ref=dst,
        send_sem=send_sem,
        recv_sem=recv_sem,
        device_id=device,
        device_id_type=MESH,
    )


def landed(ref, sem):
    pltpu.make_async_copy(ref, ref, sem).wait()


def loop(count, body):
    def step(i, carry):
        body(i)
        return carry

    lax.fori_loop(0, count, step, 0)


def near_first(p):
    return 3 * p - lax.div(5 * p * (p - 1), 2) + lax.div(4 * p * (p - 1) * (p - 2), 3)


def far_first(p):
    return 2 - p + lax.div(3 * p * (p - 1), 2) - lax.div(4 * p * (p - 1) * (p - 2), 3)


def gather_kernel(project, own, w_hbm, *refs):
    if project:
        full, sent_to, factors, weight, out, x_send, y_send, recv, o_send, o_recv, w_sem = refs
    else:
        full, sent_to, weight, out, x_send, y_send, recv, o_send, o_recv, w_sem = refs
    at = Place()
    if project:
        w_copies = [
            pltpu.make_async_copy(
                w_hbm.at[c], weight.at[:, pl.ds(c * LOCAL, LOCAL)], w_sem.at[c]
            )
            for c in range(3)
        ]
    else:
        w_copies = [pltpu.make_async_copy(w_hbm, weight, w_sem.at[0])]
    for copy in w_copies:
        copy.start()
    at.meet()

    def to_right(src, xi, h, n):
        return remote(src, full.at[0, xi, h], x_send.at[n], recv.at[0, xi, h], at.right)

    def to_left(src, xi, h, n):
        return remote(src, full.at[0, xi, h], x_send.at[n], recv.at[0, xi, h], at.left)

    def to_side(src, xi, h, n):
        return remote(src, full.at[1, xi, h], y_send.at[n], recv.at[1, xi, h], at.side[h])

    xl, xr, xf = at.along(3), at.along(1), at.along(2)
    first = [
        to_right(own.at[0], at.x, 0, 0),
        to_left(own.at[1], at.x, 1, 1),
        to_side(own.at[0], at.x, 0, 0),
        to_side(own.at[1], at.x, 1, 1),
        to_right(own.at[1], at.x, 1, 2),
        to_left(own.at[0], at.x, 0, 3),
    ]
    for copy in first:
        copy.start()
    full[0, at.x] = own[...]
    fwd = [
        to_right(full.at[0, xl, 0], xl, 0, 4),
        to_left(full.at[0, xr, 1], xr, 1, 5),
        to_side(full.at[0, xl, 0], xl, 0, 2),
        to_side(full.at[0, xl, 1], xl, 1, 3),
        to_side(full.at[0, xr, 0], xr, 0, 4),
        to_side(full.at[0, xr, 1], xr, 1, 5),
        to_side(full.at[0, xf, 0], xf, 0, 6),
        to_side(full.at[0, xf, 1], xf, 1, 7),
    ]
    for copy in w_copies:
        copy.wait()

    def arrived(slot, xi, h):
        landed(full.at[slot, xi, h], recv.at[slot, xi, h])

    def step(k):
        slot = lax.div(k, 4)
        xi = at.along(near_first(lax.rem(k, 4)))

        @pl.when(k == 1)
        def _():
            arrived(0, xl, 0)
            fwd[0].start()
            fwd[2].start()
            arrived(0, xr, 1)
            fwd[1].start()
            fwd[5].start()
            arrived(0, xl, 1)
            fwd[3].start()

        @pl.when(k == 2)
        def _():
            arrived(0, xr, 0)
            fwd[4].start()

        @pl.when(k == 3)
        def _():
            arrived(0, xf, 0)
            fwd[6].start()
            arrived(0, xf, 1)
            fwd[7].start()

        @pl.when(k >= 4)
        def _():
            arrived(1, xi, 0)
            arrived(1, xi, 1)

        tokens = full[slot, xi].reshape(2 * HALF, WIDTH)
        if project:
            both = jnp.dot(tokens, weight[...], preferred_element_type=F32)
            lane = lax.broadcasted_iota(jnp.int32, (2 * HALF, HEAD_DIM), 1)
            kept = jnp.zeros((2 * HALF, HEAD_DIM), F32)
            for j in range(3 * HEADS):
                block = both[:, j * HEAD_DIM : (j + 1) * HEAD_DIM]
                if j < 2 * HEADS:
                    factor = lax.rsqrt(jnp.mean(block * block, -1, keepdims=True) + 1e-06)
                    kept = jnp.where(lane == j, factor, kept)
                    block = block * factor
                out[k, :, :, j * HEAD_DIM : (j + 1) * HEAD_DIM] = block.astype(BF).reshape(
                    8, 16, HEAD_DIM
                )
            factors[slot, xi] = kept
        else:
            both = lax.dot_general(
                tokens, weight[...], (((1,), (1,)), ((), ())), preferred_element_type=F32
            )
            out[k] = both.astype(BF).reshape(8, 16, LOCAL)
        to_core = lax.rem(xi, 2)
        to_slot = 2 * lax.div(xi, 2) + lax.rem(at.lo + slot, 2)

        def give(g):
            target = 2 * g + to_core
            src = out.at[k, g]
            dst = sent_to.at[to_slot, at.fr]

            @pl.when(target == at.fr)
            def _():
                pltpu.make_async_copy(src, dst, o_recv.at[to_slot]).start()

            @pl.when(target != at.fr)
            def _():
                remote(src, dst, o_send.at[g], o_recv.at[to_slot], (target, at.fs)).start()

        loop(8, give)

    loop(8, step)

    for copy in first + fwd:
        copy.wait_send()

    def drain(g):
        @pl.when(g == at.group)
        def _():
            landed(out.at[pl.ds(0, 4), g], o_send.at[g])

        @pl.when(g != at.group)
        def _():
            landed(out.at[:, g], o_send.at[g])

    loop(8, drain)
    loop(4, lambda t: landed(sent_to.at[t], o_recv.at[t]))


def vmem(count):
    return [pl.BlockSpec(memory_space=pltpu.VMEM)] * count


def gather(own, weight, project):
    cols = 3 * LOCAL if project else LOCAL
    shapes = [
        jax.ShapeDtypeStruct((2, 4, 2, HALF, WIDTH), BF),
        jax.ShapeDtypeStruct((4, 16, 16, cols), BF),
    ]
    if project:
        shapes.append(jax.ShapeDtypeStruct((2, 4, 2 * HALF, HEAD_DIM), F32))
    flops = 2 * 1024 * WIDTH * cols
    return pl.pallas_call(
        functools.partial(gather_kernel, project),
        out_shape=shapes,
        in_specs=[pl.BlockSpec(memory_space=pltpu.VMEM), pl.BlockSpec(memory_space=pl.ANY)],
        out_specs=vmem(len(shapes)),
        scratch_shapes=[
            pltpu.VMEM((WIDTH, cols) if project else (LOCAL, WIDTH), BF),
            pltpu.VMEM((8, 8, 16, cols), BF),
            pltpu.SemaphoreType.DMA((6,)),
            pltpu.SemaphoreType.DMA((8,)),
            pltpu.SemaphoreType.DMA((2, 4, 2)),
            pltpu.SemaphoreType.DMA((8,)),
            pltpu.SemaphoreType.DMA((4,)),
            pltpu.SemaphoreType.DMA((3,)),
        ],
        compiler_params=pltpu.CompilerParams(
            collective_id=0 if project else 2,
            has_side_effects=True,
            vmem_limit_bytes=VMEM_BYTES,
        ),
        cost_estimate=pl.CostEstimate(flops=flops, bytes_accessed=30_000_000, transcendentals=0),
        name="gather_project" if project else "gather_back",
    )(own, weight)


def same_patch():
    rows = lax.broadcasted_iota(jnp.int32, (256, 256), 0)
    cols = lax.broadcasted_iota(jnp.int32, (256, 256), 1)
    return lax.rem(rows, 8) == lax.rem(cols, 8)


def dot_nt(a, b):
    return lax.dot_general(a, b, (((1,), (1,)), ((), ())), preferred_element_type=F32)


def dot_tn(a, b):
    return lax.dot_general(a, b, (((0,), (0,)), ((), ())), preferred_element_type=F32)


def softmax(query, key):
    scores = dot_nt(query, key) * INV_ROOT
    expo = jnp.where(same_patch(), jnp.exp(scores), 0.0)
    return expo / jnp.sum(expo, -1, keepdims=True)


class WeightSums:
    def __init__(self, at, flat, up_all, attended, dproj, result, *scratch):
        self.at = at
        self.flat, self.up_all, self.attended, self.dproj = flat, up_all, attended, dproj
        self.result = result
        (
            self.rows, self.turned, self.part, self.twin, self.far, self.near, self.last,
            self.row_sem, self.t_send, self.t_recv, self.f_send, self.f_recv,
            self.n_send, self.n_recv, self.l_send, self.l_recv,
        ) = scratch
        fr, fs = at.fr, at.fs
        self.hi = lax.rem(at.group, 2)
        self.z = lax.div(at.group, 2)
        self.sibling = (fr + 1 - 2 * at.core, fs)
        self.over = (fr + 2 - 4 * self.hi, fs)
        self.up = (lax.rem(fr + 4, 16), fs)
        self.down = (lax.rem(fr + 12, 16), fs)

    def group(self, off, hi):
        return 2 * lax.rem(self.z + off, 4) + hi

    def target(self, m):
        return self.group(far_first(lax.div(m, 2)), lax.rem(m, 2))

    def copies(self, m):
        cols = pl.ds(pl.multiple_of(self.target(m) * LOCAL, LOCAL), LOCAL)
        slot = lax.rem(m, 2)
        return [
            pltpu.make_async_copy(
                source.at[:, cols], self.rows.at[slot, i], self.row_sem.at[slot, i]
            )
            for i, source in enumerate((self.flat, self.up_all))
        ]

    def fetch(self, m):
        for copy in self.copies(m):
            copy.start()

    def to_twin(self, j):
        return remote(
            self.part.at[j, 1 - self.at.core],
            self.twin.at[j],
            self.t_send.at[j],
            self.t_recv.at[j],
            self.sibling,
        )

    def mine(self, off, hi):
        return self.part.at[self.group(off, hi), self.at.core]

    def to_far(self, d):
        return remote(
            self.mine(2, d), self.far.at[d], self.f_send.at[d], self.f_recv.at[d],
            (self.up, self.down)[d],
        )

    def to_near(self, d, hi):
        return remote(
            self.mine((1, 3)[d], hi), self.near.at[d, hi], self.n_send.at[d, hi],
            self.n_recv.at[d, hi], (self.up, self.down)[d],
        )

    def tile(self, m):
        j = self.target(m)
        slot = lax.rem(m, 2)
        for copy in self.copies(m):
            copy.wait()

        @pl.when(m < 7)
        def _():
            self.fetch(m + 1)

        self.turned[...] = jnp.transpose(self.rows[slot, 0])
        for c in range(3):
            cols = slice(c * LOCAL, (c + 1) * LOCAL)
            other = self.dproj[:, :, :, cols].reshape(1024, LOCAL)
            value = jnp.dot(self.turned[...], other, preferred_element_type=F32)
            self.part[j, :, :, cols] = value.astype(BF).reshape(2, 192, LOCAL)
        self.turned[...] = jnp.transpose(self.rows[slot, 1])
        value = jnp.dot(self.turned[...], self.attended[...], preferred_element_type=F32)
        self.part[j, :, :, 3 * LOCAL :] = value.astype(BF).reshape(2, 192, LOCAL)
        self.to_twin(j).start()

        @pl.when(m > 0)
        def _():
            self.merge(m - 1)

    def add(self, j, other):
        def rows(i):
            some = pl.ds(pl.multiple_of(i * 48, 16), 48)
            held = self.part[j, self.at.core, some, :].astype(F32)
            self.part[j, self.at.core, some, :] = (held + other[some, :].astype(F32)).astype(BF)

        loop(4, rows)

    def merge(self, m):
        j = self.target(m)
        landed(self.twin.at[j], self.t_recv.at[j])
        self.add(j, self.twin.at[j])
        for at_step, copy in (
            (0, lambda: self.to_far(0)),
            (1, lambda: self.to_far(1)),
            (3, lambda: self.to_near(0, 1)),
            (4, lambda: self.to_near(1, 0)),
        ):

            @pl.when(m == at_step)
            def _(copy=copy):
                copy().start()

    def relay(self):
        for d in range(2):
            landed(self.far.at[d], self.f_recv.at[d])
            self.add(self.group((1, 3)[d], d), self.far.at[d])
            self.to_near(d, d).start()

    def to_last(self):
        return remote(
            self.mine(0, 1 - self.hi), self.last, self.l_send, self.l_recv, self.over
        )

    def finish(self):
        def arrived(hi):
            for d in range(2):
                landed(self.near.at[d, hi], self.n_recv.at[d, hi])

        def both(hi, some):
            value = self.part[self.group(0, hi), self.at.core, some, :].astype(F32)
            for d in range(2):
                value = value + self.near[d, hi, some, :].astype(F32)
            return value

        arrived(1 - self.hi)

        def rows(i):
            some = pl.ds(pl.multiple_of(i * 48, 16), 48)
            self.part[self.group(0, 1 - self.hi), self.at.core, some, :] = both(
                1 - self.hi, some
            ).astype(BF)

        loop(4, rows)
        self.to_last().start()
        arrived(self.hi)
        landed(self.last, self.l_recv)

        def end(i):
            some = pl.ds(pl.multiple_of(i * 48, 16), 48)
            value = (both(self.hi, some) + self.last[some, :].astype(F32)).astype(BF)
            for c in range(4):
                self.result[c, some, :] = value[:, c * LOCAL : (c + 1) * LOCAL]

        loop(4, end)
        for d in range(2):
            self.to_far(d).wait_send()
            for hi in range(2):
                self.to_near(d, hi).wait_send()
        self.to_last().wait_send()
        loop(8, lambda j: self.to_twin(j).wait_send())


def scatter_kernel(back, *refs):
    if back:
        qkv, grad, factors, attended, w_hbm, flat, up_all, total, w_grad = refs[:9]
        refs = refs[9:]
    else:
        qkv, w_hbm, total, tokens = refs[:4]
        refs = refs[4:]
    (
        weight, out, part, mine, from_side, far, near,
        o_send, o_recv, y_send, y_recv, f_send, f_recv, n_send, n_recv, w_sem,
    ) = refs[:16]
    at = Place()
    if back:
        tokens, dproj = refs[16:18]
        sums = WeightSums(at, flat, up_all, attended, dproj, w_grad, *refs[18:])
    if back:
        w_copies = [
            pltpu.make_async_copy(
                w_hbm.at[c], weight.at[:, pl.ds(c * LOCAL, LOCAL)], w_sem.at[c]
            )
            for c in range(3)
        ]
    else:
        w_copies = [pltpu.make_async_copy(w_hbm, weight, w_sem.at[0])]
    for copy in w_copies:
        copy.start()
    if back:
        sums.fetch(0)
    at.meet()

    def columns(ref, t, block):
        return ref[t, :, :, block * HEAD_DIM : (block + 1) * HEAD_DIM].reshape(256, HEAD_DIM)

    def put(i, block, value):
        out[i, :, :, block * HEAD_DIM : (block + 1) * HEAD_DIM] = value.astype(BF).reshape(
            16, 16, HEAD_DIM
        )

    def attend(i):
        slot = 1 - lax.div(i, 2)
        xh = lax.rem(i, 2)
        t = 2 * xh + lax.rem(at.lo + slot, 2)
        for h in range(HEADS):
            query, key, value = (columns(qkv, t, c * HEADS + h) for c in range(3))
            probs = softmax(query, key)
            low = probs.astype(BF)
            if not back:
                put(i, h, jnp.dot(low, value, preferred_element_type=F32))
                continue
            grad_in = columns(grad, t, h)
            dprob = dot_nt(grad_in, value)
            put(i, 2 * HEADS + h, dot_tn(low, grad_in))
            dscore = (probs * (dprob - jnp.sum(probs * dprob, -1, keepdims=True))).astype(BF)
            for c, normed, product in (
                (0, query, jnp.dot(dscore, key, preferred_element_type=F32)),
                (1, key, dot_tn(dscore, query)),
            ):
                step_in = (product * INV_ROOT).astype(BF).astype(F32)
                wide = normed.astype(F32)
                put(
                    i,
                    c * HEADS + h,
                    step_in - wide * jnp.mean(step_in * wide, -1, keepdims=True),
                )
        xi = 2 * xh + at.core

        def give(f):
            src = out.at[i, f]
            dst = tokens.at[slot, xi, at.group]

            @pl.when(f == at.fr)
            def _():
                pltpu.make_async_copy(src, dst, o_recv.at[slot, xi]).start()

            @pl.when(f != at.fr)
            def _():
                remote(src, dst, o_send.at[i], o_recv.at[slot, xi], (f, at.fs)).start()

        loop(16, give)

    loop(4, attend)
    for copy in w_copies:
        copy.wait()

    def product(slot, xi, j):
        tile = pl.ds(pl.multiple_of(j * TILE, TILE), TILE)
        if back:
            return tile, dot_nt(dproj[slot, xi], weight[tile, :])
        rows = tokens[slot, xi].reshape(2 * HALF, LOCAL)
        return tile, jnp.dot(rows, weight[:, tile], preferred_element_type=F32)

    def take(slot, xi):
        landed(tokens.at[slot, xi], o_recv.at[slot, xi])
        if back:
            for j in range(3 * HEADS):
                cols = slice(j * HEAD_DIM, (j + 1) * HEAD_DIM)
                block = tokens[slot, xi, :, :, cols].reshape(2 * HALF, HEAD_DIM)
                if j < 2 * HEADS:
                    block = (block.astype(F32) * factors[slot, xi, :, j : j + 1]).astype(BF)
                dproj[slot, xi, :, cols] = block

    def first(n):
        xi = at.along(far_first(n))
        take(1, xi)

        def tiles(j):
            tile, value = product(1, xi, j)
            part[xi, :, :, tile] = value.astype(BF).reshape(2, HALF, TILE)

        loop(WIDTH // TILE, tiles)
        for h in range(2):
            remote(
                part.at[xi, h], from_side.at[xi, h], y_send.at[xi, h], y_recv.at[xi, h], at.side[h]
            ).start()

    loop(4, first)

    xl, xr, xf = at.along(3), at.along(1), at.along(2)
    far_copies = [
        remote(mine.at[xf, 0], far.at[0], f_send.at[0], f_recv.at[0], at.right),
        remote(mine.at[xf, 1], far.at[1], f_send.at[1], f_recv.at[1], at.left),
    ]
    near_copies = [
        remote(mine.at[xr, 1], near.at[0, 1], n_send.at[0, 1], n_recv.at[0, 1], at.right),
        remote(mine.at[xl, 0], near.at[1, 0], n_send.at[1, 0], n_recv.at[1, 0], at.left),
        remote(mine.at[xr, 0], near.at[0, 0], n_send.at[0, 0], n_recv.at[0, 0], at.right),
        remote(mine.at[xl, 1], near.at[1, 1], n_send.at[1, 1], n_recv.at[1, 1], at.left),
    ]

    if back:
        loop(4, lambda n: take(0, at.along(far_first(n))))

    def second(n):
        xi = at.along(far_first(n))
        if back:
            loop(2, lambda q: sums.tile(2 * n + q))
        else:
            take(0, xi)
        for h in range(2):
            landed(from_side.at[xi, h], y_recv.at[xi, h])

        def tiles(j):
            tile, value = product(0, xi, j)
            other = from_side[xi, :, :, tile].astype(F32).reshape(2 * HALF, TILE)
            mine[xi, :, :, tile] = (value + other).astype(BF).reshape(2, HALF, TILE)

        loop(WIDTH // TILE, tiles)

        @pl.when(n == 0)
        def _():
            far_copies[0].start()
            far_copies[1].start()

        @pl.when(n == 1)
        def _():
            near_copies[0].start()

        @pl.when(n == 2)
        def _():
            near_copies[1].start()

    loop(4, second)
    if back:
        sums.merge(7)
    for d, xi in ((0, xr), (1, xl)):
        landed(far.at[d], f_recv.at[d])

        def tiles(j, d=d, xi=xi):
            tile = pl.ds(pl.multiple_of(j * TILE, TILE), TILE)
            mine[xi, d, :, tile] = (
                mine[xi, d, :, tile].astype(F32) + far[d, :, tile].astype(F32)
            ).astype(BF)

        loop(WIDTH // TILE, tiles)
        near_copies[2 + d].start()
    if back:
        sums.relay()
    for d, h in ((0, 1), (1, 0), (0, 0), (1, 1)):
        landed(near.at[d, h], n_recv.at[d, h])

    def finish(j):
        tile = pl.ds(pl.multiple_of(j * TILE, TILE), TILE)
        for h in range(2):
            total[h * HALF : (h + 1) * HALF, tile] = (
                mine[at.x, h, :, tile].astype(F32)
                + near[0, h, :, tile].astype(F32)
                + near[1, h, :, tile].astype(F32)
            )

    loop(WIDTH // TILE, finish)
    if back:
        sums.finish()
    for copy in far_copies + near_copies:
        copy.wait_send()
    for xi in range(4):
        for h in range(2):
            landed(part.at[xi, h], y_send.at[xi, h])

    loop(4, lambda i: landed(out.at[i, pl.ds(0, 15)], o_send.at[i]))


def scatter(args, weight, back, streamed=()):
    cols = 3 * LOCAL if back else LOCAL
    token_shape = (2, 4, 8, 16, cols)
    shapes = [jax.ShapeDtypeStruct((2 * HALF, WIDTH), F32)]
    scratch = [
        pltpu.VMEM((WIDTH, cols) if back else (LOCAL, WIDTH), BF),
        pltpu.VMEM((4, 16, 16, cols), BF),
        pltpu.VMEM((4, 2, HALF, WIDTH), BF),
        pltpu.VMEM((4, 2, HALF, WIDTH), BF),
        pltpu.VMEM((4, 2, HALF, WIDTH), BF),
        pltpu.VMEM((2, HALF, WIDTH), BF),
        pltpu.VMEM((2, 2, HALF, WIDTH), BF),
        pltpu.SemaphoreType.DMA((4,)),
        pltpu.SemaphoreType.DMA((2, 4)),
        pltpu.SemaphoreType.DMA((4, 2)),
        pltpu.SemaphoreType.DMA((4, 2)),
        pltpu.SemaphoreType.DMA((2,)),
        pltpu.SemaphoreType.DMA((2,)),
        pltpu.SemaphoreType.DMA((2, 2)),
        pltpu.SemaphoreType.DMA((2, 2)),
        pltpu.SemaphoreType.DMA((3,)),
    ]
    if back:
        shapes.append(jax.ShapeDtypeStruct((4, 192, LOCAL), BF))
        scratch += [
            pltpu.VMEM(token_shape, BF),
            pltpu.VMEM((2, 4, 2 * HALF, cols), BF),
            pltpu.VMEM((2, 2, 1024, LOCAL), BF),
            pltpu.VMEM((LOCAL, 1024), BF),
            pltpu.VMEM((8, 2, 192, 4 * LOCAL), BF),
            pltpu.VMEM((8, 192, 4 * LOCAL), BF),
            pltpu.VMEM((2, 192, 4 * LOCAL), BF),
            pltpu.VMEM((2, 2, 192, 4 * LOCAL), BF),
            pltpu.VMEM((192, 4 * LOCAL), BF),
            pltpu.SemaphoreType.DMA((2, 2)),
            pltpu.SemaphoreType.DMA((8,)),
            pltpu.SemaphoreType.DMA((8,)),
            pltpu.SemaphoreType.DMA((2,)),
            pltpu.SemaphoreType.DMA((2,)),
            pltpu.SemaphoreType.DMA((2, 2)),
            pltpu.SemaphoreType.DMA((2, 2)),
            pltpu.SemaphoreType.DMA,
            pltpu.SemaphoreType.DMA,
        ]
    else:
        shapes.append(jax.ShapeDtypeStruct(token_shape, BF))
    return pl.pallas_call(
        functools.partial(scatter_kernel, back),
        out_shape=shapes,
        in_specs=vmem(len(args)) + [pl.BlockSpec(memory_space=pl.ANY)] * (1 + len(streamed)),
        out_specs=vmem(len(shapes)),
        scratch_shapes=scratch,
        compiler_params=pltpu.CompilerParams(
            collective_id=3 if back else 1,
            has_side_effects=True,
            vmem_limit_bytes=VMEM_BYTES,
        ),
        cost_estimate=pl.CostEstimate(
            flops=2 * 1024 * WIDTH * cols, bytes_accessed=30_000_000, transcendentals=0
        ),
        name="scatter_back" if back else "scatter_mixed",
    )(*args, weight, *streamed)


def total_kernel(own, result, by_head, by_frame, partial, s1, r1, s2, r2, s3, r3):
    fr = lax.axis_index("frame")
    fs = lax.axis_index("fsdp")
    barrier = pltpu.get_barrier_semaphore()

    def head(i):
        return (fr, lax.rem(fs + i, 8))

    def frame(i):
        return (lax.rem(fr + i, 16), fs)

    def greet(peer):
        pl.semaphore_signal(barrier, inc=1, device_id=peer, device_id_type=MESH)

    for i in range(1, 8):
        greet(head(i))
    loop(15, lambda i: greet(frame(i + 1)))
    pl.semaphore_wait(barrier, 22)

    firsts = [
        remote(own.at[head(i)[1]], by_head.at[fs], s1.at[i], r1, head(i)) for i in range(1, 8)
    ]
    for copy in firsts:
        copy.start()
    by_head[fs] = own[fs]
    landed(by_head.at[pl.ds(0, 7)], r1)
    value = by_head[0]
    for i in range(1, 8):
        value = value + by_head[i]
    partial[...] = value
    by_frame[fr] = value
    seconds = [
        remote(partial, by_frame.at[fr], s2.at[i], r2, frame(i)) for i in range(1, 16)
    ]
    for copy in seconds:
        copy.start()
    landed(by_frame.at[pl.ds(0, 15)], r2)
    value = by_frame[0]
    for i in range(1, 16):
        value = value + by_frame[i]
    result[fs] = value
    thirds = [remote(result.at[fs], result.at[fs], s3.at[i], r3, head(i)) for i in range(1, 8)]
    for copy in thirds:
        copy.start()
    landed(result.at[pl.ds(0, 7)], r3)
    for copy in firsts + seconds + thirds:
        copy.wait_send()


def total_sums(rows):
    pieces = jnp.pad(rows.reshape(3, 8, LOCAL).transpose(1, 0, 2), ((0, 0), (0, 5), (0, 0)))
    result = pl.pallas_call(
        total_kernel,
        out_shape=jax.ShapeDtypeStruct((8, 8, LOCAL), F32),
        in_specs=vmem(1),
        out_specs=vmem(1)[0],
        scratch_shapes=[
            pltpu.VMEM((8, 8, LOCAL), F32),
            pltpu.VMEM((16, 8, LOCAL), F32),
            pltpu.VMEM((8, LOCAL), F32),
            pltpu.SemaphoreType.DMA((8,)),
            pltpu.SemaphoreType.DMA,
            pltpu.SemaphoreType.DMA((16,)),
            pltpu.SemaphoreType.DMA,
            pltpu.SemaphoreType.DMA((8,)),
            pltpu.SemaphoreType.DMA,
        ],
        compiler_params=pltpu.CompilerParams(collective_id=4, has_side_effects=True),
        name="total_sums",
    )(pieces)
    return result[:, :3].transpose(1, 0, 2).reshape(3, WIDTH)


def to_rows(block):
    frames, patches, width = block.shape
    return block.reshape(frames, 8, 8, width).transpose(1, 0, 2, 3).reshape(-1, width)


def from_rows(rows):
    return rows.reshape(8, 2, 8, -1).transpose(1, 0, 2, 3).reshape(2, 64, -1)


def shards(hidden_states, teacher, mod_scale, mod_shift, out_gate, w_qkv, w_out):
    states = to_rows(hidden_states).astype(F32)
    factor = lax.rsqrt(jnp.mean(states * states, -1, keepdims=True) + 1e-06)
    normed = states * factor
    modded = (normed * (1.0 + mod_scale) + mod_shift).astype(BF)
    flat, qkv, factors = gather(modded.reshape(2, HALF, WIDTH), w_qkv, True)
    mixed, attended = scatter([qkv], w_out, False)
    diff = states + out_gate * mixed - to_rows(teacher).astype(F32)
    upstream = (out_gate * diff).astype(BF)
    up_all, grad_att = gather(upstream.reshape(2, HALF, WIDTH), w_out, False)
    dmod, w_grad = scatter(
        [qkv, grad_att, factors, attended.reshape(1024, LOCAL)],
        w_qkv,
        True,
        (flat.reshape(1024, WIDTH), up_all.reshape(1024, WIDTH)),
    )
    sums = total_sums(
        jnp.stack([jnp.sum(dmod * normed, 0), jnp.sum(dmod, 0), jnp.sum(diff * mixed, 0)])
    )
    dnorm = dmod * (1.0 + mod_scale)
    grad_hidden = (
        diff + factor * (dnorm - normed * jnp.mean(dnorm * normed, -1, keepdims=True))
    ).astype(BF)
    return (from_rows(grad_hidden), w_grad[:3], w_grad[3].T, sums[0], sums[1], sums[2])


def solution(mesh):
    in_specs = (
        P("frame", "fsdp", None),
        P("frame", "fsdp", None),
        P(),
        P(),
        P(),
        P(None, None, "fsdp"),
        P("fsdp", None),
    )
    out_specs = (
        P("frame", "fsdp", None),
        P(None, "frame", "fsdp"),
        P("fsdp", "frame"),
        P(),
        P(),
        P(),
    )
    return jax.shard_map(shards, mesh=mesh, in_specs=in_specs, out_specs=out_specs, check_vma=False)
```

```python
import functools
import jax
import jax.numpy as jnp
from jax import lax
from jax.experimental import pallas as pl
from jax.experimental.pallas import tpu as pltpu
from jax.sharding import PartitionSpec as P

HEAD_DIM = 128
HEADS = 3
LOCAL = 384
WIDTH = 3072
HALF = 64
TILE = 512
INV_ROOT = HEAD_DIM ** (-0.5)
MESH = pl.DeviceIdType.MESH
BF = jnp.bfloat16
F32 = jnp.float32
VMEM_BYTES = 60 * 1024 * 1024


class Place:
    def __init__(self):
        fr = lax.axis_index("frame")
        fs = lax.axis_index("fsdp")
        self.fr = fr
        self.fs = fs
        self.x = lax.div(fs, 2)
        self.lo = lax.rem(fs, 2)
        self.core = lax.rem(fr, 2)
        self.group = lax.div(fr, 2)
        other = fs + 1 - 2 * self.lo
        hi = lax.rem(self.group, 2)
        self.right = (fr, lax.rem(fs + 2, 8))
        self.left = (fr, lax.rem(fs + 6, 8))
        self.side = ((fr, other), (fr + 2 - 4 * hi, other))

    def along(self, off):
        return lax.rem(self.x + off, 4)

    def meet(self):
        barrier = pltpu.get_barrier_semaphore()
        for peer in (self.right, self.left) + self.side:
            pl.semaphore_signal(barrier, inc=1, device_id=peer, device_id_type=MESH)

        def greet(step, carry):
            pl.semaphore_signal(
                barrier,
                inc=1,
                device_id=(lax.rem(self.fr + step, 16), self.fs),
                device_id_type=MESH,
            )
            return carry

        lax.fori_loop(1, 16, greet, 0)
        pl.semaphore_wait(barrier, 19)


def remote(src, dst, send_sem, recv_sem, device):
    return pltpu.make_async_remote_copy(
        src_ref=src,
        dst_ref=dst,
        send_sem=send_sem,
        recv_sem=recv_sem,
        device_id=device,
        device_id_type=MESH,
    )


def landed(ref, sem):
    pltpu.make_async_copy(ref, ref, sem).wait()


def loop(count, body):
    def step(i, carry):
        body(i)
        return carry

    lax.fori_loop(0, count, step, 0)


def others_first(p):
    return 2 + p - lax.div(3 * p * (p - 1), 2)


def gather_kernel(project, own, w_hbm, *refs):
    if project:
        kept_all, sent_to, factors, full, weight, out, *sems = refs
    else:
        kept_all, sent_to, full, weight, out, *sems = refs
    x_send, y_send, recv, o_send, o_recv, w_sem, keep_sem = sems
    at = Place()
    if project:
        w_copies = [
            pltpu.make_async_copy(
                w_hbm.at[c], weight.at[:, pl.ds(c * LOCAL, LOCAL)], w_sem.at[c]
            )
            for c in range(3)
        ]
    else:
        w_copies = [pltpu.make_async_copy(w_hbm, weight, w_sem.at[0])]
    for copy in w_copies:
        copy.start()
    at.meet()

    def to_right(slot, src, xi, h, n):
        return remote(src, full.at[slot, xi, h], x_send.at[n], recv.at[slot, xi, h], at.right)

    def to_left(slot, src, xi, h, n):
        return remote(src, full.at[slot, xi, h], x_send.at[n], recv.at[slot, xi, h], at.left)

    def to_side(src, xi, h, n):
        return remote(src, full.at[1, xi, h], y_send.at[n], recv.at[1, xi, h], at.side[h])

    xl, xr, xf = at.along(3), at.along(1), at.along(2)
    first = [
        to_right(0, own.at[0], at.x, 0, 0),
        to_left(0, own.at[1], at.x, 1, 1),
        to_side(own.at[0], at.x, 0, 0),
        to_side(own.at[1], at.x, 1, 1),
    ]
    for copy in first:
        copy.start()
    full[0, at.x] = own[...]
    second = [
        to_right(0, full.at[0, xl, 0], xl, 0, 2),
        to_left(0, full.at[0, xr, 1], xr, 1, 3),
    ]
    if not project:
        second.append(to_side(full.at[0, xl, 0], xl, 0, 2))
        second.append(to_side(full.at[0, xr, 1], xr, 1, 3))
    third = [
        to_right(0, own.at[1], at.x, 1, 4),
        to_side(full.at[0, xf, 0], xf, 0, 4),
        to_left(0, own.at[0], at.x, 0, 5),
        to_side(full.at[0, xf, 1], xf, 1, 5),
    ]
    fourth = [
        to_right(1, full.at[1, at.x, 1], at.x, 1, 6),
        to_left(1, full.at[1, at.x, 0], at.x, 0, 7),
    ]
    if project:
        fourth.append(to_right(1, full.at[1, at.x, 0], at.x, 0, 8))
        fourth.append(to_left(1, full.at[1, at.x, 1], at.x, 1, 9))
    for copy in w_copies:
        copy.wait()

    def arrived(slot, xi, h):
        landed(full.at[slot, xi, h], recv.at[slot, xi, h])

    def early(k):
        @pl.when(k == 1)
        def _():
            arrived(0, xl, 0)
            for copy in second[0::2]:
                copy.start()
            arrived(0, xr, 1)
            for copy in second[1::2]:
                copy.start()
            arrived(1, at.x, 0)
            arrived(1, at.x, 1)

        work(k, k, at.x)

    def late(i):
        slot = lax.div(i, 3)
        xi = at.along(others_first(lax.rem(i, 3)))

        @pl.when(i == 0)
        def _():
            arrived(0, xf, 0)
            third[0].start()
            third[1].start()
            arrived(0, xf, 1)
            third[2].start()
            third[3].start()

        @pl.when(i == 1)
        def _():
            arrived(0, xl, 1)
            for copy in fourth[0::2]:
                copy.start()

        @pl.when(i == 2)
        def _():
            arrived(0, xr, 0)
            for copy in fourth[1::2]:
                copy.start()

        @pl.when(i >= 3)
        def _():
            arrived(1, xi, 0)
            arrived(1, xi, 1)

        work(i + 2, slot, xi)

    def work(k, slot, xi):
        pltpu.make_async_copy(full.at[slot, xi], kept_all.at[slot, xi], keep_sem).start()
        tokens = full[slot, xi].reshape(2 * HALF, WIDTH)
        if project:
            both = jnp.dot(tokens, weight[...], preferred_element_type=F32)
            lane = lax.broadcasted_iota(jnp.int32, (2 * HALF, HEAD_DIM), 1)
            kept = jnp.zeros((2 * HALF, HEAD_DIM), F32)
            for j in range(3 * HEADS):
                block = both[:, j * HEAD_DIM : (j + 1) * HEAD_DIM]
                if j < 2 * HEADS:
                    factor = lax.rsqrt(jnp.mean(block * block, -1, keepdims=True) + 1e-06)
                    kept = jnp.where(lane == j, factor, kept)
                    block = block * factor
                out[k, :, :, j * HEAD_DIM : (j + 1) * HEAD_DIM] = block.astype(BF).reshape(
                    8, 16, HEAD_DIM
                )
            factors[slot, xi] = kept
        else:
            both = lax.dot_general(
                tokens, weight[...], (((1,), (1,)), ((), ())), preferred_element_type=F32
            )
            out[k] = both.astype(BF).reshape(8, 16, LOCAL)
        to_core = lax.rem(xi, 2)
        to_slot = 2 * lax.div(xi, 2) + lax.rem(at.lo + slot, 2)

        def give(g):
            target = 2 * g + to_core
            src = out.at[k, g]
            dst = sent_to.at[to_slot, at.fr]

            @pl.when(target == at.fr)
            def _():
                pltpu.make_async_copy(src, dst, o_recv.at[to_slot]).start()

            @pl.when(target != at.fr)
            def _():
                remote(src, dst, o_send.at[g], o_recv.at[to_slot], (target, at.fs)).start()

        loop(8, give)

    loop(2, early)
    loop(6, late)

    for copy in first + second + third + fourth:
        copy.wait_send()

    def drain(g):
        @pl.when(g == at.group)
        def _():
            landed(out.at[pl.ds(0, 4), g], o_send.at[g])

        @pl.when(g != at.group)
        def _():
            landed(out.at[:, g], o_send.at[g])

    loop(8, drain)
    pltpu.make_async_copy(full, kept_all, keep_sem).wait()
    loop(4, lambda t: landed(sent_to.at[t], o_recv.at[t]))


def vmem(count):
    return [pl.BlockSpec(memory_space=pltpu.VMEM)] * count


def gather(own, weight, project):
    cols = 3 * LOCAL if project else LOCAL
    shapes = [
        jax.ShapeDtypeStruct((2, 4, 2, HALF, WIDTH), BF),
        jax.ShapeDtypeStruct((4, 16, 16, cols), BF),
    ]
    if project:
        shapes.append(jax.ShapeDtypeStruct((2, 4, 2 * HALF, HEAD_DIM), F32))
    flops = 2 * 1024 * WIDTH * cols
    return pl.pallas_call(
        functools.partial(gather_kernel, project),
        out_shape=shapes,
        in_specs=[pl.BlockSpec(memory_space=pltpu.VMEM), pl.BlockSpec(memory_space=pl.ANY)],
        out_specs=[pl.BlockSpec(memory_space=pl.ANY)] + vmem(len(shapes) - 1),
        scratch_shapes=[
            pltpu.VMEM((2, 4, 2, HALF, WIDTH), BF),
            pltpu.VMEM((WIDTH, cols) if project else (LOCAL, WIDTH), BF),
            pltpu.VMEM((8, 8, 16, cols), BF),
            pltpu.SemaphoreType.DMA((10,)),
            pltpu.SemaphoreType.DMA((6,)),
            pltpu.SemaphoreType.DMA((2, 4, 2)),
            pltpu.SemaphoreType.DMA((8,)),
            pltpu.SemaphoreType.DMA((4,)),
            pltpu.SemaphoreType.DMA((3,)),
            pltpu.SemaphoreType.DMA,
        ],
        compiler_params=pltpu.CompilerParams(
            collective_id=0 if project else 2,
            has_side_effects=True,
            vmem_limit_bytes=VMEM_BYTES,
        ),
        cost_estimate=pl.CostEstimate(flops=flops, bytes_accessed=30_000_000, transcendentals=0),
        name="gather_project" if project else "gather_back",
    )(own, weight)


def same_patch():
    rows = lax.broadcasted_iota(jnp.int32, (256, 256), 0)
    cols = lax.broadcasted_iota(jnp.int32, (256, 256), 1)
    return lax.rem(rows, 8) == lax.rem(cols, 8)


def dot_nt(a, b):
    return lax.dot_general(a, b, (((1,), (1,)), ((), ())), preferred_element_type=F32)


def dot_tn(a, b):
    return lax.dot_general(a, b, (((0,), (0,)), ((), ())), preferred_element_type=F32)


def softmax(query, key):
    scores = dot_nt(query, key) * INV_ROOT
    expo = jnp.where(same_patch(), jnp.exp(scores), 0.0)
    return expo / jnp.sum(expo, -1, keepdims=True)


class WeightSums:
    def __init__(self, at, flat, up_all, attended, dproj, result, *scratch):
        self.at = at
        self.flat, self.up_all, self.attended, self.dproj = flat, up_all, attended, dproj
        self.result = result
        (
            self.rows, self.turned, self.part, self.twin, self.far, self.near, self.last,
            self.row_sem, self.t_send, self.t_recv, self.f_send, self.f_recv,
            self.n_send, self.n_recv, self.l_send, self.l_recv,
        ) = scratch
        fr, fs = at.fr, at.fs
        self.hi = lax.rem(at.group, 2)
        self.z = lax.div(at.group, 2)
        self.sibling = (fr + 1 - 2 * at.core, fs)
        self.over = (fr + 2 - 4 * self.hi, fs)
        self.up = (lax.rem(fr + 4, 16), fs)
        self.down = (lax.rem(fr + 12, 16), fs)

    def group(self, off, hi):
        return 2 * lax.rem(self.z + off, 4) + hi

    def flagged(self, flag):
        return flag * self.hi + (1 - flag) * (1 - self.hi)

    def target(self, m):
        q, b = lax.div(m, 2), lax.rem(m, 2)
        inner = lax.div(q * (3 - q), 2)
        base = 2 - q + lax.div(q * (q - 1), 2) - lax.div(q * (q - 1) * (q - 2), 3)
        flag = (1 - inner) * b + inner * (q - 1)
        return self.group(base + 2 * inner * b, self.flagged(flag))

    def load(self, source, j, slot):
        cols = pl.ds(pl.multiple_of(j * LOCAL, LOCAL), LOCAL)
        return pltpu.make_async_copy(
            source.at[:, cols], self.rows.at[slot], self.row_sem.at[slot]
        )

    def fetch(self, source, j, slot):
        self.load(source, j, slot).start()

    def out_rows(self, m):
        slot = lax.rem(m, 2)
        self.load(self.up_all, m, slot).wait()

        @pl.when(m < 7)
        def _():
            self.fetch(self.up_all, m + 1, 1 - slot)

        @pl.when(m == 7)
        def _():
            self.fetch(self.flat, self.target(0), 0)

        self.turned[...] = jnp.transpose(self.rows[slot])
        value = jnp.dot(self.turned[...], self.attended[...], preferred_element_type=F32)
        self.part[m, :, :, 3 * LOCAL :] = value.astype(BF).reshape(2, 192, LOCAL)

    def to_twin(self, j):
        return remote(
            self.part.at[j, 1 - self.at.core],
            self.twin.at[j],
            self.t_send.at[j],
            self.t_recv.at[j],
            self.sibling,
        )

    def rows_of(self, off, flag, half):
        j = self.group(off, self.flagged(flag))
        return self.part.at[j, self.at.core, pl.ds(half * 96, 96)]

    def to_far(self, d, flag):
        return remote(
            self.rows_of(2, flag, d), self.far.at[d, flag], self.f_send.at[d, flag],
            self.f_recv.at[d, flag], (self.up, self.down)[d],
        )

    def to_near(self, d, flag, half):
        return remote(
            self.rows_of((1, 3)[d], flag, half), self.near.at[d, flag, half],
            self.n_send.at[d, flag, half], self.n_recv.at[d, flag, half],
            (self.up, self.down)[d],
        )

    def tile(self, m):
        j = self.target(m)
        slot = lax.rem(m, 2)
        self.load(self.flat, j, slot).wait()

        @pl.when(m < 7)
        def _():
            self.fetch(self.flat, self.target(m + 1), 1 - slot)

        self.turned[...] = jnp.transpose(self.rows[slot])
        for c in range(3):
            cols = slice(c * LOCAL, (c + 1) * LOCAL)
            other = self.dproj[:, :, :, cols].reshape(1024, LOCAL)
            value = jnp.dot(self.turned[...], other, preferred_element_type=F32)
            self.part[j, :, :, cols] = value.astype(BF).reshape(2, 192, LOCAL)
        self.to_twin(j).start()

        @pl.when(m > 0)
        def _():
            self.merge(m - 1)

    def add(self, held, other, count):
        def rows(i):
            some = pl.ds(pl.multiple_of(i * 48, 16), 48)
            held[some, :] = (held[some, :].astype(F32) + other[some, :].astype(F32)).astype(BF)

        loop(count, rows)

    def merge(self, m):
        j = self.target(m)
        landed(self.twin.at[j], self.t_recv.at[j])
        self.add(self.part.at[j, self.at.core], self.twin.at[j], 4)
        for flag in range(2):

            @pl.when(m == flag)
            def _(flag=flag):
                for d in range(2):
                    self.to_far(d, flag).start()

            @pl.when(m == 2 + 2 * flag)
            def _(flag=flag):
                if flag == 1:
                    self.relay(0)
                self.to_near(0, flag, 1).start()

            @pl.when(m == 3 + 2 * flag)
            def _(flag=flag):
                self.to_near(1, flag, 0).start()

    def relay(self, flag):
        for d in range(2):
            landed(self.far.at[d, flag], self.f_recv.at[d, flag])
            self.add(self.rows_of((1, 3)[d], flag, d), self.far.at[d, flag], 2)
            self.to_near(d, flag, d).start()

    def arrived(self, flag):
        for d in range(2):
            for half in range(2):
                landed(self.near.at[d, flag, half], self.n_recv.at[d, flag, half])

    def both(self, flag, half, some):
        value = self.rows_of(0, flag, half)[some, :].astype(F32)
        for d in range(2):
            value = value + self.near[d, flag, half, some, :].astype(F32)
        return value

    def to_last(self):
        source = self.part.at[self.group(0, self.flagged(0)), self.at.core]
        return remote(source, self.last, self.l_send, self.l_recv, self.over)

    def turn(self):
        self.arrived(0)
        for half in range(2):
            held = self.rows_of(0, 0, half)

            def rows(i, half=half, held=held):
                some = pl.ds(pl.multiple_of(i * 48, 16), 48)
                held[some, :] = self.both(0, half, some).astype(BF)

            loop(2, rows)
        self.to_last().start()

    def finish(self):
        self.arrived(1)
        landed(self.last, self.l_recv)
        for half in range(2):

            def end(i, half=half):
                some = pl.ds(pl.multiple_of(i * 48, 16), 48)
                there = pl.ds(pl.multiple_of(half * 96 + i * 48, 16), 48)
                value = self.both(1, half, some) + self.last[there, :].astype(F32)
                value = value.astype(BF)
                for c in range(4):
                    self.result[c, there, :] = value[:, c * LOCAL : (c + 1) * LOCAL]

            loop(2, end)
        for d in range(2):
            for flag in range(2):
                self.to_far(d, flag).wait_send()
                for half in range(2):
                    self.to_near(d, flag, half).wait_send()
        self.to_last().wait_send()
        loop(8, lambda j: self.to_twin(j).wait_send())


def scatter_kernel(back, *refs):
    if back:
        qkv, grad, factors, attended, w_hbm, flat, up_all, total, w_grad = refs[:9]
        refs = refs[9:]
    else:
        qkv, w_hbm, total, tokens = refs[:4]
        refs = refs[4:]
    (
        weight, out, part, mine, from_side, far, near,
        passed, o_send, o_recv, y_send, y_recv, f_send, f_recv, n_send, n_recv, p_send, p_recv,
        w_sem,
    ) = refs[:19]
    at = Place()
    if back:
        tokens, dproj = refs[19:21]
        sums = WeightSums(at, flat, up_all, attended, dproj, w_grad, *refs[21:])
    if back:
        w_copies = [
            pltpu.make_async_copy(
                w_hbm.at[c], weight.at[:, pl.ds(c * LOCAL, LOCAL)], w_sem.at[c]
            )
            for c in range(3)
        ]
    else:
        w_copies = [pltpu.make_async_copy(w_hbm, weight, w_sem.at[0])]
    for copy in w_copies:
        copy.start()
    if back:
        sums.fetch(up_all, 0, 0)
    at.meet()

    def columns(ref, t, block):
        return ref[t, :, :, block * HEAD_DIM : (block + 1) * HEAD_DIM].reshape(256, HEAD_DIM)

    def put(i, block, value):
        out[i, :, :, block * HEAD_DIM : (block + 1) * HEAD_DIM] = value.astype(BF).reshape(
            16, 16, HEAD_DIM
        )

    def attend(i):
        slot = 1 - lax.div(i, 2)
        xh = lax.rem(i, 2)
        t = 2 * xh + lax.rem(at.lo + slot, 2)
        for h in range(HEADS):
            query, key, value = (columns(qkv, t, c * HEADS + h) for c in range(3))
            probs = softmax(query, key)
            low = probs.astype(BF)
            if not back:
                put(i, h, jnp.dot(low, value, preferred_element_type=F32))
                continue
            grad_in = columns(grad, t, h)
            dprob = dot_nt(grad_in, value)
            put(i, 2 * HEADS + h, dot_tn(low, grad_in))
            dscore = (probs * (dprob - jnp.sum(probs * dprob, -1, keepdims=True))).astype(BF)
            for c, normed, product in (
                (0, query, jnp.dot(dscore, key, preferred_element_type=F32)),
                (1, key, dot_tn(dscore, query)),
            ):
                step_in = (product * INV_ROOT).astype(BF).astype(F32)
                wide = normed.astype(F32)
                put(
                    i,
                    c * HEADS + h,
                    step_in - wide * jnp.mean(step_in * wide, -1, keepdims=True),
                )
        xi = 2 * xh + at.core

        def give(f):
            src = out.at[i, f]
            dst = tokens.at[slot, xi, at.group]

            @pl.when(f == at.fr)
            def _():
                pltpu.make_async_copy(src, dst, o_recv.at[slot, xi]).start()

            @pl.when(f != at.fr)
            def _():
                remote(src, dst, o_send.at[i], o_recv.at[slot, xi], (f, at.fs)).start()

        loop(16, give)

    loop(4, attend)
    if back:
        loop(8, sums.out_rows)
    for copy in w_copies:
        copy.wait()

    def take(slot, xi):
        landed(tokens.at[slot, xi], o_recv.at[slot, xi])
        if back:
            for j in range(3 * HEADS):
                cols = slice(j * HEAD_DIM, (j + 1) * HEAD_DIM)
                block = tokens[slot, xi, :, :, cols].reshape(2 * HALF, HEAD_DIM)
                if j < 2 * HEADS:
                    block = (block.astype(F32) * factors[slot, xi, :, j : j + 1]).astype(BF)
                dproj[slot, xi, :, cols] = block

    xl, xr, xf = at.along(3), at.along(1), at.along(2)

    def tile_loop(body):
        loop(WIDTH // TILE, lambda j: body(pl.ds(pl.multiple_of(j * TILE, TILE), TILE)))

    def products(slot, p, into):
        pair = (at.along(1 + p), at.along(3 - 3 * p))
        source = dproj if back else tokens
        rows = jnp.concatenate([source[slot, xi].reshape(2 * HALF, -1) for xi in pair])

        def tiles(tile):
            if back:
                value = dot_nt(rows, weight[tile, :])
            else:
                value = jnp.dot(rows, weight[:, tile], preferred_element_type=F32)
            value = value.astype(BF)
            for n, xi in enumerate(pair):
                some = value[n * 2 * HALF : (n + 1) * 2 * HALF]
                into[xi, :, :, tile] = some.reshape(2, HALF, TILE)

        tile_loop(tiles)

    def add(into, xi, h, other):
        def tiles(tile):
            value = into[xi, h, :, tile].astype(F32) + other[:, tile].astype(F32)
            into[xi, h, :, tile] = value.astype(BF)

        tile_loop(tiles)

    def to_side(xi, h):
        return remote(
            part.at[xi, h], from_side.at[xi, h], y_send.at[xi, h], y_recv.at[xi, h], at.side[h]
        )

    def side_arrived(xi, h):
        landed(from_side.at[xi, h], y_recv.at[xi, h])
        add(mine, xi, h, from_side.at[xi, h])

    pass_copies = [
        remote(part.at[xr, 0], passed.at[0], p_send.at[0], p_recv.at[0], at.right),
        remote(part.at[xl, 1], passed.at[1], p_send.at[1], p_recv.at[1], at.left),
    ]
    far_copies = [
        remote(mine.at[xf, 0], far.at[0], f_send.at[0], f_recv.at[0], at.right),
        remote(mine.at[xf, 1], far.at[1], f_send.at[1], f_recv.at[1], at.left),
    ]
    near_copies = [
        remote(mine.at[xr, 1], near.at[0, 1], n_send.at[0, 1], n_recv.at[0, 1], at.right),
        remote(mine.at[xl, 0], near.at[1, 0], n_send.at[1, 0], n_recv.at[1, 0], at.left),
        remote(mine.at[xr, 0], near.at[0, 0], n_send.at[0, 0], n_recv.at[0, 0], at.right),
        remote(mine.at[xl, 1], near.at[1, 1], n_send.at[1, 1], n_recv.at[1, 1], at.left),
    ]

    def first(p):
        take(1, at.along(1 + p))
        take(1, at.along(3 - 3 * p))
        products(1, p, part)

        @pl.when(p == 0)
        def _():
            pass_copies[0].start()
            pass_copies[1].start()
            to_side(xr, 1).start()
            to_side(xl, 0).start()

    loop(2, first)
    if back:
        loop(4, lambda xi: take(0, xi))
        loop(2, sums.tile)

    def second(p):
        if not back:
            take(0, at.along(1 + p))
            take(0, at.along(3 - 3 * p))
        products(0, p, mine)

        @pl.when(p == 0)
        def _():
            for h in range(2):
                to_side((xl, xr)[h], h).wait_send()
                to_side(xf, h).start()
            for h in range(2):
                landed(passed.at[h], p_recv.at[h])
                add(part, at.x, h, passed.at[h])
            side_arrived(xr, 1)
            near_copies[0].start()
            side_arrived(xl, 0)
            near_copies[1].start()

        if back:
            loop(2, lambda q: sums.tile(2 + 2 * p + q))

    loop(2, second)
    for h in range(2):
        to_side(xf, h).wait_send()
        to_side(at.x, h).start()
    for h in range(2):
        side_arrived(xf, h)
        far_copies[h].start()
    if back:
        loop(2, lambda q: sums.tile(6 + q))
        sums.merge(7)
    for d, xi in ((0, xr), (1, xl)):
        landed(far.at[d], f_recv.at[d])
        add(mine, xi, d, far.at[d])
        near_copies[2 + d].start()
    if back:
        sums.relay(1)
    for h in range(2):
        side_arrived(at.x, h)
    if back:
        sums.turn()
    for d, h in ((0, 1), (1, 0), (0, 0), (1, 1)):
        landed(near.at[d, h], n_recv.at[d, h])

    def finish(j):
        tile = pl.ds(pl.multiple_of(j * TILE, TILE), TILE)
        for h in range(2):
            total[h * HALF : (h + 1) * HALF, tile] = (
                mine[at.x, h, :, tile].astype(F32)
                + near[0, h, :, tile].astype(F32)
                + near[1, h, :, tile].astype(F32)
            )

    loop(WIDTH // TILE, finish)
    if back:
        sums.finish()
    for copy in pass_copies + far_copies + near_copies:
        copy.wait_send()
    for h in range(2):
        to_side(at.x, h).wait_send()

    loop(4, lambda i: landed(out.at[i, pl.ds(0, 15)], o_send.at[i]))


def scatter(args, weight, back, streamed=()):
    cols = 3 * LOCAL if back else LOCAL
    token_shape = (2, 4, 8, 16, cols)
    shapes = [jax.ShapeDtypeStruct((2 * HALF, WIDTH), F32)]
    scratch = [
        pltpu.VMEM((WIDTH, cols) if back else (LOCAL, WIDTH), BF),
        pltpu.VMEM((4, 16, 16, cols), BF),
        pltpu.VMEM((4, 2, HALF, WIDTH), BF),
        pltpu.VMEM((4, 2, HALF, WIDTH), BF),
        pltpu.VMEM((4, 2, HALF, WIDTH), BF),
        pltpu.VMEM((2, HALF, WIDTH), BF),
        pltpu.VMEM((2, 2, HALF, WIDTH), BF),
        pltpu.VMEM((2, HALF, WIDTH), BF),
        pltpu.SemaphoreType.DMA((4,)),
        pltpu.SemaphoreType.DMA((2, 4)),
        pltpu.SemaphoreType.DMA((4, 2)),
        pltpu.SemaphoreType.DMA((4, 2)),
        pltpu.SemaphoreType.DMA((2,)),
        pltpu.SemaphoreType.DMA((2,)),
        pltpu.SemaphoreType.DMA((2, 2)),
        pltpu.SemaphoreType.DMA((2, 2)),
        pltpu.SemaphoreType.DMA((2,)),
        pltpu.SemaphoreType.DMA((2,)),
        pltpu.SemaphoreType.DMA((3,)),
    ]
    if back:
        shapes.append(jax.ShapeDtypeStruct((4, 192, LOCAL), BF))
        scratch += [
            pltpu.VMEM(token_shape, BF),
            pltpu.VMEM((2, 4, 2 * HALF, cols), BF),
            pltpu.VMEM((2, 1024, LOCAL), BF),
            pltpu.VMEM((LOCAL, 1024), BF),
            pltpu.VMEM((8, 2, 192, 4 * LOCAL), BF),
            pltpu.VMEM((8, 192, 4 * LOCAL), BF),
            pltpu.VMEM((2, 2, 96, 4 * LOCAL), BF),
            pltpu.VMEM((2, 2, 2, 96, 4 * LOCAL), BF),
            pltpu.VMEM((192, 4 * LOCAL), BF),
            pltpu.SemaphoreType.DMA((2,)),
            pltpu.SemaphoreType.DMA((8,)),
            pltpu.SemaphoreType.DMA((8,)),
            pltpu.SemaphoreType.DMA((2, 2)),
            pltpu.SemaphoreType.DMA((2, 2)),
            pltpu.SemaphoreType.DMA((2, 2, 2)),
            pltpu.SemaphoreType.DMA((2, 2, 2)),
            pltpu.SemaphoreType.DMA,
            pltpu.SemaphoreType.DMA,
        ]
    else:
        shapes.append(jax.ShapeDtypeStruct(token_shape, BF))
    return pl.pallas_call(
        functools.partial(scatter_kernel, back),
        out_shape=shapes,
        in_specs=vmem(len(args)) + [pl.BlockSpec(memory_space=pl.ANY)] * (1 + len(streamed)),
        out_specs=vmem(len(shapes)),
        scratch_shapes=scratch,
        compiler_params=pltpu.CompilerParams(
            collective_id=3 if back else 1,
            has_side_effects=True,
            vmem_limit_bytes=VMEM_BYTES,
        ),
        cost_estimate=pl.CostEstimate(
            flops=2 * 1024 * WIDTH * cols, bytes_accessed=30_000_000, transcendentals=0
        ),
        name="scatter_back" if back else "scatter_mixed",
    )(*args, weight, *streamed)


def total_kernel(own, result, by_head, by_frame, partial, s1, r1, s2, r2, s3, r3):
    fr = lax.axis_index("frame")
    fs = lax.axis_index("fsdp")
    barrier = pltpu.get_barrier_semaphore()

    def head(i):
        return (fr, lax.rem(fs + i, 8))

    def frame(i):
        return (lax.rem(fr + i, 16), fs)

    def greet(peer):
        pl.semaphore_signal(barrier, inc=1, device_id=peer, device_id_type=MESH)

    for i in range(1, 8):
        greet(head(i))
    loop(15, lambda i: greet(frame(i + 1)))
    pl.semaphore_wait(barrier, 22)

    firsts = [
        remote(own.at[head(i)[1]], by_head.at[fs], s1.at[i], r1, head(i)) for i in range(1, 8)
    ]
    for copy in firsts:
        copy.start()
    by_head[fs] = own[fs]
    landed(by_head.at[pl.ds(0, 7)], r1)
    value = by_head[0]
    for i in range(1, 8):
        value = value + by_head[i]
    partial[...] = value
    by_frame[fr] = value
    seconds = [
        remote(partial, by_frame.at[fr], s2.at[i], r2, frame(i)) for i in range(1, 16)
    ]
    for copy in seconds:
        copy.start()
    landed(by_frame.at[pl.ds(0, 15)], r2)
    value = by_frame[0]
    for i in range(1, 16):
        value = value + by_frame[i]
    result[fs] = value
    thirds = [remote(result.at[fs], result.at[fs], s3.at[i], r3, head(i)) for i in range(1, 8)]
    for copy in thirds:
        copy.start()
    landed(result.at[pl.ds(0, 7)], r3)
    for copy in firsts + seconds + thirds:
        copy.wait_send()


def total_sums(rows):
    pieces = jnp.pad(rows.reshape(3, 8, LOCAL).transpose(1, 0, 2), ((0, 0), (0, 5), (0, 0)))
    result = pl.pallas_call(
        total_kernel,
        out_shape=jax.ShapeDtypeStruct((8, 8, LOCAL), F32),
        in_specs=vmem(1),
        out_specs=vmem(1)[0],
        scratch_shapes=[
            pltpu.VMEM((8, 8, LOCAL), F32),
            pltpu.VMEM((16, 8, LOCAL), F32),
            pltpu.VMEM((8, LOCAL), F32),
            pltpu.SemaphoreType.DMA((8,)),
            pltpu.SemaphoreType.DMA,
            pltpu.SemaphoreType.DMA((16,)),
            pltpu.SemaphoreType.DMA,
            pltpu.SemaphoreType.DMA((8,)),
            pltpu.SemaphoreType.DMA,
        ],
        compiler_params=pltpu.CompilerParams(collective_id=4, has_side_effects=True),
        name="total_sums",
    )(pieces)
    return result[:, :3].transpose(1, 0, 2).reshape(3, WIDTH)


def to_rows(block):
    frames, patches, width = block.shape
    return block.reshape(frames, 8, 8, width).transpose(1, 0, 2, 3).reshape(-1, width)


def from_rows(rows):
    return rows.reshape(8, 2, 8, -1).transpose(1, 0, 2, 3).reshape(2, 64, -1)


def shards(hidden_states, teacher, mod_scale, mod_shift, out_gate, w_qkv, w_out):
    states = to_rows(hidden_states).astype(F32)
    factor = lax.rsqrt(jnp.mean(states * states, -1, keepdims=True) + 1e-06)
    normed = states * factor
    modded = (normed * (1.0 + mod_scale) + mod_shift).astype(BF)
    flat, qkv, factors = gather(modded.reshape(2, HALF, WIDTH), w_qkv, True)
    mixed, attended = scatter([qkv], w_out, False)
    diff = states + out_gate * mixed - to_rows(teacher).astype(F32)
    upstream = (out_gate * diff).astype(BF)
    up_all, grad_att = gather(upstream.reshape(2, HALF, WIDTH), w_out, False)
    dmod, w_grad = scatter(
        [qkv, grad_att, factors, attended.reshape(1024, LOCAL)],
        w_qkv,
        True,
        (flat.reshape(1024, WIDTH), up_all.reshape(1024, WIDTH)),
    )
    sums = total_sums(
        jnp.stack([jnp.sum(dmod * normed, 0), jnp.sum(dmod, 0), jnp.sum(diff * mixed, 0)])
    )
    dnorm = dmod * (1.0 + mod_scale)
    grad_hidden = (
        diff + factor * (dnorm - normed * jnp.mean(dnorm * normed, -1, keepdims=True))
    ).astype(BF)
    return (from_rows(grad_hidden), w_grad[:3], w_grad[3].T, sums[0], sums[1], sums[2])


def solution(mesh):
    in_specs = (
        P("frame", "fsdp", None),
        P("frame", "fsdp", None),
        P(),
        P(),
        P(),
        P(None, None, "fsdp"),
        P("fsdp", None),
    )
    out_specs = (
        P("frame", "fsdp", None),
        P(None, "frame", "fsdp"),
        P("fsdp", "frame"),
        P(),
        P(),
        P(),
    )
    return jax.shard_map(shards, mesh=mesh, in_specs=in_specs, out_specs=out_specs, check_vma=False)
```

```python
import functools
import jax
import jax.numpy as jnp
from jax import lax
from jax.experimental import pallas as pl
from jax.experimental.pallas import tpu as pltpu
from jax.sharding import PartitionSpec as P

HEAD_DIM = 128
HEADS = 3
LOCAL = 384
WIDTH = 3072
HALF = 64
TILE = 512
INV_ROOT = HEAD_DIM ** (-0.5)
MESH = pl.DeviceIdType.MESH
BF = jnp.bfloat16
F32 = jnp.float32
VMEM_BYTES = 60 * 1024 * 1024


class Place:
    def __init__(self):
        fr = lax.axis_index("frame")
        fs = lax.axis_index("fsdp")
        self.fr = fr
        self.fs = fs
        self.x = lax.div(fs, 2)
        self.lo = lax.rem(fs, 2)
        self.core = lax.rem(fr, 2)
        self.group = lax.div(fr, 2)
        other = fs + 1 - 2 * self.lo
        hi = lax.rem(self.group, 2)
        self.right = (fr, lax.rem(fs + 2, 8))
        self.left = (fr, lax.rem(fs + 6, 8))
        self.side = ((fr, other), (fr + 2 - 4 * hi, other))

    def along(self, off):
        return lax.rem(self.x + off, 4)

    def greet(self, heads):
        barrier = pltpu.get_barrier_semaphore()

        def signal(peer):
            pl.semaphore_signal(barrier, inc=1, device_id=peer, device_id_type=MESH)

        signal(self.side[1])
        if heads:
            for step in range(1, 8):
                signal((self.fr, lax.rem(self.fs + step, 8)))
        else:
            for peer in (self.right, self.left, self.side[0]):
                signal(peer)
        loop(15, lambda i: signal((lax.rem(self.fr + i + 1, 16), self.fs)))

    def met(self, heads):
        pl.semaphore_wait(pltpu.get_barrier_semaphore(), 23 if heads else 19)


def remote(src, dst, send_sem, recv_sem, device):
    return pltpu.make_async_remote_copy(
        src_ref=src,
        dst_ref=dst,
        send_sem=send_sem,
        recv_sem=recv_sem,
        device_id=device,
        device_id_type=MESH,
    )


def landed(ref, sem):
    pltpu.make_async_copy(ref, ref, sem).wait()


def loop(count, body):
    def step(i, carry):
        body(i)
        return carry

    lax.fori_loop(0, count, step, 0)


def others_first(p):
    return 2 + p - lax.div(3 * p * (p - 1), 2)


def load_weight(w_hbm, weight, sem):
    if len(w_hbm.shape) == 3:
        copies = [
            pltpu.make_async_copy(w_hbm.at[c], weight.at[:, pl.ds(c * LOCAL, LOCAL)], sem.at[c])
            for c in range(3)
        ]
    else:
        copies = [pltpu.make_async_copy(w_hbm, weight, sem.at[0])]
    for copy in copies:
        copy.start()
    return copies


def gather_phase(at, own, weight, w_copies, kept_all, sent_to, factors, scratch, between=None):
    full, out, x_send, y_send, recv, o_send, o_recv, keep_sem = scratch
    project = factors is not None

    def to_right(slot, src, xi, h, n):
        return remote(src, full.at[slot, xi, h], x_send.at[n], recv.at[slot, xi, h], at.right)

    def to_left(slot, src, xi, h, n):
        return remote(src, full.at[slot, xi, h], x_send.at[n], recv.at[slot, xi, h], at.left)

    def to_side(src, xi, h, n):
        return remote(src, full.at[1, xi, h], y_send.at[n], recv.at[1, xi, h], at.side[h])

    xl, xr, xf = at.along(3), at.along(1), at.along(2)
    first = [
        to_right(0, own.at[0], at.x, 0, 0),
        to_left(0, own.at[1], at.x, 1, 1),
        to_side(own.at[0], at.x, 0, 0),
        to_side(own.at[1], at.x, 1, 1),
    ]
    for copy in first:
        copy.start()
    full[0, at.x] = own[...]
    second = [
        to_right(0, full.at[0, xl, 0], xl, 0, 2),
        to_left(0, full.at[0, xr, 1], xr, 1, 3),
    ]
    if not project:
        second.append(to_side(full.at[0, xl, 0], xl, 0, 2))
        second.append(to_side(full.at[0, xr, 1], xr, 1, 3))
    third = [
        to_right(0, own.at[1], at.x, 1, 4),
        to_side(full.at[0, xf, 0], xf, 0, 4),
        to_left(0, own.at[0], at.x, 0, 5),
        to_side(full.at[0, xf, 1], xf, 1, 5),
    ]
    fourth = [
        to_right(1, full.at[1, at.x, 1], at.x, 1, 6),
        to_left(1, full.at[1, at.x, 0], at.x, 0, 7),
    ]
    if project:
        fourth.append(to_right(1, full.at[1, at.x, 0], at.x, 0, 8))
        fourth.append(to_left(1, full.at[1, at.x, 1], at.x, 1, 9))
    for copy in w_copies:
        copy.wait()

    def arrived(slot, xi, h):
        landed(full.at[slot, xi, h], recv.at[slot, xi, h])

    def early(k):
        @pl.when(k == 1)
        def _():
            arrived(0, xl, 0)
            for copy in second[0::2]:
                copy.start()
            arrived(0, xr, 1)
            for copy in second[1::2]:
                copy.start()
            arrived(1, at.x, 0)
            arrived(1, at.x, 1)

        work(k, k, at.x)

    def late(i):
        slot = lax.div(i, 3)
        xi = at.along(others_first(lax.rem(i, 3)))

        @pl.when(i == 0)
        def _():
            arrived(0, xf, 0)
            third[0].start()
            third[1].start()
            arrived(0, xf, 1)
            third[2].start()
            third[3].start()

        @pl.when(i == 1)
        def _():
            arrived(0, xl, 1)
            for copy in fourth[0::2]:
                copy.start()

        @pl.when(i == 2)
        def _():
            arrived(0, xr, 0)
            for copy in fourth[1::2]:
                copy.start()

        if between is not None:
            pl.when(i == 4)(between)

        @pl.when(i >= 3)
        def _():
            arrived(1, xi, 0)
            arrived(1, xi, 1)

        work(i + 2, slot, xi)

    def work(k, slot, xi):
        pltpu.make_async_copy(full.at[slot, xi], kept_all.at[slot, xi], keep_sem).start()
        tokens = full[slot, xi].reshape(2 * HALF, WIDTH)
        if project:
            both = jnp.dot(tokens, weight[...], preferred_element_type=F32)
            lane = lax.broadcasted_iota(jnp.int32, (2 * HALF, HEAD_DIM), 1)
            kept = jnp.zeros((2 * HALF, HEAD_DIM), F32)
            for j in range(3 * HEADS):
                block = both[:, j * HEAD_DIM : (j + 1) * HEAD_DIM]
                if j < 2 * HEADS:
                    factor = lax.rsqrt(jnp.mean(block * block, -1, keepdims=True) + 1e-06)
                    kept = jnp.where(lane == j, factor, kept)
                    block = block * factor
                out[k, :, :, j * HEAD_DIM : (j + 1) * HEAD_DIM] = block.astype(BF).reshape(
                    8, 16, HEAD_DIM
                )
            factors[slot, xi] = kept
        else:
            both = lax.dot_general(
                tokens, weight[...], (((1,), (1,)), ((), ())), preferred_element_type=F32
            )
            out[k] = both.astype(BF).reshape(8, 16, LOCAL)
        to_core = lax.rem(xi, 2)
        to_slot = 2 * lax.div(xi, 2) + lax.rem(at.lo + slot, 2)

        def give(g):
            target = 2 * g + to_core
            src = out.at[k, g]
            dst = sent_to.at[to_slot, at.fr]

            @pl.when(target == at.fr)
            def _():
                pltpu.make_async_copy(src, dst, o_recv.at[to_slot]).start()

            @pl.when(target != at.fr)
            def _():
                remote(src, dst, o_send.at[g], o_recv.at[to_slot], (target, at.fs)).start()

        loop(8, give)

    loop(2, early)
    loop(6, late)

    def drain(g):
        @pl.when(g == at.group)
        def _():
            landed(out.at[pl.ds(0, 4), g], o_send.at[g])

        @pl.when(g != at.group)
        def _():
            landed(out.at[:, g], o_send.at[g])

    def end():
        for copy in first + second + third + fourth:
            copy.wait_send()
        loop(8, drain)
        pltpu.make_async_copy(full, kept_all, keep_sem).wait()

    return end


def gather_scratch(cols):
    return [
        pltpu.VMEM((2, 4, 2, HALF, WIDTH), BF),
        pltpu.VMEM((8, 8, 16, cols), BF),
        pltpu.SemaphoreType.DMA((10,)),
        pltpu.SemaphoreType.DMA((6,)),
        pltpu.SemaphoreType.DMA((2, 4, 2)),
        pltpu.SemaphoreType.DMA((8,)),
        pltpu.SemaphoreType.DMA((4,)),
        pltpu.SemaphoreType.DMA,
    ]


def vmem(count):
    return [pl.BlockSpec(memory_space=pltpu.VMEM)] * count


def anywhere(count):
    return [pl.BlockSpec(memory_space=pl.ANY)] * count


def same_patch():
    rows = lax.broadcasted_iota(jnp.int32, (256, 256), 0)
    cols = lax.broadcasted_iota(jnp.int32, (256, 256), 1)
    return lax.rem(rows, 8) == lax.rem(cols, 8)


def dot_nt(a, b):
    return lax.dot_general(a, b, (((1,), (1,)), ((), ())), preferred_element_type=F32)


def dot_tn(a, b):
    return lax.dot_general(a, b, (((0,), (0,)), ((), ())), preferred_element_type=F32)


def softmax(query, key):
    scores = dot_nt(query, key) * INV_ROOT
    expo = jnp.where(same_patch(), jnp.exp(scores), 0.0)
    return expo / jnp.sum(expo, -1, keepdims=True)


class WeightSums:
    def __init__(self, at, flat, up_all, attended, dproj, result, *scratch):
        self.at = at
        self.flat, self.up_all, self.attended, self.dproj = flat, up_all, attended, dproj
        self.result = result
        (
            self.rows, self.turned, self.part, self.twin, self.far, self.near, self.last,
            self.row_sem, self.t_send, self.t_recv, self.f_send, self.f_recv,
            self.n_send, self.n_recv, self.l_send, self.l_recv,
        ) = scratch
        fr, fs = at.fr, at.fs
        self.hi = lax.rem(at.group, 2)
        self.z = lax.div(at.group, 2)
        self.sibling = (fr + 1 - 2 * at.core, fs)
        self.over = (fr + 2 - 4 * self.hi, fs)
        self.up = (lax.rem(fr + 4, 16), fs)
        self.down = (lax.rem(fr + 12, 16), fs)

    def group(self, off, hi):
        return 2 * lax.rem(self.z + off, 4) + hi

    def flagged(self, flag):
        return flag * self.hi + (1 - flag) * (1 - self.hi)

    def target(self, m):
        q, b = lax.div(m, 2), lax.rem(m, 2)
        inner = lax.div(q * (3 - q), 2)
        base = 2 - q + lax.div(q * (q - 1), 2) - lax.div(q * (q - 1) * (q - 2), 3)
        flag = (1 - inner) * b + inner * (q - 1)
        return self.group(base + 2 * inner * b, self.flagged(flag))

    def load(self, source, j, slot):
        cols = pl.ds(pl.multiple_of(j * LOCAL, LOCAL), LOCAL)
        return pltpu.make_async_copy(
            source.at[:, cols], self.rows.at[slot], self.row_sem.at[slot]
        )

    def fetch(self, source, j, slot):
        self.load(source, j, slot).start()

    def out_rows(self, m):
        slot = lax.rem(m, 2)
        self.load(self.up_all, m, slot).wait()

        @pl.when(m < 7)
        def _():
            self.fetch(self.up_all, m + 1, 1 - slot)

        @pl.when(m == 7)
        def _():
            self.fetch(self.flat, self.target(0), 0)

        self.turned[...] = jnp.transpose(self.rows[slot])
        value = jnp.dot(self.turned[...], self.attended[...], preferred_element_type=F32)
        self.part[m, :, :, 3 * LOCAL :] = value.astype(BF).reshape(2, 192, LOCAL)

    def to_twin(self, j):
        return remote(
            self.part.at[j, 1 - self.at.core],
            self.twin.at[j],
            self.t_send.at[j],
            self.t_recv.at[j],
            self.sibling,
        )

    def rows_of(self, off, flag, half):
        j = self.group(off, self.flagged(flag))
        return self.part.at[j, self.at.core, pl.ds(half * 96, 96)]

    def to_far(self, d, flag):
        return remote(
            self.rows_of(2, flag, d), self.far.at[d, flag], self.f_send.at[d, flag],
            self.f_recv.at[d, flag], (self.up, self.down)[d],
        )

    def to_near(self, d, flag, half):
        return remote(
            self.rows_of((1, 3)[d], flag, half), self.near.at[d, flag, half],
            self.n_send.at[d, flag, half], self.n_recv.at[d, flag, half],
            (self.up, self.down)[d],
        )

    def tile(self, m):
        j = self.target(m)
        slot = lax.rem(m, 2)
        self.load(self.flat, j, slot).wait()

        @pl.when(m < 7)
        def _():
            self.fetch(self.flat, self.target(m + 1), 1 - slot)

        self.turned[...] = jnp.transpose(self.rows[slot])
        for c in range(3):
            cols = slice(c * LOCAL, (c + 1) * LOCAL)
            other = self.dproj[:, :, :, cols].reshape(1024, LOCAL)
            value = jnp.dot(self.turned[...], other, preferred_element_type=F32)
            self.part[j, :, :, cols] = value.astype(BF).reshape(2, 192, LOCAL)
        self.to_twin(j).start()

        @pl.when(m > 0)
        def _():
            self.merge(m - 1)

    def add(self, held, other, count):
        def rows(i):
            some = pl.ds(pl.multiple_of(i * 48, 16), 48)
            held[some, :] = (held[some, :].astype(F32) + other[some, :].astype(F32)).astype(BF)

        loop(count, rows)

    def merge(self, m):
        j = self.target(m)
        landed(self.twin.at[j], self.t_recv.at[j])
        self.add(self.part.at[j, self.at.core], self.twin.at[j], 4)
        for flag in range(2):

            @pl.when(m == flag)
            def _(flag=flag):
                for d in range(2):
                    self.to_far(d, flag).start()

            @pl.when(m == 2 + 2 * flag)
            def _(flag=flag):
                if flag == 1:
                    self.relay(0)
                self.to_near(0, flag, 1).start()

            @pl.when(m == 3 + 2 * flag)
            def _(flag=flag):
                self.to_near(1, flag, 0).start()

    def relay(self, flag):
        for d in range(2):
            landed(self.far.at[d, flag], self.f_recv.at[d, flag])
            self.add(self.rows_of((1, 3)[d], flag, d), self.far.at[d, flag], 2)
            self.to_near(d, flag, d).start()

    def arrived(self, flag):
        for d in range(2):
            for half in range(2):
                landed(self.near.at[d, flag, half], self.n_recv.at[d, flag, half])

    def both(self, flag, half, some):
        value = self.rows_of(0, flag, half)[some, :].astype(F32)
        for d in range(2):
            value = value + self.near[d, flag, half, some, :].astype(F32)
        return value

    def to_last(self):
        source = self.part.at[self.group(0, self.flagged(0)), self.at.core]
        return remote(source, self.last, self.l_send, self.l_recv, self.over)

    def turn(self):
        self.arrived(0)
        for half in range(2):
            held = self.rows_of(0, 0, half)

            def rows(i, half=half, held=held):
                some = pl.ds(pl.multiple_of(i * 48, 16), 48)
                held[some, :] = self.both(0, half, some).astype(BF)

            loop(2, rows)
        self.to_last().start()

    def finish(self):
        self.arrived(1)
        landed(self.last, self.l_recv)
        for half in range(2):

            def end(i, half=half):
                some = pl.ds(pl.multiple_of(i * 48, 16), 48)
                there = pl.ds(pl.multiple_of(half * 96 + i * 48, 16), 48)
                value = self.both(1, half, some) + self.last[there, :].astype(F32)
                value = value.astype(BF)
                for c in range(4):
                    self.result[c, there, :] = value[:, c * LOCAL : (c + 1) * LOCAL]

            loop(2, end)
        for d in range(2):
            for flag in range(2):
                self.to_far(d, flag).wait_send()
                for half in range(2):
                    self.to_near(d, flag, half).wait_send()
        self.to_last().wait_send()
        loop(8, lambda j: self.to_twin(j).wait_send())


def tile_loop(body):
    loop(WIDTH // TILE, lambda j: body(pl.ds(pl.multiple_of(j * TILE, TILE), TILE)))


class Scatter:
    def __init__(self, at, qkv, qkv_sem, grad, weight, tokens, dproj, factors, scratch):
        self.at, self.qkv, self.qkv_sem, self.grad = at, qkv, qkv_sem, grad
        self.weight, self.tokens, self.dproj, self.factors = weight, tokens, dproj, factors
        (
            self.out, self.part, self.own, self.from_side, self.far, self.near, self.passed,
            self.o_send, self.o_recv, self.y_send, self.y_recv, self.f_send, self.f_recv,
            self.n_send, self.n_recv, self.p_send, self.p_recv,
        ) = scratch
        self.back = grad is not None
        self.xl, self.xr, self.xf = at.along(3), at.along(1), at.along(2)

    def put(self, i, block, value):
        cols = slice(block * HEAD_DIM, (block + 1) * HEAD_DIM)
        self.out[i, :, :, cols] = value.astype(BF).reshape(16, 16, HEAD_DIM)

    def attend(self, i):
        at, put = self.at, self.put
        slot = lax.div(i, 2)
        if self.back:
            slot = 1 - slot
        xh = lax.rem(lax.div(at.x, 2) + i, 2)
        t = 2 * xh + lax.rem(at.lo + slot, 2)
        if self.qkv_sem is not None:
            landed(self.qkv.at[t], self.qkv_sem.at[t])

        def columns(ref, block):
            return ref[t, :, :, block * HEAD_DIM : (block + 1) * HEAD_DIM].reshape(256, HEAD_DIM)

        for h in range(HEADS):
            query, key, value = (columns(self.qkv, c * HEADS + h) for c in range(3))
            probs = softmax(query, key)
            low = probs.astype(BF)
            if not self.back:
                put(i, h, jnp.dot(low, value, preferred_element_type=F32))
                continue
            grad_in = columns(self.grad, h)
            dprob = dot_nt(grad_in, value)
            put(i, 2 * HEADS + h, dot_tn(low, grad_in))
            dscore = (probs * (dprob - jnp.sum(probs * dprob, -1, keepdims=True))).astype(BF)
            for c, normed, product in (
                (0, query, jnp.dot(dscore, key, preferred_element_type=F32)),
                (1, key, dot_tn(dscore, query)),
            ):
                step_in = (product * INV_ROOT).astype(BF).astype(F32)
                wide = normed.astype(F32)
                put(
                    i,
                    c * HEADS + h,
                    step_in - wide * jnp.mean(step_in * wide, -1, keepdims=True),
                )
        xi = 2 * xh + at.core

        def give(f):
            src = self.out.at[i, f]
            dst = self.tokens.at[slot, xi, at.group]

            @pl.when(f == at.fr)
            def _():
                pltpu.make_async_copy(src, dst, self.o_recv.at[slot, xi]).start()

            @pl.when(f != at.fr)
            def _():
                remote(
                    src, dst, self.o_send.at[i], self.o_recv.at[slot, xi], (f, at.fs)
                ).start()

        loop(16, give)

    def take(self, slot, xi):
        landed(self.tokens.at[slot, xi], self.o_recv.at[slot, xi])
        if self.back:
            for j in range(3 * HEADS):
                cols = slice(j * HEAD_DIM, (j + 1) * HEAD_DIM)
                block = self.tokens[slot, xi, :, :, cols].reshape(2 * HALF, HEAD_DIM)
                if j < 2 * HEADS:
                    block = (block.astype(F32) * self.factors[slot, xi, :, j : j + 1]).astype(BF)
                self.dproj[slot, xi, :, cols] = block

    def pair(self, p):
        return self.at.along(1 + p), self.at.along(3 - 3 * p)

    def products(self, slot, p, into):
        pair = self.pair(p)
        source = self.dproj if self.back else self.tokens
        rows = jnp.concatenate([source[slot, xi].reshape(2 * HALF, -1) for xi in pair])

        def tiles(tile):
            if self.back:
                value = dot_nt(rows, self.weight[tile, :])
            else:
                value = jnp.dot(rows, self.weight[:, tile], preferred_element_type=F32)
            value = value.astype(BF)
            for n, xi in enumerate(pair):
                some = value[n * 2 * HALF : (n + 1) * 2 * HALF]
                into[xi, :, :, tile] = some.reshape(2, HALF, TILE)

        tile_loop(tiles)

    def add(self, into, xi, h, other):
        def tiles(tile):
            value = into[xi, h, :, tile].astype(F32) + other[:, tile].astype(F32)
            into[xi, h, :, tile] = value.astype(BF)

        tile_loop(tiles)

    def to_side(self, xi, h):
        return remote(
            self.part.at[xi, h], self.from_side.at[xi, h], self.y_send.at[xi, h],
            self.y_recv.at[xi, h], self.at.side[h],
        )

    def side_arrived(self, xi, h):
        landed(self.from_side.at[xi, h], self.y_recv.at[xi, h])
        self.add(self.own, xi, h, self.from_side.at[xi, h])

    def way(self, d):
        return (self.at.right, self.at.left)[d]

    def pass_on(self, d):
        source = self.part.at[(self.xr, self.xl)[d], d]
        return remote(source, self.passed.at[d], self.p_send.at[d], self.p_recv.at[d], self.way(d))

    def to_far(self, d):
        source = self.own.at[self.xf, d]
        return remote(source, self.far.at[d], self.f_send.at[d], self.f_recv.at[d], self.way(d))

    def to_near(self, d, h):
        source = self.own.at[(self.xr, self.xl)[d], h]
        return remote(
            source, self.near.at[d, h], self.n_send.at[d, h], self.n_recv.at[d, h], self.way(d)
        )

    def add_passed(self):
        for h in range(2):
            landed(self.passed.at[h], self.p_recv.at[h])
            self.add(self.part, self.at.x, h, self.passed.at[h])

    def sides_to_near(self):
        self.side_arrived(self.xr, 1)
        self.to_near(0, 1).start()
        self.side_arrived(self.xl, 0)
        self.to_near(1, 0).start()

    def sides_to_far(self):
        for h in range(2):
            self.side_arrived(self.xf, h)
            self.to_far(h).start()

    def far_to_near(self):
        for d, xi in ((0, self.xr), (1, self.xl)):
            landed(self.far.at[d], self.f_recv.at[d])
            self.add(self.own, xi, d, self.far.at[d])
            self.to_near(d, d).start()

    def arrive(self):
        for d, h in ((0, 1), (1, 0), (0, 0), (1, 1)):
            landed(self.near.at[d, h], self.n_recv.at[d, h])

    def total(self, h, some):
        return (
            self.own[self.at.x, h, some, :].astype(F32)
            + self.near[0, h, some, :].astype(F32)
            + self.near[1, h, some, :].astype(F32)
        )

    def forward(self):
        x = self.at.x
        for slot, into in ((1, self.part), (0, self.own)):
            for xi in self.pair(1):
                self.take(slot, xi)
            self.products(slot, 1, into)
            if slot == 1:
                for h in range(2):
                    self.to_side(self.xf, h).start()
        for xi in self.pair(0):
            self.take(1, xi)
        self.products(1, 0, self.part)
        self.pass_on(0).start()
        self.pass_on(1).start()
        for h in range(2):
            self.to_side(self.xf, h).wait_send()
            self.to_side((self.xl, self.xr)[h], h).start()
        self.sides_to_far()
        for xi in self.pair(0):
            self.take(0, xi)
        self.products(0, 0, self.own)
        self.add_passed()
        for h in range(2):
            self.to_side((self.xl, self.xr)[h], h).wait_send()
            self.to_side(x, h).start()
        self.sides_to_near()
        self.far_to_near()
        for h in range(2):
            self.side_arrived(x, h)
        self.arrive()

    def backward(self, sums):
        x = self.at.x

        def first(p):
            for xi in self.pair(p):
                self.take(1, xi)
            self.products(1, p, self.part)

            @pl.when(p == 0)
            def _():
                for d in range(2):
                    self.pass_on(d).start()
                    self.to_side((self.xl, self.xr)[d], d).start()

        loop(2, first)
        loop(4, lambda xi: self.take(0, xi))
        loop(2, sums.tile)

        def second(p):
            self.products(0, p, self.own)

            @pl.when(p == 0)
            def _():
                for h in range(2):
                    self.to_side((self.xl, self.xr)[h], h).wait_send()
                    self.to_side(self.xf, h).start()
                self.add_passed()
                self.sides_to_near()

            loop(2, lambda q: sums.tile(2 + 2 * p + q))

        loop(2, second)
        for h in range(2):
            self.to_side(self.xf, h).wait_send()
            self.to_side(x, h).start()
        self.sides_to_far()
        loop(2, lambda q: sums.tile(6 + q))
        sums.merge(7)
        self.far_to_near()
        sums.relay(1)
        for h in range(2):
            self.side_arrived(x, h)
        sums.turn()
        self.arrive()

    def end(self):
        for d in range(2):
            self.pass_on(d).wait_send()
            self.to_far(d).wait_send()
            for h in range(2):
                self.to_near(d, h).wait_send()
            self.to_side(self.at.x, d).wait_send()
        loop(4, lambda i: landed(self.out.at[i, pl.ds(0, 15)], self.o_send.at[i]))


def scatter_scratch(cols):
    return [
        pltpu.VMEM((4, 16, 16, cols), BF),
        pltpu.VMEM((4, 2, HALF, WIDTH), BF),
        pltpu.VMEM((4, 2, HALF, WIDTH), BF),
        pltpu.VMEM((4, 2, HALF, WIDTH), BF),
        pltpu.VMEM((2, HALF, WIDTH), BF),
        pltpu.VMEM((2, 2, HALF, WIDTH), BF),
        pltpu.VMEM((2, HALF, WIDTH), BF),
        pltpu.SemaphoreType.DMA((4,)),
        pltpu.SemaphoreType.DMA((2, 4)),
        pltpu.SemaphoreType.DMA((4, 2)),
        pltpu.SemaphoreType.DMA((4, 2)),
        pltpu.SemaphoreType.DMA((2,)),
        pltpu.SemaphoreType.DMA((2,)),
        pltpu.SemaphoreType.DMA((2, 2)),
        pltpu.SemaphoreType.DMA((2, 2)),
        pltpu.SemaphoreType.DMA((2,)),
        pltpu.SemaphoreType.DMA((2,)),
    ]


def each_rows(body):
    def step(i):
        inner = pl.ds(pl.multiple_of(lax.rem(i, 4) * 16, 16), 16)
        body(lax.div(i, 4), inner, pl.ds(pl.multiple_of(i * 16, 16), 16))

    loop(8, step)


def row_factor(states):
    return lax.rsqrt(jnp.mean(states * states, -1, keepdims=True) + 1e-06)


def front_kernel(
    hidden, teacher, scale, shift, gate, w_qkv, w_out,
    kept_modded, kept_up, qkv, factors, tokens, grad_att, diff, gate_rows,
    own, own_up, qkv_weight, out_weight, w_sem, *scratch,
):
    at = Place()
    qkv_copies = load_weight(w_qkv, qkv_weight, w_sem.at[0])
    out_copies = load_weight(w_out, out_weight, w_sem.at[1])
    at.greet(False)

    def modulate(h, inner, some):
        states = hidden[some, :].astype(F32)
        value = states * row_factor(states) * (1.0 + scale[...]) + shift[...]
        own[h, inner, :] = value.astype(BF)

    each_rows(modulate)
    at.met(False)
    ahead, middle, behind = scratch[:8], scratch[8:25], scratch[25:]
    mix = Scatter(at, qkv, ahead[6], None, out_weight, tokens, None, None, middle)
    end_ahead = gather_phase(
        at, own, qkv_weight, qkv_copies, kept_modded, qkv, factors, ahead,
        lambda: loop(2, mix.attend),
    )
    loop(2, lambda i: mix.attend(2 + i))
    for copy in out_copies:
        copy.wait()
    mix.forward()
    gate_rows[...] = jnp.zeros_like(gate_rows)

    def compare(h, inner, some):
        mixed = mix.total(h, inner)
        change = hidden[some, :].astype(F32) + gate[...] * mixed - teacher[some, :].astype(F32)
        diff[some, :] = change
        own_up[h, inner, :] = (gate[...] * change).astype(BF)
        both = change * mixed
        gate_rows[...] += both[:8] + both[8:]

    each_rows(compare)
    end_behind = gather_phase(at, own_up, out_weight, [], kept_up, grad_att, None, behind)
    end_ahead()
    mix.end()
    end_behind()
    loop(4, lambda t: landed(grad_att.at[t], behind[6].at[t]))


def front(hidden, teacher, scale, shift, gate, w_qkv, w_out):
    kept = jax.ShapeDtypeStruct((2, 4, 2, HALF, WIDTH), BF)
    return pl.pallas_call(
        front_kernel,
        out_shape=[
            kept,
            kept,
            jax.ShapeDtypeStruct((4, 16, 16, 3 * LOCAL), BF),
            jax.ShapeDtypeStruct((2, 4, 2 * HALF, HEAD_DIM), F32),
            jax.ShapeDtypeStruct((2, 4, 8, 16, LOCAL), BF),
            jax.ShapeDtypeStruct((4, 16, 16, LOCAL), BF),
            jax.ShapeDtypeStruct((2 * HALF, WIDTH), F32),
            jax.ShapeDtypeStruct((8, WIDTH), F32),
        ],
        in_specs=vmem(5) + anywhere(2),
        out_specs=anywhere(2) + vmem(6),
        scratch_shapes=[
            pltpu.VMEM((2, HALF, WIDTH), BF),
            pltpu.VMEM((2, HALF, WIDTH), BF),
            pltpu.VMEM((WIDTH, 3 * LOCAL), BF),
            pltpu.VMEM((LOCAL, WIDTH), BF),
            pltpu.SemaphoreType.DMA((2, 3)),
        ]
        + gather_scratch(3 * LOCAL)
        + scatter_scratch(LOCAL)
        + gather_scratch(LOCAL),
        compiler_params=pltpu.CompilerParams(
            collective_id=0, has_side_effects=True, vmem_limit_bytes=VMEM_BYTES
        ),
        cost_estimate=pl.CostEstimate(
            flops=2 * 1024 * WIDTH * 5 * LOCAL, bytes_accessed=50_000_000, transcendentals=0
        ),
        name="front",
    )(hidden, teacher, scale, shift, gate, w_qkv, w_out)


class Totals:
    def __init__(self, at, rows, result, scratch):
        self.at, self.rows, self.result = at, rows, result
        (
            self.by_head, self.by_frame, self.partial,
            self.s1, self.r1, self.s2, self.r2, self.s3, self.r3,
        ) = scratch
        self.started = []

    def piece(self, ref, i):
        return ref.at[:, pl.ds(pl.multiple_of(i * LOCAL, LOCAL), LOCAL)]

    def send(self, copies):
        for copy in copies:
            copy.start()
        self.started += copies

    def head(self, i):
        return (self.at.fr, lax.rem(self.at.fs + i, 8))

    def run(self, between):
        fr, fs = self.at.fr, self.at.fs
        self.send(
            [
                remote(
                    self.piece(self.rows, self.head(i)[1]), self.by_head.at[fs], self.s1.at[i],
                    self.r1, self.head(i),
                )
                for i in range(1, 8)
            ]
        )
        self.by_head[fs] = self.piece(self.rows, fs)[...]
        between()
        landed(self.by_head.at[pl.ds(0, 7)], self.r1)
        value = self.by_head[0]
        for i in range(1, 8):
            value = value + self.by_head[i]
        self.partial[...] = value
        self.by_frame[fr] = value
        self.send(
            [
                remote(
                    self.partial, self.by_frame.at[fr], self.s2.at[i], self.r2,
                    (lax.rem(fr + i, 16), fs),
                )
                for i in range(1, 16)
            ]
        )
        landed(self.by_frame.at[pl.ds(0, 15)], self.r2)
        value = self.by_frame[0]
        for i in range(1, 16):
            value = value + self.by_frame[i]
        here = self.piece(self.result, fs)
        here[...] = value
        self.send(
            [remote(here, here, self.s3.at[i], self.r3, self.head(i)) for i in range(1, 8)]
        )

    def end(self):
        landed(self.result.at[:, pl.ds(0, 7 * LOCAL)], self.r3)
        for copy in self.started:
            copy.wait_send()


def rear_kernel(
    hidden, diff, gate_rows, scale, qkv, grad, factors, attended, w_qkv, modded, up_all,
    grad_hidden, w_grad, totals, weight, w_sem, tokens, dproj, scale_rows, shift_rows, rows,
    *scratch,
):
    at = Place()
    w_copies = load_weight(w_qkv, weight, w_sem)
    sums = WeightSums(at, modded, up_all, attended, dproj, w_grad, *scratch[17:33])
    sums.fetch(up_all, 0, 0)
    at.greet(True)
    at.met(True)
    back = Scatter(at, qkv, None, grad, weight, tokens, dproj, factors, scratch[:17])
    loop(4, back.attend)
    loop(8, sums.out_rows)
    for copy in w_copies:
        copy.wait()
    back.backward(sums)
    scale_rows[...] = jnp.zeros_like(scale_rows)
    shift_rows[...] = jnp.zeros_like(shift_rows)

    def close(h, inner, some):
        dmod = back.total(h, inner)
        states = hidden[some, :].astype(F32)
        factor = row_factor(states)
        normed = states * factor
        both = dmod * normed
        scale_rows[...] += both[:8] + both[8:]
        shift_rows[...] += dmod[:8] + dmod[8:]
        wide = both * (1.0 + scale[...])
        dnorm = dmod * (1.0 + scale[...])
        value = dnorm - normed * jnp.mean(wide, -1, keepdims=True)
        grad_hidden[some, :] = (diff[some, :] + factor * value).astype(BF)

    each_rows(close)
    rows[...] = jnp.zeros_like(rows)
    for i, ref in enumerate((scale_rows, shift_rows, gate_rows)):
        rows[i : i + 1, :] = jnp.sum(ref[...], 0, keepdims=True)
    total = Totals(at, rows, totals, scratch[33:])
    total.run(sums.finish)
    total.end()
    back.end()


def rear(hidden, diff, gate_rows, scale, qkv, grad, factors, attended, w_qkv, modded, up_all):
    cols = 3 * LOCAL
    return pl.pallas_call(
        rear_kernel,
        out_shape=[
            jax.ShapeDtypeStruct((2 * HALF, WIDTH), BF),
            jax.ShapeDtypeStruct((4, 192, LOCAL), BF),
            jax.ShapeDtypeStruct((8, WIDTH), F32),
        ],
        in_specs=vmem(8) + anywhere(3),
        out_specs=vmem(3),
        scratch_shapes=[
            pltpu.VMEM((WIDTH, cols), BF),
            pltpu.SemaphoreType.DMA((3,)),
            pltpu.VMEM((2, 4, 8, 16, cols), BF),
            pltpu.VMEM((2, 4, 2 * HALF, cols), BF),
            pltpu.VMEM((8, WIDTH), F32),
            pltpu.VMEM((8, WIDTH), F32),
            pltpu.VMEM((8, WIDTH), F32),
        ]
        + scatter_scratch(cols)
        + [
            pltpu.VMEM((2, 1024, LOCAL), BF),
            pltpu.VMEM((LOCAL, 1024), BF),
            pltpu.VMEM((8, 2, 192, 4 * LOCAL), BF),
            pltpu.VMEM((8, 192, 4 * LOCAL), BF),
            pltpu.VMEM((2, 2, 96, 4 * LOCAL), BF),
            pltpu.VMEM((2, 2, 2, 96, 4 * LOCAL), BF),
            pltpu.VMEM((192, 4 * LOCAL), BF),
            pltpu.SemaphoreType.DMA((2,)),
            pltpu.SemaphoreType.DMA((8,)),
            pltpu.SemaphoreType.DMA((8,)),
            pltpu.SemaphoreType.DMA((2, 2)),
            pltpu.SemaphoreType.DMA((2, 2)),
            pltpu.SemaphoreType.DMA((2, 2, 2)),
            pltpu.SemaphoreType.DMA((2, 2, 2)),
            pltpu.SemaphoreType.DMA,
            pltpu.SemaphoreType.DMA,
        ]
        + [
            pltpu.VMEM((8, 8, LOCAL), F32),
            pltpu.VMEM((16, 8, LOCAL), F32),
            pltpu.VMEM((8, LOCAL), F32),
            pltpu.SemaphoreType.DMA((8,)),
            pltpu.SemaphoreType.DMA,
            pltpu.SemaphoreType.DMA((16,)),
            pltpu.SemaphoreType.DMA,
            pltpu.SemaphoreType.DMA((8,)),
            pltpu.SemaphoreType.DMA,
        ],
        compiler_params=pltpu.CompilerParams(
            collective_id=1, has_side_effects=True, vmem_limit_bytes=VMEM_BYTES
        ),
        cost_estimate=pl.CostEstimate(
            flops=2 * 1024 * WIDTH * 7 * LOCAL, bytes_accessed=50_000_000, transcendentals=0
        ),
        name="rear",
    )(hidden, diff, gate_rows, scale, qkv, grad, factors, attended, w_qkv, modded, up_all)


def to_rows(block):
    frames, patches, width = block.shape
    return block.reshape(frames, 8, 8, width).transpose(1, 0, 2, 3).reshape(-1, width)


def from_rows(rows):
    return rows.reshape(8, 2, 8, -1).transpose(1, 0, 2, 3).reshape(2, 64, -1)


def shards(hidden_states, teacher, mod_scale, mod_shift, out_gate, w_qkv, w_out):
    hidden = to_rows(hidden_states)
    scale = mod_scale.reshape(1, WIDTH)
    modded, up_all, qkv, factors, attended, grad_att, diff, gate_rows = front(
        hidden,
        to_rows(teacher),
        scale,
        mod_shift.reshape(1, WIDTH),
        out_gate.reshape(1, WIDTH),
        w_qkv,
        w_out,
    )
    grad_hidden, w_grad, sums = rear(
        hidden,
        diff,
        gate_rows,
        scale,
        qkv,
        grad_att,
        factors,
        attended.reshape(1024, LOCAL),
        w_qkv,
        modded.reshape(1024, WIDTH),
        up_all.reshape(1024, WIDTH),
    )
    return (from_rows(grad_hidden), w_grad[:3], w_grad[3].T, sums[0], sums[1], sums[2])


def solution(mesh):
    in_specs = (
        P("frame", "fsdp", None),
        P("frame", "fsdp", None),
        P(),
        P(),
        P(),
        P(None, None, "fsdp"),
        P("fsdp", None),
    )
    out_specs = (
        P("frame", "fsdp", None),
        P(None, "frame", "fsdp"),
        P("fsdp", "frame"),
        P(),
        P(),
        P(),
    )
    return jax.shard_map(shards, mesh=mesh, in_specs=in_specs, out_specs=out_specs, check_vma=False)
```

```python
import functools
import jax
import jax.numpy as jnp
from jax import lax
from jax.experimental import pallas as pl
from jax.experimental.pallas import tpu as pltpu
from jax.sharding import PartitionSpec as P

HEAD_DIM = 128
HEADS = 3
LOCAL = 384
WIDTH = 3072
HALF = 64
TILE = 512
INV_ROOT = HEAD_DIM ** (-0.5)
MESH = pl.DeviceIdType.MESH
BF = jnp.bfloat16
F32 = jnp.float32
VMEM_BYTES = 60 * 1024 * 1024


class Place:
    def __init__(self):
        fr = lax.axis_index("frame")
        fs = lax.axis_index("fsdp")
        self.fr = fr
        self.fs = fs
        self.x = lax.div(fs, 2)
        self.lo = lax.rem(fs, 2)
        self.core = lax.rem(fr, 2)
        self.group = lax.div(fr, 2)
        other = fs + 1 - 2 * self.lo
        self.hi = lax.rem(self.group, 2)
        self.z = lax.div(self.group, 2)
        self.right = (fr, lax.rem(fs + 2, 8))
        self.left = (fr, lax.rem(fs + 6, 8))
        self.side = tuple((self.frame(self.z, h, self.core), other) for h in range(2))
        self.across = (fr + 2 - 4 * self.hi, other)
        self.beside = (fr, other)

    def frame(self, z, hi, core):
        return 4 * z + 2 * hi + core

    def along(self, off):
        return lax.rem(self.x + off, 4)

    def greet(self, heads):
        barrier = pltpu.get_barrier_semaphore()

        def signal(peer):
            pl.semaphore_signal(barrier, inc=1, device_id=peer, device_id_type=MESH)

        signal(self.across)
        if heads:
            for step in range(1, 8):
                signal((self.fr, lax.rem(self.fs + step, 8)))
        else:
            for peer in (self.right, self.left, self.beside):
                signal(peer)
        loop(15, lambda i: signal((lax.rem(self.fr + i + 1, 16), self.fs)))

    def met(self, heads):
        pl.semaphore_wait(pltpu.get_barrier_semaphore(), 23 if heads else 19)


def remote(src, dst, send_sem, recv_sem, device):
    return pltpu.make_async_remote_copy(
        src_ref=src,
        dst_ref=dst,
        send_sem=send_sem,
        recv_sem=recv_sem,
        device_id=device,
        device_id_type=MESH,
    )


def landed(ref, sem):
    pltpu.make_async_copy(ref, ref, sem).wait()


def loop(count, body):
    def step(i, carry):
        body(i)
        return carry

    lax.fori_loop(0, count, step, 0)


def others_first(p):
    return 2 + p - lax.div(3 * p * (p - 1), 2)


def load_weight(w_hbm, weight, sem):
    if len(w_hbm.shape) == 3:
        copies = [
            pltpu.make_async_copy(w_hbm.at[c], weight.at[:, pl.ds(c * LOCAL, LOCAL)], sem.at[c])
            for c in range(3)
        ]
    else:
        copies = [pltpu.make_async_copy(w_hbm, weight, sem.at[0])]
    for copy in copies:
        copy.start()
    return copies


def gather_phase(at, own, weight, w_copies, kept_all, sent_to, factors, scratch, between=None):
    full, out, x_send, y_send, recv, o_send, o_recv, keep_sem = scratch
    project = factors is not None

    def to_right(slot, src, xi, h, n):
        return remote(src, full.at[slot, xi, h], x_send.at[n], recv.at[slot, xi, h], at.right)

    def to_left(slot, src, xi, h, n):
        return remote(src, full.at[slot, xi, h], x_send.at[n], recv.at[slot, xi, h], at.left)

    def to_side(src, xi, h, n):
        return remote(
            src, full.at[1, xi, at.hi], y_send.at[n], recv.at[1, xi, at.hi], at.side[h]
        )

    xl, xr, xf = at.along(3), at.along(1), at.along(2)
    first = [
        to_right(0, own.at[0], at.x, 0, 0),
        to_left(0, own.at[1], at.x, 1, 1),
        to_side(own.at[0], at.x, 0, 0),
        to_side(own.at[1], at.x, 1, 1),
    ]
    for copy in first:
        copy.start()
    full[0, at.x] = own[...]
    second = [
        to_right(0, full.at[0, xl, 0], xl, 0, 2),
        to_left(0, full.at[0, xr, 1], xr, 1, 3),
    ]
    third = [
        to_right(0, own.at[1], at.x, 1, 4),
        to_side(full.at[0, xf, 0], xf, 0, 4),
        to_left(0, own.at[0], at.x, 0, 5),
        to_side(full.at[0, xf, 1], xf, 1, 5),
    ]
    fourth = [
        to_right(1, full.at[1, at.x, 1], at.x, 1, 6),
        to_left(1, full.at[1, at.x, 0], at.x, 0, 7),
    ]
    if project:
        fourth.append(to_right(1, full.at[1, at.x, 0], at.x, 0, 8))
        fourth.append(to_left(1, full.at[1, at.x, 1], at.x, 1, 9))
    early_sides = [to_side(full.at[0, (xl, xr)[h], h], (xl, xr)[h], h, 2) for h in range(2)]
    late_sides = [to_side(full.at[0, (xl, xr)[h], 1 - h], (xl, xr)[h], 1 - h, 3) for h in range(2)]
    for copy in w_copies:
        copy.wait()

    def arrived(slot, xi, h):
        landed(full.at[slot, xi, h], recv.at[slot, xi, h])

    def early(k):
        @pl.when(k == 1)
        def _():
            arrived(0, xl, 0)
            second[0].start()
            if not project:
                pl.when(at.hi == 0)(lambda: early_sides[0].start())
            arrived(0, xr, 1)
            second[1].start()
            if not project:
                pl.when(at.hi == 1)(lambda: early_sides[1].start())
            arrived(1, at.x, 0)
            arrived(1, at.x, 1)

        work(k, k, at.x)

    def late(i):
        slot = lax.div(i, 3)
        xi = at.along(others_first(lax.rem(i, 3)))

        @pl.when(i == 0)
        def _():
            arrived(0, xf, 0)
            third[0].start()
            third[1].start()
            arrived(0, xf, 1)
            third[2].start()
            third[3].start()

        @pl.when(i == 1)
        def _():
            arrived(0, xl, 1)
            for copy in fourth[0::2]:
                copy.start()
            if not project:
                pl.when(at.hi == 0)(lambda: late_sides[0].start())

        @pl.when(i == 2)
        def _():
            arrived(0, xr, 0)
            for copy in fourth[1::2]:
                copy.start()
            if not project:
                pl.when(at.hi == 1)(lambda: late_sides[1].start())

        if between is not None:
            pl.when(i == 4)(between)

        @pl.when(i >= 3)
        def _():
            arrived(1, xi, 0)
            arrived(1, xi, 1)

        work(i + 2, slot, xi)

    def work(k, slot, xi):
        pltpu.make_async_copy(full.at[slot, xi], kept_all.at[slot, xi], keep_sem).start()
        tokens = full[slot, xi].reshape(2 * HALF, WIDTH)
        if project:
            both = jnp.dot(tokens, weight[...], preferred_element_type=F32)
            lane = lax.broadcasted_iota(jnp.int32, (2 * HALF, HEAD_DIM), 1)
            kept = jnp.zeros((2 * HALF, HEAD_DIM), F32)
            for j in range(3 * HEADS):
                block = both[:, j * HEAD_DIM : (j + 1) * HEAD_DIM]
                if j < 2 * HEADS:
                    factor = lax.rsqrt(jnp.mean(block * block, -1, keepdims=True) + 1e-06)
                    kept = jnp.where(lane == j, factor, kept)
                    block = block * factor
                out[pl.ds(8 * k, 8), :, j * HEAD_DIM : (j + 1) * HEAD_DIM] = block.astype(BF).reshape(
                    8, 16, HEAD_DIM
                )
            factors[slot, xi] = kept
        else:
            both = lax.dot_general(
                tokens, weight[...], (((1,), (1,)), ((), ())), preferred_element_type=F32
            )
            out[pl.ds(8 * k, 8)] = both.astype(BF).reshape(8, 16, LOCAL)
        to_core = lax.rem(xi, 2)
        to_slot = 2 * lax.div(xi, 2) + lax.rem(at.lo + slot, 2)

        def give(b):
            z, upper = lax.rem(b, 4), lax.div(b, 4)
            target = at.frame(z, (1 - slot) * upper + slot * at.hi, to_core)
            origin = at.frame(at.z, (1 - slot) * at.hi + slot * upper, at.core)
            src = out.at[8 * k + b]
            dst = sent_to.at[to_slot, origin]

            @pl.when(target == at.fr)
            def _():
                pltpu.make_async_copy(src, dst, o_recv.at[to_slot]).start()

            @pl.when(target != at.fr)
            def _():
                remote(src, dst, o_send, o_recv.at[to_slot], (target, at.fs)).start()

        loop(8, give)

    loop(2, early)
    loop(6, late)

    def end():
        for copy in first + second + third + fourth:
            copy.wait_send()
        for h in range(0 if project else 2):

            @pl.when(at.hi == h)
            def _(h=h):
                early_sides[h].wait_send()
                late_sides[h].wait_send()

        landed(out.at[pl.ds(0, 58)], o_send)
        pltpu.make_async_copy(full, kept_all, keep_sem).wait()

    return end


def gather_scratch(cols):
    return [
        pltpu.VMEM((2, 4, 2, HALF, WIDTH), BF),
        pltpu.VMEM((64, 16, cols), BF),
        pltpu.SemaphoreType.DMA((10,)),
        pltpu.SemaphoreType.DMA((6,)),
        pltpu.SemaphoreType.DMA((2, 4, 2)),
        pltpu.SemaphoreType.DMA,
        pltpu.SemaphoreType.DMA((4,)),
        pltpu.SemaphoreType.DMA,
    ]


def vmem(count):
    return [pl.BlockSpec(memory_space=pltpu.VMEM)] * count


def anywhere(count):
    return [pl.BlockSpec(memory_space=pl.ANY)] * count


def same_patch():
    rows = lax.broadcasted_iota(jnp.int32, (256, 256), 0)
    cols = lax.broadcasted_iota(jnp.int32, (256, 256), 1)
    return lax.rem(rows, 8) == lax.rem(cols, 8)


def dot_nt(a, b):
    return lax.dot_general(a, b, (((1,), (1,)), ((), ())), preferred_element_type=F32)


def dot_tn(a, b):
    return lax.dot_general(a, b, (((0,), (0,)), ((), ())), preferred_element_type=F32)


def softmax(query, key):
    scores = dot_nt(query, key) * INV_ROOT
    expo = jnp.where(same_patch(), jnp.exp(scores), 0.0)
    return expo / jnp.sum(expo, -1, keepdims=True)


class WeightSums:
    def __init__(self, at, flat, up_all, attended, dproj, result, *scratch):
        self.at = at
        self.flat, self.up_all, self.attended, self.dproj = flat, up_all, attended, dproj
        self.result = result
        (
            self.rows, self.turned, self.part, self.twin, self.far, self.near, self.last,
            self.row_sem, self.t_send, self.t_recv, self.f_send, self.f_recv,
            self.n_send, self.n_recv, self.l_send, self.l_recv,
        ) = scratch
        fr, fs = at.fr, at.fs
        self.hi = lax.rem(at.group, 2)
        self.z = lax.div(at.group, 2)
        self.sibling = (fr + 1 - 2 * at.core, fs)
        self.over = (fr + 2 - 4 * self.hi, fs)
        self.up = (lax.rem(fr + 4, 16), fs)
        self.down = (lax.rem(fr + 12, 16), fs)

    def group(self, off, hi):
        return 2 * lax.rem(self.z + off, 4) + hi

    def flagged(self, flag):
        return flag * self.hi + (1 - flag) * (1 - self.hi)

    def target(self, m):
        q, b = lax.div(m, 2), lax.rem(m, 2)
        inner = lax.div(q * (3 - q), 2)
        base = 2 - q + lax.div(q * (q - 1), 2) - lax.div(q * (q - 1) * (q - 2), 3)
        flag = (1 - inner) * b + inner * (q - 1)
        return self.group(base + 2 * inner * b, self.flagged(flag))

    def load(self, source, j, slot):
        cols = pl.ds(pl.multiple_of(j * LOCAL, LOCAL), LOCAL)
        return pltpu.make_async_copy(
            source.at[:, cols], self.rows.at[slot], self.row_sem.at[slot]
        )

    def fetch(self, source, j, slot):
        self.load(source, j, slot).start()

    def out_rows(self, m):
        slot = lax.rem(m, 2)
        self.load(self.up_all, m, slot).wait()

        @pl.when(m < 7)
        def _():
            self.fetch(self.up_all, m + 1, 1 - slot)

        @pl.when(m == 7)
        def _():
            self.fetch(self.flat, self.target(0), 0)

        self.turned[...] = jnp.transpose(self.rows[slot])
        value = jnp.dot(self.turned[...], self.attended[...], preferred_element_type=F32)
        self.part[m, :, :, 3 * LOCAL :] = value.astype(BF).reshape(2, 192, LOCAL)

    def to_twin(self, j):
        return remote(
            self.part.at[j, 1 - self.at.core],
            self.twin.at[j],
            self.t_send.at[j],
            self.t_recv.at[j],
            self.sibling,
        )

    def rows_of(self, off, flag, half):
        j = self.group(off, self.flagged(flag))
        return self.part.at[j, self.at.core, pl.ds(half * 96, 96)]

    def to_far(self, d, flag):
        return remote(
            self.rows_of(2, flag, d), self.far.at[d, flag], self.f_send.at[d, flag],
            self.f_recv.at[d, flag], (self.up, self.down)[d],
        )

    def to_near(self, d, flag, half):
        return remote(
            self.rows_of((1, 3)[d], flag, half), self.near.at[d, flag, half],
            self.n_send.at[d, flag, half], self.n_recv.at[d, flag, half],
            (self.up, self.down)[d],
        )

    def tile(self, m):
        j = self.target(m)
        slot = lax.rem(m, 2)
        self.load(self.flat, j, slot).wait()

        @pl.when(m < 7)
        def _():
            self.fetch(self.flat, self.target(m + 1), 1 - slot)

        self.turned[...] = jnp.transpose(self.rows[slot])
        for c in range(3):
            cols = slice(c * LOCAL, (c + 1) * LOCAL)
            other = self.dproj[:, :, :, cols].reshape(1024, LOCAL)
            value = jnp.dot(self.turned[...], other, preferred_element_type=F32)
            self.part[j, :, :, cols] = value.astype(BF).reshape(2, 192, LOCAL)
        self.to_twin(j).start()

        @pl.when(m > 0)
        def _():
            self.merge(m - 1)

    def add(self, held, other, count):
        def rows(i):
            some = pl.ds(pl.multiple_of(i * 48, 16), 48)
            held[some, :] = (held[some, :].astype(F32) + other[some, :].astype(F32)).astype(BF)

        loop(count, rows)

    def merge(self, m):
        j = self.target(m)
        landed(self.twin.at[j], self.t_recv.at[j])
        self.add(self.part.at[j, self.at.core], self.twin.at[j], 4)
        for flag in range(2):

            @pl.when(m == flag)
            def _(flag=flag):
                for d in range(2):
                    self.to_far(d, flag).start()

            @pl.when(m == 2 + 2 * flag)
            def _(flag=flag):
                if flag == 1:
                    self.relay(0)
                self.to_near(0, flag, 1).start()

            @pl.when(m == 3 + 2 * flag)
            def _(flag=flag):
                self.to_near(1, flag, 0).start()

    def relay(self, flag):
        for d in range(2):
            landed(self.far.at[d, flag], self.f_recv.at[d, flag])
            self.add(self.rows_of((1, 3)[d], flag, d), self.far.at[d, flag], 2)
            self.to_near(d, flag, d).start()

    def arrived(self, flag):
        for d in range(2):
            for half in range(2):
                landed(self.near.at[d, flag, half], self.n_recv.at[d, flag, half])

    def both(self, flag, half, some):
        value = self.rows_of(0, flag, half)[some, :].astype(F32)
        for d in range(2):
            value = value + self.near[d, flag, half, some, :].astype(F32)
        return value

    def to_last(self):
        source = self.part.at[self.group(0, self.flagged(0)), self.at.core]
        return remote(source, self.last, self.l_send, self.l_recv, self.over)

    def turn(self):
        self.arrived(0)
        for half in range(2):
            held = self.rows_of(0, 0, half)

            def rows(i, half=half, held=held):
                some = pl.ds(pl.multiple_of(i * 48, 16), 48)
                held[some, :] = self.both(0, half, some).astype(BF)

            loop(2, rows)
        self.to_last().start()

    def finish(self):
        self.arrived(1)
        landed(self.last, self.l_recv)
        for half in range(2):

            def end(i, half=half):
                some = pl.ds(pl.multiple_of(i * 48, 16), 48)
                there = pl.ds(pl.multiple_of(half * 96 + i * 48, 16), 48)
                value = self.both(1, half, some) + self.last[there, :].astype(F32)
                value = value.astype(BF)
                for c in range(3):
                    self.result[0][c, there, :] = value[:, c * LOCAL : (c + 1) * LOCAL]
                self.result[1][there, :] = value[:, 3 * LOCAL :]

            loop(2, end)
        for d in range(2):
            for flag in range(2):
                self.to_far(d, flag).wait_send()
                for half in range(2):
                    self.to_near(d, flag, half).wait_send()
        self.to_last().wait_send()
        loop(8, lambda j: self.to_twin(j).wait_send())


def tile_loop(body):
    loop(WIDTH // TILE, lambda j: body(pl.ds(pl.multiple_of(j * TILE, TILE), TILE)))


class Scatter:
    def __init__(self, at, qkv, qkv_sem, grad, weight, tokens, dproj, factors, scratch):
        self.at, self.qkv, self.qkv_sem, self.grad = at, qkv, qkv_sem, grad
        self.weight, self.tokens, self.dproj, self.factors = weight, tokens, dproj, factors
        (
            self.out, self.part, self.own, self.from_side, self.far, self.near, self.passed,
            self.o_send, self.o_recv, self.y_send, self.y_recv, self.f_send, self.f_recv,
            self.n_send, self.n_recv, self.p_send, self.p_recv,
        ) = scratch
        self.back = grad is not None
        self.xl, self.xr, self.xf = at.along(3), at.along(1), at.along(2)

    def put(self, i, block, value):
        cols = slice(block * HEAD_DIM, (block + 1) * HEAD_DIM)
        self.out[i, :, :, cols] = value.astype(BF).reshape(16, 16, HEAD_DIM)

    def attend(self, i):
        at, put = self.at, self.put
        slot = lax.div(i, 2)
        if self.back:
            slot = 1 - slot
        xh = lax.rem(lax.div(at.x, 2) + i, 2)
        t = 2 * xh + lax.rem(at.lo + slot, 2)
        if self.qkv_sem is not None:
            landed(self.qkv.at[t], self.qkv_sem.at[t])

        def columns(ref, block):
            return ref[t, :, :, block * HEAD_DIM : (block + 1) * HEAD_DIM].reshape(256, HEAD_DIM)

        for h in range(HEADS):
            query, key, value = (columns(self.qkv, c * HEADS + h) for c in range(3))
            probs = softmax(query, key)
            low = probs.astype(BF)
            if not self.back:
                put(i, h, jnp.dot(low, value, preferred_element_type=F32))
                continue
            grad_in = columns(self.grad, h)
            dprob = dot_nt(grad_in, value)
            put(i, 2 * HEADS + h, dot_tn(low, grad_in))
            dscore = (probs * (dprob - jnp.sum(probs * dprob, -1, keepdims=True))).astype(BF)
            for c, normed, product in (
                (0, query, jnp.dot(dscore, key, preferred_element_type=F32)),
                (1, key, dot_tn(dscore, query)),
            ):
                step_in = (product * INV_ROOT).astype(BF).astype(F32)
                wide = normed.astype(F32)
                put(
                    i,
                    c * HEADS + h,
                    step_in - wide * jnp.mean(step_in * wide, -1, keepdims=True),
                )
        xi = 2 * xh + at.core

        def give(f):
            upper = lax.rem(lax.div(f, 2), 2)
            target = f + 2 * slot * (at.hi - upper)
            piece = 4 * ((1 - slot) * at.hi + slot * upper) + at.z
            src = self.out.at[i, f]
            dst = self.tokens.at[slot, xi, piece]

            @pl.when(target == at.fr)
            def _():
                pltpu.make_async_copy(src, dst, self.o_recv.at[slot, xi]).start()

            @pl.when(target != at.fr)
            def _():
                remote(
                    src, dst, self.o_send.at[i], self.o_recv.at[slot, xi], (target, at.fs)
                ).start()

        loop(16, give)

    def take(self, slot, xi):
        landed(self.tokens.at[slot, xi], self.o_recv.at[slot, xi])
        if self.back:
            for j in range(3 * HEADS):
                cols = slice(j * HEAD_DIM, (j + 1) * HEAD_DIM)
                block = self.tokens[slot, xi, :, :, cols].reshape(2 * HALF, HEAD_DIM)
                if j < 2 * HEADS:
                    block = (block.astype(F32) * self.factors[slot, xi, :, j : j + 1]).astype(BF)
                self.dproj[slot, xi, :, cols] = block

    def pair(self, p):
        return self.at.along(1 + p), self.at.along(3 - 3 * p)

    def products(self, slot, p, into):
        pair = self.pair(p)
        source = self.dproj if self.back else self.tokens
        rows = jnp.concatenate([source[slot, xi].reshape(2 * HALF, -1) for xi in pair])

        def tiles(tile):
            if self.back:
                value = dot_nt(rows, self.weight[tile, :])
            else:
                value = jnp.dot(rows, self.weight[:, tile], preferred_element_type=F32)
            value = value.astype(BF)
            for n, xi in enumerate(pair):
                some = value[n * 2 * HALF : (n + 1) * 2 * HALF]
                into[xi, :, :, tile] = some.reshape(2, HALF, TILE)

        tile_loop(tiles)

    def add(self, into, xi, h, other):
        def tiles(tile):
            value = into[xi, h, :, tile].astype(F32) + other[:, tile].astype(F32)
            into[xi, h, :, tile] = value.astype(BF)

        tile_loop(tiles)

    def to_side(self, xi, h):
        return remote(
            self.part.at[xi, h], self.from_side.at[xi, self.at.hi], self.y_send.at[xi, h],
            self.y_recv.at[xi, self.at.hi], self.at.side[h],
        )

    def side_arrived(self, xi, h):
        landed(self.from_side.at[xi, h], self.y_recv.at[xi, h])
        self.add(self.own, xi, h, self.from_side.at[xi, h])

    def way(self, d):
        return (self.at.right, self.at.left)[d]

    def pass_on(self, d):
        source = self.part.at[(self.xr, self.xl)[d], d]
        return remote(source, self.passed.at[d], self.p_send.at[d], self.p_recv.at[d], self.way(d))

    def to_far(self, d):
        source = self.own.at[self.xf, d]
        return remote(source, self.far.at[d], self.f_send.at[d], self.f_recv.at[d], self.way(d))

    def to_near(self, d, h):
        source = self.own.at[(self.xr, self.xl)[d], h]
        return remote(
            source, self.near.at[d, h], self.n_send.at[d, h], self.n_recv.at[d, h], self.way(d)
        )

    def add_passed(self):
        for h in range(2):
            landed(self.passed.at[h], self.p_recv.at[h])
            self.add(self.part, self.at.x, h, self.passed.at[h])

    def sides_to_near(self):
        for h in range(2):
            self.side_arrived(self.at.along(3 - 2 * self.at.hi), h)
        self.to_near(0, 1).start()
        self.to_near(1, 0).start()

    def sides_to_far(self):
        for h in range(2):
            self.side_arrived(self.xf, h)
            self.to_far(h).start()

    def far_to_near(self):
        for d, xi in ((0, self.xr), (1, self.xl)):
            landed(self.far.at[d], self.f_recv.at[d])
            self.add(self.own, xi, d, self.far.at[d])
            self.to_near(d, d).start()

    def arrive(self):
        for d, h in ((0, 1), (1, 0), (0, 0), (1, 1)):
            landed(self.near.at[d, h], self.n_recv.at[d, h])

    def total(self, h, some):
        return (
            self.own[self.at.x, h, some, :].astype(F32)
            + self.near[0, h, some, :].astype(F32)
            + self.near[1, h, some, :].astype(F32)
        )

    def forward(self):
        x = self.at.x
        for slot, into in ((1, self.part), (0, self.own)):
            for xi in self.pair(1):
                self.take(slot, xi)
            self.products(slot, 1, into)
            if slot == 1:
                for h in range(2):
                    self.to_side(self.xf, h).start()
        for xi in self.pair(0):
            self.take(1, xi)
        self.products(1, 0, self.part)
        self.pass_on(0).start()
        self.pass_on(1).start()
        for h in range(2):
            self.to_side(self.xf, h).wait_send()
            self.to_side((self.xl, self.xr)[h], h).start()
        self.sides_to_far()
        for xi in self.pair(0):
            self.take(0, xi)
        self.products(0, 0, self.own)
        self.add_passed()
        for h in range(2):
            self.to_side((self.xl, self.xr)[h], h).wait_send()
            self.to_side(x, h).start()
        self.sides_to_near()
        self.far_to_near()
        for h in range(2):
            self.side_arrived(x, h)
        self.arrive()

    def backward(self, sums):
        x = self.at.x

        def first(p):
            for xi in self.pair(p):
                self.take(1, xi)
            self.products(1, p, self.part)

            @pl.when(p == 0)
            def _():
                for d in range(2):
                    self.pass_on(d).start()
                    self.to_side((self.xl, self.xr)[d], d).start()

        loop(2, first)
        loop(4, lambda xi: self.take(0, xi))
        loop(2, sums.tile)

        def second(p):
            self.products(0, p, self.own)

            @pl.when(p == 0)
            def _():
                for h in range(2):
                    self.to_side((self.xl, self.xr)[h], h).wait_send()
                    self.to_side(self.xf, h).start()
                self.add_passed()
                self.sides_to_near()

            loop(2, lambda q: sums.tile(2 + 2 * p + q))

        loop(2, second)
        for h in range(2):
            self.to_side(self.xf, h).wait_send()
            self.to_side(x, h).start()
        self.sides_to_far()
        loop(2, lambda q: sums.tile(6 + q))
        sums.merge(7)
        self.far_to_near()
        sums.relay(1)
        for h in range(2):
            self.side_arrived(x, h)
        sums.turn()
        self.arrive()

    def end(self):
        for d in range(2):
            self.pass_on(d).wait_send()
            self.to_far(d).wait_send()
            for h in range(2):
                self.to_near(d, h).wait_send()
            self.to_side(self.at.x, d).wait_send()
        for i in range(4):
            other = (i < 2) == self.back
            landed(self.out.at[i, pl.ds(0, 14 if other else 15)], self.o_send.at[i])


def scatter_scratch(cols):
    return [
        pltpu.VMEM((4, 16, 16, cols), BF),
        pltpu.VMEM((4, 2, HALF, WIDTH), BF),
        pltpu.VMEM((4, 2, HALF, WIDTH), BF),
        pltpu.VMEM((4, 2, HALF, WIDTH), BF),
        pltpu.VMEM((2, HALF, WIDTH), BF),
        pltpu.VMEM((2, 2, HALF, WIDTH), BF),
        pltpu.VMEM((2, HALF, WIDTH), BF),
        pltpu.SemaphoreType.DMA((4,)),
        pltpu.SemaphoreType.DMA((2, 4)),
        pltpu.SemaphoreType.DMA((4, 2)),
        pltpu.SemaphoreType.DMA((4, 2)),
        pltpu.SemaphoreType.DMA((2,)),
        pltpu.SemaphoreType.DMA((2,)),
        pltpu.SemaphoreType.DMA((2, 2)),
        pltpu.SemaphoreType.DMA((2, 2)),
        pltpu.SemaphoreType.DMA((2,)),
        pltpu.SemaphoreType.DMA((2,)),
    ]


def each_rows(body):
    loop(4, lambda j: body(j))


def pieces(ref, j):
    first, second = (ref[f, pl.ds(pl.multiple_of(16 * j, 16), 16), :].astype(F32) for f in range(2))
    return [jnp.concatenate([first[i : i + 8], second[i : i + 8]]) for i in (0, 8)]


def place_of(j, n):
    inner = pl.ds(pl.multiple_of(lax.rem(j, 2) * 32 + 16 * n, 16), 16)
    return lax.div(j, 2), inner, pl.ds(pl.multiple_of(j * 32 + 16 * n, 16), 16)


def row_factor(states):
    return lax.rsqrt(jnp.mean(states * states, -1, keepdims=True) + 1e-06)


def front_kernel(
    hidden, teacher, scale, shift, gate, w_qkv, w_out,
    kept_modded, kept_up, qkv, factors, tokens, grad_att, diff, gate_rows,
    own, own_up, qkv_weight, out_weight, w_sem, *scratch,
):
    at = Place()
    qkv_copies = load_weight(w_qkv, qkv_weight, w_sem.at[0])
    out_copies = load_weight(w_out, out_weight, w_sem.at[1])
    at.greet(False)

    def modulate(j):
        for n, states in enumerate(pieces(hidden, j)):
            h, inner, _ = place_of(j, n)
            value = states * row_factor(states) * (1.0 + scale[...]) + shift[...]
            own[h, inner, :] = value.astype(BF)

    each_rows(modulate)
    at.met(False)
    ahead, middle, behind = scratch[:8], scratch[8:25], scratch[25:]
    mix = Scatter(at, qkv, ahead[6], None, out_weight, tokens, None, None, middle)
    end_ahead = gather_phase(
        at, own, qkv_weight, qkv_copies, kept_modded, qkv, factors, ahead,
        lambda: loop(2, mix.attend),
    )
    loop(2, lambda i: mix.attend(2 + i))
    for copy in out_copies:
        copy.wait()
    mix.forward()
    gate_rows[...] = jnp.zeros_like(gate_rows)

    def compare(j):
        for n, (states, target) in enumerate(zip(pieces(hidden, j), pieces(teacher, j))):
            h, inner, some = place_of(j, n)
            mixed = mix.total(h, inner)
            change = states + gate[...] * mixed - target
            diff[some, :] = change
            own_up[h, inner, :] = (gate[...] * change).astype(BF)
            both = change * mixed
            gate_rows[...] += both[:8] + both[8:]

    each_rows(compare)
    end_behind = gather_phase(at, own_up, out_weight, [], kept_up, grad_att, None, behind)
    end_ahead()
    mix.end()
    end_behind()
    loop(4, lambda t: landed(grad_att.at[t], behind[6].at[t]))


def front(hidden, teacher, scale, shift, gate, w_qkv, w_out):
    kept = jax.ShapeDtypeStruct((2, 4, 2, HALF, WIDTH), BF)
    return pl.pallas_call(
        front_kernel,
        out_shape=[
            kept,
            kept,
            jax.ShapeDtypeStruct((4, 16, 16, 3 * LOCAL), BF),
            jax.ShapeDtypeStruct((2, 4, 2 * HALF, HEAD_DIM), F32),
            jax.ShapeDtypeStruct((2, 4, 8, 16, LOCAL), BF),
            jax.ShapeDtypeStruct((4, 16, 16, LOCAL), BF),
            jax.ShapeDtypeStruct((2 * HALF, WIDTH), F32),
            jax.ShapeDtypeStruct((8, WIDTH), F32),
        ],
        in_specs=vmem(5) + anywhere(2),
        out_specs=anywhere(2) + vmem(6),
        scratch_shapes=[
            pltpu.VMEM((2, HALF, WIDTH), BF),
            pltpu.VMEM((2, HALF, WIDTH), BF),
            pltpu.VMEM((WIDTH, 3 * LOCAL), BF),
            pltpu.VMEM((LOCAL, WIDTH), BF),
            pltpu.SemaphoreType.DMA((2, 3)),
        ]
        + gather_scratch(3 * LOCAL)
        + scatter_scratch(LOCAL)
        + gather_scratch(LOCAL),
        compiler_params=pltpu.CompilerParams(
            collective_id=0, has_side_effects=True, vmem_limit_bytes=VMEM_BYTES
        ),
        cost_estimate=pl.CostEstimate(
            flops=2 * 1024 * WIDTH * 5 * LOCAL, bytes_accessed=50_000_000, transcendentals=0
        ),
        name="front",
    )(hidden, teacher, scale, shift, gate, w_qkv, w_out)


class Totals:
    def __init__(self, at, rows, result, scratch):
        self.at, self.rows, self.result = at, rows, result
        (
            self.by_head, self.by_frame, self.partial,
            self.s1, self.r1, self.s2, self.r2, self.s3, self.r3,
        ) = scratch
        self.started = []

    def piece(self, ref, i):
        return ref.at[:, pl.ds(pl.multiple_of(i * LOCAL, LOCAL), LOCAL)]

    def send(self, copies):
        for copy in copies:
            copy.start()
        self.started += copies

    def head(self, i):
        return (self.at.fr, lax.rem(self.at.fs + i, 8))

    def run(self, between, later):
        fr, fs = self.at.fr, self.at.fs
        self.send(
            [
                remote(
                    self.piece(self.rows, self.head(i)[1]), self.by_head.at[fs], self.s1.at[i],
                    self.r1, self.head(i),
                )
                for i in range(1, 8)
            ]
        )
        self.by_head[fs] = self.piece(self.rows, fs)[...]
        between()
        landed(self.by_head.at[pl.ds(0, 7)], self.r1)
        value = self.by_head[0]
        for i in range(1, 8):
            value = value + self.by_head[i]
        self.partial[...] = value
        self.by_frame[fr] = value
        self.send(
            [
                remote(
                    self.partial, self.by_frame.at[fr], self.s2.at[i], self.r2,
                    (lax.rem(fr + i, 16), fs),
                )
                for i in range(1, 16)
            ]
        )
        later()
        landed(self.by_frame.at[pl.ds(0, 15)], self.r2)
        value = self.by_frame[0]
        for i in range(1, 16):
            value = value + self.by_frame[i]
        here = self.piece(self.result, fs)
        here[...] = value
        self.send(
            [remote(here, here, self.s3.at[i], self.r3, self.head(i)) for i in range(1, 8)]
        )

    def end(self):
        landed(self.result.at[:, pl.ds(0, 7 * LOCAL)], self.r3)
        for copy in self.started:
            copy.wait_send()


def rear_kernel(
    hidden, diff, gate_rows, scale, qkv, grad, factors, attended, w_qkv, modded, up_all,
    grad_hidden, qkv_grad, out_grad, totals, weight, w_sem, tokens, dproj, scale_rows, shift_rows, rows,
    *scratch,
):
    at = Place()
    w_copies = load_weight(w_qkv, weight, w_sem)
    sums = WeightSums(at, modded, up_all, attended, dproj, (qkv_grad, out_grad), *scratch[17:33])
    sums.fetch(up_all, 0, 0)
    at.greet(True)
    at.met(True)
    back = Scatter(at, qkv, None, grad, weight, tokens, dproj, factors, scratch[:17])
    loop(4, back.attend)
    loop(8, sums.out_rows)
    for copy in w_copies:
        copy.wait()
    back.backward(sums)
    scale_rows[...] = jnp.zeros_like(scale_rows)
    shift_rows[...] = jnp.zeros_like(shift_rows)

    def add_up(j):
        for n, states in enumerate(pieces(hidden, j)):
            h, inner, _ = place_of(j, n)
            dmod = back.total(h, inner)
            both = dmod * (states * row_factor(states))
            scale_rows[...] += both[:8] + both[8:]
            shift_rows[...] += dmod[:8] + dmod[8:]

    def close(j):
        done = []
        for n, states in enumerate(pieces(hidden, j)):
            h, inner, some = place_of(j, n)
            factor = row_factor(states)
            normed = states * factor
            dnorm = back.total(h, inner) * (1.0 + scale[...])
            value = dnorm - normed * jnp.mean(dnorm * normed, -1, keepdims=True)
            done.append(diff[some, :] + factor * value)
        for f in range(2):
            both = jnp.concatenate([value[8 * f : 8 * f + 8] for value in done])
            grad_hidden[f, pl.ds(pl.multiple_of(16 * j, 16), 16), :] = both.astype(BF)

    each_rows(add_up)
    rows[...] = jnp.zeros_like(rows)
    for i, ref in enumerate((scale_rows, shift_rows, gate_rows)):
        rows[i : i + 1, :] = jnp.sum(ref[...], 0, keepdims=True)
    total = Totals(at, rows, totals, scratch[33:])
    total.run(lambda: each_rows(close), sums.finish)
    total.end()
    back.end()


def rear(hidden, diff, gate_rows, scale, qkv, grad, factors, attended, w_qkv, modded, up_all):
    cols = 3 * LOCAL
    return pl.pallas_call(
        rear_kernel,
        out_shape=[
            jax.ShapeDtypeStruct((2, HALF, WIDTH), BF),
            jax.ShapeDtypeStruct((3, 192, LOCAL), BF),
            jax.ShapeDtypeStruct((192, LOCAL), BF),
            jax.ShapeDtypeStruct((8, WIDTH), F32),
        ],
        in_specs=vmem(8) + anywhere(3),
        out_specs=vmem(4),
        scratch_shapes=[
            pltpu.VMEM((WIDTH, cols), BF),
            pltpu.SemaphoreType.DMA((3,)),
            pltpu.VMEM((2, 4, 8, 16, cols), BF),
            pltpu.VMEM((2, 4, 2 * HALF, cols), BF),
            pltpu.VMEM((8, WIDTH), F32),
            pltpu.VMEM((8, WIDTH), F32),
            pltpu.VMEM((8, WIDTH), F32),
        ]
        + scatter_scratch(cols)
        + [
            pltpu.VMEM((2, 1024, LOCAL), BF),
            pltpu.VMEM((LOCAL, 1024), BF),
            pltpu.VMEM((8, 2, 192, 4 * LOCAL), BF),
            pltpu.VMEM((8, 192, 4 * LOCAL), BF),
            pltpu.VMEM((2, 2, 96, 4 * LOCAL), BF),
            pltpu.VMEM((2, 2, 2, 96, 4 * LOCAL), BF),
            pltpu.VMEM((192, 4 * LOCAL), BF),
            pltpu.SemaphoreType.DMA((2,)),
            pltpu.SemaphoreType.DMA((8,)),
            pltpu.SemaphoreType.DMA((8,)),
            pltpu.SemaphoreType.DMA((2, 2)),
            pltpu.SemaphoreType.DMA((2, 2)),
            pltpu.SemaphoreType.DMA((2, 2, 2)),
            pltpu.SemaphoreType.DMA((2, 2, 2)),
            pltpu.SemaphoreType.DMA,
            pltpu.SemaphoreType.DMA,
        ]
        + [
            pltpu.VMEM((8, 8, LOCAL), F32),
            pltpu.VMEM((16, 8, LOCAL), F32),
            pltpu.VMEM((8, LOCAL), F32),
            pltpu.SemaphoreType.DMA((8,)),
            pltpu.SemaphoreType.DMA,
            pltpu.SemaphoreType.DMA((16,)),
            pltpu.SemaphoreType.DMA,
            pltpu.SemaphoreType.DMA((8,)),
            pltpu.SemaphoreType.DMA,
        ],
        compiler_params=pltpu.CompilerParams(
            collective_id=1, has_side_effects=True, vmem_limit_bytes=VMEM_BYTES
        ),
        cost_estimate=pl.CostEstimate(
            flops=2 * 1024 * WIDTH * 7 * LOCAL, bytes_accessed=50_000_000, transcendentals=0
        ),
        name="rear",
    )(hidden, diff, gate_rows, scale, qkv, grad, factors, attended, w_qkv, modded, up_all)


def hand_over_kernel(hidden, qkv, out, totals, to_hidden, to_qkv, to_out, *to_rows):
    to_hidden[...] = hidden[...]
    to_qkv[...] = qkv[...]
    to_out[...] = out[...].astype(F32).T.astype(BF)
    for i, ref in enumerate(to_rows):
        ref[...] = totals[i]


def hand_over(hidden, qkv, out, totals):
    row = jax.ShapeDtypeStruct((WIDTH,), F32)
    return pl.pallas_call(
        hand_over_kernel,
        out_shape=[
            jax.ShapeDtypeStruct(hidden.shape, BF),
            jax.ShapeDtypeStruct(qkv.shape, BF),
            jax.ShapeDtypeStruct(out.shape[::-1], BF),
            row,
            row,
            row,
        ],
        in_specs=vmem(4),
        out_specs=vmem(6),
        compiler_params=pltpu.CompilerParams(vmem_limit_bytes=VMEM_BYTES),
        name="hand_over",
    )(hidden, qkv, out, totals)


def shards(hidden_states, teacher, mod_scale, mod_shift, out_gate, w_qkv, w_out):
    scale = mod_scale.reshape(1, WIDTH)
    modded, up_all, qkv, factors, attended, grad_att, diff, gate_rows = front(
        hidden_states,
        teacher,
        scale,
        mod_shift.reshape(1, WIDTH),
        out_gate.reshape(1, WIDTH),
        w_qkv,
        w_out,
    )
    results = rear(
        hidden_states,
        diff,
        gate_rows,
        scale,
        qkv,
        grad_att,
        factors,
        attended.reshape(1024, LOCAL),
        w_qkv,
        modded.reshape(1024, WIDTH),
        up_all.reshape(1024, WIDTH),
    )
    return hand_over(*results)


def solution(mesh):
    in_specs = (
        P("frame", "fsdp", None),
        P("frame", "fsdp", None),
        P(),
        P(),
        P(),
        P(None, None, "fsdp"),
        P("fsdp", None),
    )
    out_specs = (
        P("frame", "fsdp", None),
        P(None, "frame", "fsdp"),
        P("fsdp", "frame"),
        P(),
        P(),
        P(),
    )
    return jax.shard_map(shards, mesh=mesh, in_specs=in_specs, out_specs=out_specs, check_vma=False)
```

```python
import functools
import jax
import jax.numpy as jnp
from jax import lax
from jax.experimental import pallas as pl
from jax.experimental.pallas import tpu as pltpu
from jax.sharding import PartitionSpec as P

HEAD_DIM = 128
HEADS = 3
LOCAL = 384
WIDTH = 3072
HALF = 64
TILE = 512
INV_ROOT = HEAD_DIM ** (-0.5)
MESH = pl.DeviceIdType.MESH
BF = jnp.bfloat16
F32 = jnp.float32
VMEM_BYTES = 60 * 1024 * 1024


class Place:
    def __init__(self):
        fr = lax.axis_index("frame")
        fs = lax.axis_index("fsdp")
        self.fr = fr
        self.fs = fs
        self.x = lax.div(fs, 2)
        self.lo = lax.rem(fs, 2)
        self.core = lax.rem(fr, 2)
        self.group = lax.div(fr, 2)
        other = fs + 1 - 2 * self.lo
        self.hi = lax.rem(self.group, 2)
        self.z = lax.div(self.group, 2)
        self.right = (fr, lax.rem(fs + 2, 8))
        self.left = (fr, lax.rem(fs + 6, 8))
        self.side = tuple((self.frame(self.z, h, self.core), other) for h in range(2))
        self.across = (fr + 2 - 4 * self.hi, other)
        self.beside = (fr, other)

    def frame(self, z, hi, core):
        return 4 * z + 2 * hi + core

    def along(self, off):
        return lax.rem(self.x + off, 4)

    def greet(self, heads):
        barrier = pltpu.get_barrier_semaphore()

        def signal(peer):
            pl.semaphore_signal(barrier, inc=1, device_id=peer, device_id_type=MESH)

        signal(self.across)
        if heads:
            for step in range(1, 8):
                signal((self.fr, lax.rem(self.fs + step, 8)))
        else:
            for peer in (self.right, self.left, self.beside):
                signal(peer)
        loop(15, lambda i: signal((lax.rem(self.fr + i + 1, 16), self.fs)))

    def met(self, heads):
        pl.semaphore_wait(pltpu.get_barrier_semaphore(), 23 if heads else 19)


def remote(src, dst, send_sem, recv_sem, device):
    return pltpu.make_async_remote_copy(
        src_ref=src,
        dst_ref=dst,
        send_sem=send_sem,
        recv_sem=recv_sem,
        device_id=device,
        device_id_type=MESH,
    )


def landed(ref, sem):
    pltpu.make_async_copy(ref, ref, sem).wait()


def loop(count, body):
    def step(i, carry):
        body(i)
        return carry

    lax.fori_loop(0, count, step, 0)


def others_first(p):
    return 2 + p - lax.div(3 * p * (p - 1), 2)


def load_weight(w_hbm, weight, sem):
    if len(w_hbm.shape) == 3:
        copies = [
            pltpu.make_async_copy(w_hbm.at[c], weight.at[:, pl.ds(c * LOCAL, LOCAL)], sem.at[c])
            for c in range(3)
        ]
    else:
        copies = [pltpu.make_async_copy(w_hbm, weight, sem.at[0])]
    for copy in copies:
        copy.start()
    return copies


def gather_phase(at, own, weight, w_copies, kept_all, sent_to, factors, scratch, between=None):
    full, out, x_send, y_send, recv, o_send, o_recv, keep_sem = scratch
    project = factors is not None

    def to_right(slot, src, xi, h, n):
        return remote(src, full.at[slot, xi, h], x_send.at[n], recv.at[slot, xi, h], at.right)

    def to_left(slot, src, xi, h, n):
        return remote(src, full.at[slot, xi, h], x_send.at[n], recv.at[slot, xi, h], at.left)

    def to_side(src, xi, h, n):
        return remote(
            src, full.at[1, xi, at.hi], y_send.at[n], recv.at[1, xi, at.hi], at.side[h]
        )

    xl, xr, xf = at.along(3), at.along(1), at.along(2)
    first = [
        to_right(0, own.at[0], at.x, 0, 0),
        to_left(0, own.at[1], at.x, 1, 1),
        to_side(own.at[0], at.x, 0, 0),
        to_side(own.at[1], at.x, 1, 1),
    ]
    for copy in first:
        copy.start()
    full[0, at.x] = own[...]
    second = [
        to_right(0, full.at[0, xl, 0], xl, 0, 2),
        to_left(0, full.at[0, xr, 1], xr, 1, 3),
    ]
    third = [
        to_right(0, own.at[1], at.x, 1, 4),
        to_side(full.at[0, xf, 0], xf, 0, 4),
        to_left(0, own.at[0], at.x, 0, 5),
        to_side(full.at[0, xf, 1], xf, 1, 5),
    ]
    fourth = [
        to_right(1, full.at[1, at.x, 1], at.x, 1, 6),
        to_left(1, full.at[1, at.x, 0], at.x, 0, 7),
    ]
    if project:
        fourth.append(to_right(1, full.at[1, at.x, 0], at.x, 0, 8))
        fourth.append(to_left(1, full.at[1, at.x, 1], at.x, 1, 9))
    early_sides = [to_side(full.at[0, (xl, xr)[h], h], (xl, xr)[h], h, 2) for h in range(2)]
    late_sides = [to_side(full.at[0, (xl, xr)[h], 1 - h], (xl, xr)[h], 1 - h, 3) for h in range(2)]
    for copy in w_copies:
        copy.wait()

    def arrived(slot, xi, h):
        landed(full.at[slot, xi, h], recv.at[slot, xi, h])

    def early(k):
        @pl.when(k == 1)
        def _():
            arrived(0, xl, 0)
            second[0].start()
            if not project:
                pl.when(at.hi == 0)(lambda: early_sides[0].start())
            arrived(0, xr, 1)
            second[1].start()
            if not project:
                pl.when(at.hi == 1)(lambda: early_sides[1].start())
            arrived(1, at.x, 0)
            arrived(1, at.x, 1)

        work(k, k, at.x)

    def late(i):
        slot = lax.div(i, 3)
        xi = at.along(others_first(lax.rem(i, 3)))

        @pl.when(i == 0)
        def _():
            arrived(0, xf, 0)
            third[0].start()
            third[1].start()
            arrived(0, xf, 1)
            third[2].start()
            third[3].start()

        @pl.when(i == 1)
        def _():
            arrived(0, xl, 1)
            for copy in fourth[0::2]:
                copy.start()
            if not project:
                pl.when(at.hi == 0)(lambda: late_sides[0].start())

        @pl.when(i == 2)
        def _():
            arrived(0, xr, 0)
            for copy in fourth[1::2]:
                copy.start()
            if not project:
                pl.when(at.hi == 1)(lambda: late_sides[1].start())

        if between is not None:
            pl.when(i == 4)(between)

        @pl.when(i >= 3)
        def _():
            arrived(1, xi, 0)
            arrived(1, xi, 1)

        work(i + 2, slot, xi)

    def work(k, slot, xi):
        pltpu.make_async_copy(full.at[slot, xi], kept_all.at[slot, xi], keep_sem).start()
        tokens = full[slot, xi].reshape(2 * HALF, WIDTH)
        if project:
            both = jnp.dot(tokens, weight[...], preferred_element_type=F32)
            lane = lax.broadcasted_iota(jnp.int32, (2 * HALF, HEAD_DIM), 1)
            kept = jnp.zeros((2 * HALF, HEAD_DIM), F32)
            for j in range(3 * HEADS):
                block = both[:, j * HEAD_DIM : (j + 1) * HEAD_DIM]
                if j < 2 * HEADS:
                    factor = lax.rsqrt(jnp.mean(block * block, -1, keepdims=True) + 1e-06)
                    kept = jnp.where(lane == j, factor, kept)
                    block = block * factor
                out[pl.ds(8 * k, 8), :, j * HEAD_DIM : (j + 1) * HEAD_DIM] = block.astype(BF).reshape(
                    8, 16, HEAD_DIM
                )
            factors[slot, xi] = kept
        else:
            both = lax.dot_general(
                tokens, weight[...], (((1,), (1,)), ((), ())), preferred_element_type=F32
            )
            out[pl.ds(8 * k, 8)] = both.astype(BF).reshape(8, 16, LOCAL)
        to_core = lax.rem(xi, 2)
        to_slot = 2 * lax.div(xi, 2) + lax.rem(at.lo + slot, 2)

        def give(b):
            z, upper = lax.rem(b, 4), lax.div(b, 4)
            target = at.frame(z, (1 - slot) * upper + slot * at.hi, to_core)
            origin = at.frame(at.z, (1 - slot) * at.hi + slot * upper, at.core)
            src = out.at[8 * k + b]
            dst = sent_to.at[to_slot, origin]

            @pl.when(target == at.fr)
            def _():
                pltpu.make_async_copy(src, dst, o_recv.at[to_slot]).start()

            @pl.when(target != at.fr)
            def _():
                remote(src, dst, o_send, o_recv.at[to_slot], (target, at.fs)).start()

        loop(8, give)

    loop(2, early)
    loop(6, late)

    def end():
        for copy in first + second + third + fourth:
            copy.wait_send()
        for h in range(0 if project else 2):

            @pl.when(at.hi == h)
            def _(h=h):
                early_sides[h].wait_send()
                late_sides[h].wait_send()

        landed(out.at[pl.ds(0, 58)], o_send)
        pltpu.make_async_copy(full, kept_all, keep_sem).wait()

    return end


def gather_scratch(cols):
    return [
        pltpu.VMEM((2, 4, 2, HALF, WIDTH), BF),
        pltpu.VMEM((64, 16, cols), BF),
        pltpu.SemaphoreType.DMA((10,)),
        pltpu.SemaphoreType.DMA((6,)),
        pltpu.SemaphoreType.DMA((2, 4, 2)),
        pltpu.SemaphoreType.DMA,
        pltpu.SemaphoreType.DMA((4,)),
        pltpu.SemaphoreType.DMA,
    ]


def vmem(count):
    return [pl.BlockSpec(memory_space=pltpu.VMEM)] * count


def anywhere(count):
    return [pl.BlockSpec(memory_space=pl.ANY)] * count


def same_patch():
    rows = lax.broadcasted_iota(jnp.int32, (256, 256), 0)
    cols = lax.broadcasted_iota(jnp.int32, (256, 256), 1)
    return lax.rem(rows, 8) == lax.rem(cols, 8)


def dot_nt(a, b):
    return lax.dot_general(a, b, (((1,), (1,)), ((), ())), preferred_element_type=F32)


def dot_tn(a, b):
    return lax.dot_general(a, b, (((0,), (0,)), ((), ())), preferred_element_type=F32)


def softmax(query, key):
    scores = dot_nt(query, key) * INV_ROOT
    expo = jnp.where(same_patch(), jnp.exp(scores), 0.0)
    return expo / jnp.sum(expo, -1, keepdims=True)


class WeightSums:
    def __init__(self, at, flat, up_all, attended, dproj, result, *scratch):
        self.at = at
        self.flat, self.up_all, self.attended, self.dproj = flat, up_all, attended, dproj
        self.result = result
        (
            self.rows, self.turned, self.part, self.twin, self.far, self.near, self.last,
            self.row_sem, self.t_send, self.t_recv, self.f_send, self.f_recv,
            self.n_send, self.n_recv, self.l_send, self.l_recv,
        ) = scratch
        fr, fs = at.fr, at.fs
        self.hi = lax.rem(at.group, 2)
        self.z = lax.div(at.group, 2)
        self.sibling = (fr + 1 - 2 * at.core, fs)
        self.over = (fr + 2 - 4 * self.hi, fs)
        self.up = (lax.rem(fr + 4, 16), fs)
        self.down = (lax.rem(fr + 12, 16), fs)

    def group(self, off, hi):
        return 2 * lax.rem(self.z + off, 4) + hi

    def flagged(self, flag):
        return flag * self.hi + (1 - flag) * (1 - self.hi)

    def target(self, m):
        q, b = lax.div(m, 2), lax.rem(m, 2)
        inner = lax.div(q * (3 - q), 2)
        base = 2 - q + lax.div(q * (q - 1), 2) - lax.div(q * (q - 1) * (q - 2), 3)
        flag = (1 - inner) * b + inner * (q - 1)
        return self.group(base + 2 * inner * b, self.flagged(flag))

    def load(self, source, j, slot):
        cols = pl.ds(pl.multiple_of(j * LOCAL, LOCAL), LOCAL)
        return pltpu.make_async_copy(
            source.at[:, cols], self.rows.at[slot], self.row_sem.at[slot]
        )

    def fetch(self, source, j, slot):
        self.load(source, j, slot).start()

    def out_rows(self, m):
        slot = lax.rem(m, 2)
        self.load(self.up_all, m, slot).wait()

        @pl.when(m < 7)
        def _():
            self.fetch(self.up_all, m + 1, 1 - slot)

        @pl.when(m == 7)
        def _():
            self.fetch(self.flat, self.target(0), 0)

        self.turned[...] = jnp.transpose(self.rows[slot])
        value = jnp.dot(self.turned[...], self.attended[...], preferred_element_type=F32)
        self.part[m, :, :, 3 * LOCAL :] = value.astype(BF).reshape(2, 192, LOCAL)

    def to_twin(self, j):
        return remote(
            self.part.at[j, 1 - self.at.core],
            self.twin.at[j],
            self.t_send.at[j],
            self.t_recv.at[j],
            self.sibling,
        )

    def rows_of(self, off, flag, half):
        j = self.group(off, self.flagged(flag))
        return self.part.at[j, self.at.core, pl.ds(half * 96, 96)]

    def to_far(self, d, flag):
        return remote(
            self.rows_of(2, flag, d), self.far.at[d, flag], self.f_send.at[d, flag],
            self.f_recv.at[d, flag], (self.up, self.down)[d],
        )

    def to_near(self, d, flag, half):
        return remote(
            self.rows_of((1, 3)[d], flag, half), self.near.at[d, flag, half],
            self.n_send.at[d, flag, half], self.n_recv.at[d, flag, half],
            (self.up, self.down)[d],
        )

    def tile(self, m):
        j = self.target(m)
        slot = lax.rem(m, 2)
        self.load(self.flat, j, slot).wait()

        @pl.when(m < 7)
        def _():
            self.fetch(self.flat, self.target(m + 1), 1 - slot)

        self.turned[...] = jnp.transpose(self.rows[slot])
        for c in range(3):
            cols = slice(c * LOCAL, (c + 1) * LOCAL)
            other = self.dproj[:, :, :, cols].reshape(1024, LOCAL)
            value = jnp.dot(self.turned[...], other, preferred_element_type=F32)
            self.part[j, :, :, cols] = value.astype(BF).reshape(2, 192, LOCAL)
        self.to_twin(j).start()

        @pl.when(m > 0)
        def _():
            self.merge(m - 1)

    def add(self, held, other, count):
        def rows(i):
            some = pl.ds(pl.multiple_of(i * 48, 16), 48)
            held[some, :] = (held[some, :].astype(F32) + other[some, :].astype(F32)).astype(BF)

        loop(count, rows)

    def merge(self, m):
        j = self.target(m)
        landed(self.twin.at[j], self.t_recv.at[j])
        self.add(self.part.at[j, self.at.core], self.twin.at[j], 4)
        for flag in range(2):

            @pl.when(m == flag)
            def _(flag=flag):
                for d in range(2):
                    self.to_far(d, flag).start()

            @pl.when(m == 2 + 2 * flag)
            def _(flag=flag):
                if flag == 1:
                    self.relay(0)
                self.to_near(0, flag, 1).start()

            @pl.when(m == 3 + 2 * flag)
            def _(flag=flag):
                self.to_near(1, flag, 0).start()

    def relay(self, flag):
        for d in range(2):
            landed(self.far.at[d, flag], self.f_recv.at[d, flag])
            self.add(self.rows_of((1, 3)[d], flag, d), self.far.at[d, flag], 2)
            self.to_near(d, flag, d).start()

    def arrived(self, flag):
        for d in range(2):
            for half in range(2):
                landed(self.near.at[d, flag, half], self.n_recv.at[d, flag, half])

    def both(self, flag, half, some):
        value = self.rows_of(0, flag, half)[some, :].astype(F32)
        for d in range(2):
            value = value + self.near[d, flag, half, some, :].astype(F32)
        return value

    def to_last(self):
        source = self.part.at[self.group(0, self.flagged(0)), self.at.core]
        return remote(source, self.last, self.l_send, self.l_recv, self.over)

    def turn(self):
        self.arrived(0)
        for half in range(2):
            held = self.rows_of(0, 0, half)

            def rows(i, half=half, held=held):
                some = pl.ds(pl.multiple_of(i * 48, 16), 48)
                held[some, :] = self.both(0, half, some).astype(BF)

            loop(2, rows)
        self.to_last().start()

    def finish(self):
        self.arrived(1)
        landed(self.last, self.l_recv)
        for half in range(2):

            def end(i, half=half):
                some = pl.ds(pl.multiple_of(i * 48, 16), 48)
                there = pl.ds(pl.multiple_of(half * 96 + i * 48, 16), 48)
                value = self.both(1, half, some) + self.last[there, :].astype(F32)
                value = value.astype(BF)
                for c in range(3):
                    self.result[0][c, there, :] = value[:, c * LOCAL : (c + 1) * LOCAL]
                self.result[1][there, :] = value[:, 3 * LOCAL :]

            loop(2, end)
        for d in range(2):
            for flag in range(2):
                self.to_far(d, flag).wait_send()
                for half in range(2):
                    self.to_near(d, flag, half).wait_send()
        self.to_last().wait_send()
        loop(8, lambda j: self.to_twin(j).wait_send())


def tile_loop(body):
    loop(WIDTH // TILE, lambda j: body(pl.ds(pl.multiple_of(j * TILE, TILE), TILE)))


class Scatter:
    def __init__(self, at, qkv, qkv_sem, grad, weight, tokens, dproj, factors, scratch):
        self.at, self.qkv, self.qkv_sem, self.grad = at, qkv, qkv_sem, grad
        self.weight, self.tokens, self.dproj, self.factors = weight, tokens, dproj, factors
        (
            self.out, self.part, self.own, self.from_side, self.far, self.near, self.passed,
            self.o_send, self.o_recv, self.y_send, self.y_recv, self.f_send, self.f_recv,
            self.n_send, self.n_recv, self.p_send, self.p_recv,
        ) = scratch
        self.back = grad is not None
        self.xl, self.xr, self.xf = at.along(3), at.along(1), at.along(2)

    def put(self, i, block, value):
        cols = slice(block * HEAD_DIM, (block + 1) * HEAD_DIM)
        self.out[i, :, :, cols] = value.astype(BF).reshape(16, 16, HEAD_DIM)

    def attend(self, i):
        at, put = self.at, self.put
        slot = lax.div(i, 2)
        if self.back:
            slot = 1 - slot
        xh = lax.rem(lax.div(at.x, 2) + i, 2)
        t = 2 * xh + lax.rem(at.lo + slot, 2)
        if self.qkv_sem is not None:
            landed(self.qkv.at[t], self.qkv_sem.at[t])

        def columns(ref, block):
            return ref[t, :, :, block * HEAD_DIM : (block + 1) * HEAD_DIM].reshape(256, HEAD_DIM)

        for h in range(HEADS):
            query, key, value = (columns(self.qkv, c * HEADS + h) for c in range(3))
            probs = softmax(query, key)
            low = probs.astype(BF)
            if not self.back:
                put(i, h, jnp.dot(low, value, preferred_element_type=F32))
                continue
            grad_in = columns(self.grad, h)
            dprob = dot_nt(grad_in, value)
            put(i, 2 * HEADS + h, dot_tn(low, grad_in))
            dscore = (probs * (dprob - jnp.sum(probs * dprob, -1, keepdims=True))).astype(BF)
            for c, normed, product in (
                (0, query, jnp.dot(dscore, key, preferred_element_type=F32)),
                (1, key, dot_tn(dscore, query)),
            ):
                step_in = (product * INV_ROOT).astype(BF).astype(F32)
                wide = normed.astype(F32)
                put(
                    i,
                    c * HEADS + h,
                    step_in - wide * jnp.mean(step_in * wide, -1, keepdims=True),
                )
        xi = 2 * xh + at.core

        def give(f):
            upper = lax.rem(lax.div(f, 2), 2)
            target = f + 2 * slot * (at.hi - upper)
            piece = 4 * ((1 - slot) * at.hi + slot * upper) + at.z
            src = self.out.at[i, f]
            dst = self.tokens.at[slot, xi, piece]

            @pl.when(target == at.fr)
            def _():
                pltpu.make_async_copy(src, dst, self.o_recv.at[slot, xi]).start()

            @pl.when(target != at.fr)
            def _():
                remote(
                    src, dst, self.o_send.at[i], self.o_recv.at[slot, xi], (target, at.fs)
                ).start()

        loop(16, give)

    def take(self, slot, xi):
        landed(self.tokens.at[slot, xi], self.o_recv.at[slot, xi])
        if self.back:
            for j in range(3 * HEADS):
                cols = slice(j * HEAD_DIM, (j + 1) * HEAD_DIM)
                block = self.tokens[slot, xi, :, :, cols].reshape(2 * HALF, HEAD_DIM)
                if j < 2 * HEADS:
                    block = (block.astype(F32) * self.factors[slot, xi, :, j : j + 1]).astype(BF)
                self.dproj[slot, xi, :, cols] = block

    def pair(self, p):
        return self.at.along(1 + p), self.at.along(3 - 3 * p)

    def products(self, slot, p, into):
        pair = self.pair(p)
        source = self.dproj if self.back else self.tokens
        rows = jnp.concatenate([source[slot, xi].reshape(2 * HALF, -1) for xi in pair])

        def tiles(tile):
            if self.back:
                value = dot_nt(rows, self.weight[tile, :])
            else:
                value = jnp.dot(rows, self.weight[:, tile], preferred_element_type=F32)
            value = value.astype(BF)
            for n, xi in enumerate(pair):
                some = value[n * 2 * HALF : (n + 1) * 2 * HALF]
                into[xi, :, :, tile] = some.reshape(2, HALF, TILE)

        tile_loop(tiles)

    def add(self, into, xi, h, other):
        def tiles(tile):
            value = into[xi, h, :, tile].astype(F32) + other[:, tile].astype(F32)
            into[xi, h, :, tile] = value.astype(BF)

        tile_loop(tiles)

    def to_side(self, xi, h):
        return remote(
            self.part.at[xi, h], self.from_side.at[xi, self.at.hi], self.y_send.at[xi, h],
            self.y_recv.at[xi, self.at.hi], self.at.side[h],
        )

    def side_arrived(self, xi, h):
        landed(self.from_side.at[xi, h], self.y_recv.at[xi, h])
        self.add(self.own, xi, h, self.from_side.at[xi, h])

    def way(self, d):
        return (self.at.right, self.at.left)[d]

    def pass_on(self, d):
        source = self.part.at[(self.xr, self.xl)[d], d]
        return remote(source, self.passed.at[d], self.p_send.at[d], self.p_recv.at[d], self.way(d))

    def to_far(self, d):
        source = self.own.at[self.xf, d]
        return remote(source, self.far.at[d], self.f_send.at[d], self.f_recv.at[d], self.way(d))

    def to_near(self, d, h):
        source = self.own.at[(self.xr, self.xl)[d], h]
        return remote(
            source, self.near.at[d, h], self.n_send.at[d, h], self.n_recv.at[d, h], self.way(d)
        )

    def add_passed(self):
        for h in range(2):
            landed(self.passed.at[h], self.p_recv.at[h])
            self.add(self.part, self.at.x, h, self.passed.at[h])

    def sides_to_near(self):
        for h in range(2):
            self.side_arrived(self.at.along(3 - 2 * self.at.hi), h)
        self.to_near(0, 1).start()
        self.to_near(1, 0).start()

    def sides_to_far(self):
        for h in range(2):
            self.side_arrived(self.xf, h)
            self.to_far(h).start()

    def far_to_near(self):
        for d, xi in ((0, self.xr), (1, self.xl)):
            landed(self.far.at[d], self.f_recv.at[d])
            self.add(self.own, xi, d, self.far.at[d])
            self.to_near(d, d).start()

    def arrive(self):
        for d, h in ((0, 1), (1, 0), (0, 0), (1, 1)):
            landed(self.near.at[d, h], self.n_recv.at[d, h])

    def total(self, h, some):
        return (
            self.own[self.at.x, h, some, :].astype(F32)
            + self.near[0, h, some, :].astype(F32)
            + self.near[1, h, some, :].astype(F32)
        )

    def forward(self):
        x = self.at.x
        for slot, into in ((1, self.part), (0, self.own)):
            for xi in self.pair(1):
                self.take(slot, xi)
            self.products(slot, 1, into)
            if slot == 1:
                for h in range(2):
                    self.to_side(self.xf, h).start()
        for xi in self.pair(0):
            self.take(1, xi)
        self.products(1, 0, self.part)
        self.pass_on(0).start()
        self.pass_on(1).start()
        for h in range(2):
            self.to_side(self.xf, h).wait_send()
            self.to_side((self.xl, self.xr)[h], h).start()
        self.sides_to_far()
        for xi in self.pair(0):
            self.take(0, xi)
        self.products(0, 0, self.own)
        self.add_passed()
        for h in range(2):
            self.to_side((self.xl, self.xr)[h], h).wait_send()
            self.to_side(x, h).start()
        self.sides_to_near()
        self.far_to_near()
        for h in range(2):
            self.side_arrived(x, h)
        self.arrive()

    def backward(self, sums):
        x = self.at.x

        def first(p):
            for xi in self.pair(p):
                self.take(1, xi)
            self.products(1, p, self.part)

            @pl.when(p == 0)
            def _():
                for d in range(2):
                    self.pass_on(d).start()
                    self.to_side((self.xl, self.xr)[d], d).start()

        loop(2, first)
        loop(4, lambda xi: self.take(0, xi))
        loop(2, sums.tile)

        def second(p):
            self.products(0, p, self.own)

            @pl.when(p == 0)
            def _():
                for h in range(2):
                    self.to_side((self.xl, self.xr)[h], h).wait_send()
                    self.to_side(self.xf, h).start()
                self.add_passed()
                self.sides_to_near()

            loop(2, lambda q: sums.tile(2 + 2 * p + q))

        loop(2, second)
        for h in range(2):
            self.to_side(self.xf, h).wait_send()
            self.to_side(x, h).start()
        self.sides_to_far()
        loop(2, lambda q: sums.tile(6 + q))
        sums.merge(7)
        self.far_to_near()
        sums.relay(1)
        for h in range(2):
            self.side_arrived(x, h)
        sums.turn()
        self.arrive()

    def end(self):
        for d in range(2):
            self.pass_on(d).wait_send()
            self.to_far(d).wait_send()
            for h in range(2):
                self.to_near(d, h).wait_send()
            self.to_side(self.at.x, d).wait_send()
        for i in range(4):
            other = (i < 2) == self.back
            landed(self.out.at[i, pl.ds(0, 14 if other else 15)], self.o_send.at[i])


def scatter_scratch(cols):
    return [
        pltpu.VMEM((4, 16, 16, cols), BF),
        pltpu.VMEM((4, 2, HALF, WIDTH), BF),
        pltpu.VMEM((4, 2, HALF, WIDTH), BF),
        pltpu.VMEM((4, 2, HALF, WIDTH), BF),
        pltpu.VMEM((2, HALF, WIDTH), BF),
        pltpu.VMEM((2, 2, HALF, WIDTH), BF),
        pltpu.VMEM((2, HALF, WIDTH), BF),
        pltpu.SemaphoreType.DMA((4,)),
        pltpu.SemaphoreType.DMA((2, 4)),
        pltpu.SemaphoreType.DMA((4, 2)),
        pltpu.SemaphoreType.DMA((4, 2)),
        pltpu.SemaphoreType.DMA((2,)),
        pltpu.SemaphoreType.DMA((2,)),
        pltpu.SemaphoreType.DMA((2, 2)),
        pltpu.SemaphoreType.DMA((2, 2)),
        pltpu.SemaphoreType.DMA((2,)),
        pltpu.SemaphoreType.DMA((2,)),
    ]


def each_rows(body):
    loop(4, lambda j: body(j))


def pieces(ref, j):
    first, second = (ref[f, pl.ds(pl.multiple_of(16 * j, 16), 16), :].astype(F32) for f in range(2))
    return [jnp.concatenate([first[i : i + 8], second[i : i + 8]]) for i in (0, 8)]


def place_of(j, n):
    inner = pl.ds(pl.multiple_of(lax.rem(j, 2) * 32 + 16 * n, 16), 16)
    return lax.div(j, 2), inner, pl.ds(pl.multiple_of(j * 32 + 16 * n, 16), 16)


def row_factor(states):
    return lax.rsqrt(jnp.mean(states * states, -1, keepdims=True) + 1e-06)


def front_kernel(
    hidden, teacher, scale, shift, gate, w_qkv, w_out,
    kept_modded, kept_up, qkv_hbm, factors_hbm, tokens_hbm, diff_hbm, grad_att, gate_rows,
    qkv, factors, tokens, diff, out_sem, own, own_up, qkv_weight, out_weight, w_sem, *scratch,
):
    at = Place()
    qkv_copies = load_weight(w_qkv, qkv_weight, w_sem.at[0])
    out_copies = load_weight(w_out, out_weight, w_sem.at[1])
    at.greet(False)

    def modulate(j):
        for n, states in enumerate(pieces(hidden, j)):
            h, inner, _ = place_of(j, n)
            value = states * row_factor(states) * (1.0 + scale[...]) + shift[...]
            own[h, inner, :] = value.astype(BF)

    each_rows(modulate)
    at.met(False)
    ahead, middle, behind = scratch[:8], scratch[8:25], scratch[25:]
    mix = Scatter(at, qkv, ahead[6], None, out_weight, tokens, None, None, middle)
    end_ahead = gather_phase(
        at, own, qkv_weight, qkv_copies, kept_modded, qkv, factors, ahead,
        lambda: loop(2, mix.attend),
    )
    loop(2, lambda i: mix.attend(2 + i))
    for copy in out_copies:
        copy.wait()
    mix.forward()
    gate_rows[...] = jnp.zeros_like(gate_rows)

    def compare(j):
        for n, (states, target) in enumerate(zip(pieces(hidden, j), pieces(teacher, j))):
            h, inner, some = place_of(j, n)
            mixed = mix.total(h, inner)
            change = states + gate[...] * mixed - target
            diff[some, :] = change
            own_up[h, inner, :] = (gate[...] * change).astype(BF)
            both = change * mixed
            gate_rows[...] += both[:8] + both[8:]

    each_rows(compare)
    leaving = [
        pltpu.make_async_copy(here, there, out_sem.at[i])
        for i, (here, there) in enumerate(
            ((qkv, qkv_hbm), (factors, factors_hbm), (tokens, tokens_hbm), (diff, diff_hbm))
        )
    ]
    for copy in leaving:
        copy.start()
    end_behind = gather_phase(at, own_up, out_weight, [], kept_up, grad_att, None, behind)
    for copy in leaving:
        copy.wait()
    end_ahead()
    mix.end()
    end_behind()
    loop(4, lambda t: landed(grad_att.at[t], behind[6].at[t]))


def front(hidden, teacher, scale, shift, gate, w_qkv, w_out):
    kept = jax.ShapeDtypeStruct((2, 4, 2, HALF, WIDTH), BF)
    return pl.pallas_call(
        front_kernel,
        out_shape=[
            kept,
            kept,
            jax.ShapeDtypeStruct((4, 16, 16, 3 * LOCAL), BF),
            jax.ShapeDtypeStruct((2, 4, 2 * HALF, HEAD_DIM), F32),
            jax.ShapeDtypeStruct((2, 4, 8, 16, LOCAL), BF),
            jax.ShapeDtypeStruct((2 * HALF, WIDTH), F32),
            jax.ShapeDtypeStruct((4, 16, 16, LOCAL), BF),
            jax.ShapeDtypeStruct((8, WIDTH), F32),
        ],
        in_specs=vmem(5) + anywhere(2),
        out_specs=anywhere(6) + vmem(2),
        scratch_shapes=[
            pltpu.VMEM((4, 16, 16, 3 * LOCAL), BF),
            pltpu.VMEM((2, 4, 2 * HALF, HEAD_DIM), F32),
            pltpu.VMEM((2, 4, 8, 16, LOCAL), BF),
            pltpu.VMEM((2 * HALF, WIDTH), F32),
            pltpu.SemaphoreType.DMA((4,)),
            pltpu.VMEM((2, HALF, WIDTH), BF),
            pltpu.VMEM((2, HALF, WIDTH), BF),
            pltpu.VMEM((WIDTH, 3 * LOCAL), BF),
            pltpu.VMEM((LOCAL, WIDTH), BF),
            pltpu.SemaphoreType.DMA((2, 3)),
        ]
        + gather_scratch(3 * LOCAL)
        + scatter_scratch(LOCAL)
        + gather_scratch(LOCAL),
        compiler_params=pltpu.CompilerParams(
            collective_id=0, has_side_effects=True, vmem_limit_bytes=VMEM_BYTES
        ),
        cost_estimate=pl.CostEstimate(
            flops=2 * 1024 * WIDTH * 5 * LOCAL, bytes_accessed=50_000_000, transcendentals=0
        ),
        name="front",
    )(hidden, teacher, scale, shift, gate, w_qkv, w_out)


class Totals:
    def __init__(self, at, rows, result, scratch):
        self.at, self.rows, self.result = at, rows, result
        (
            self.by_head, self.by_frame, self.partial,
            self.s1, self.r1, self.s2, self.r2, self.s3, self.r3,
        ) = scratch
        self.started = []

    def piece(self, ref, i):
        return ref.at[:, pl.ds(pl.multiple_of(i * LOCAL, LOCAL), LOCAL)]

    def send(self, copies):
        for copy in copies:
            copy.start()
        self.started += copies

    def head(self, i):
        return (self.at.fr, lax.rem(self.at.fs + i, 8))

    def run(self, between, later):
        fr, fs = self.at.fr, self.at.fs
        self.send(
            [
                remote(
                    self.piece(self.rows, self.head(i)[1]), self.by_head.at[fs], self.s1.at[i],
                    self.r1, self.head(i),
                )
                for i in range(1, 8)
            ]
        )
        self.by_head[fs] = self.piece(self.rows, fs)[...]
        between()
        landed(self.by_head.at[pl.ds(0, 7)], self.r1)
        value = self.by_head[0]
        for i in range(1, 8):
            value = value + self.by_head[i]
        self.partial[...] = value
        self.by_frame[fr] = value
        self.send(
            [
                remote(
                    self.partial, self.by_frame.at[fr], self.s2.at[i], self.r2,
                    (lax.rem(fr + i, 16), fs),
                )
                for i in range(1, 16)
            ]
        )
        later()
        landed(self.by_frame.at[pl.ds(0, 15)], self.r2)
        value = self.by_frame[0]
        for i in range(1, 16):
            value = value + self.by_frame[i]
        here = self.piece(self.result, fs)
        here[...] = value
        self.send(
            [remote(here, here, self.s3.at[i], self.r3, self.head(i)) for i in range(1, 8)]
        )

    def end(self):
        landed(self.result.at[:, pl.ds(0, 7 * LOCAL)], self.r3)
        for copy in self.started:
            copy.wait_send()


def rear_kernel(
    gate_rows, scale, qkv, grad, hidden_hbm, diff_hbm, factors_hbm, attended_hbm, w_qkv, modded,
    up_all, grad_hidden, qkv_grad, out_grad, totals, hidden, diff, factors, attended, in_sem, weight,
    w_sem, tokens, dproj, scale_rows, shift_rows, rows,
    *scratch,
):
    at = Place()
    late = [
        pltpu.make_async_copy(source, here, in_sem.at[i])
        for i, (source, here) in enumerate(
            (
                (attended_hbm, attended),
                (factors_hbm, factors),
                (hidden_hbm, hidden),
                (diff_hbm, diff),
            )
        )
    ]
    w_copies = load_weight(w_qkv, weight, w_sem)
    for copy in late:
        copy.start()
    sums = WeightSums(at, modded, up_all, attended, dproj, (qkv_grad, out_grad), *scratch[17:33])
    sums.fetch(up_all, 0, 0)
    at.greet(True)
    at.met(True)
    back = Scatter(at, qkv, None, grad, weight, tokens, dproj, factors, scratch[:17])
    loop(4, back.attend)
    for copy in late:
        copy.wait()
    loop(8, sums.out_rows)
    for copy in w_copies:
        copy.wait()
    back.backward(sums)
    scale_rows[...] = jnp.zeros_like(scale_rows)
    shift_rows[...] = jnp.zeros_like(shift_rows)

    def add_up(j):
        for n, states in enumerate(pieces(hidden, j)):
            h, inner, _ = place_of(j, n)
            dmod = back.total(h, inner)
            both = dmod * (states * row_factor(states))
            scale_rows[...] += both[:8] + both[8:]
            shift_rows[...] += dmod[:8] + dmod[8:]

    def close(j):
        done = []
        for n, states in enumerate(pieces(hidden, j)):
            h, inner, some = place_of(j, n)
            factor = row_factor(states)
            normed = states * factor
            dnorm = back.total(h, inner) * (1.0 + scale[...])
            value = dnorm - normed * jnp.mean(dnorm * normed, -1, keepdims=True)
            done.append(diff[some, :] + factor * value)
        for f in range(2):
            both = jnp.concatenate([value[8 * f : 8 * f + 8] for value in done])
            grad_hidden[f, pl.ds(pl.multiple_of(16 * j, 16), 16), :] = both.astype(BF)

    each_rows(add_up)
    rows[...] = jnp.zeros_like(rows)
    for i, ref in enumerate((scale_rows, shift_rows, gate_rows)):
        rows[i : i + 1, :] = jnp.sum(ref[...], 0, keepdims=True)
    total = Totals(at, rows, totals, scratch[33:])
    total.run(lambda: each_rows(close), sums.finish)
    total.end()
    back.end()


def rear(hidden, diff, gate_rows, scale, qkv, grad, factors, attended, w_qkv, modded, up_all):
    cols = 3 * LOCAL
    return pl.pallas_call(
        rear_kernel,
        out_shape=[
            jax.ShapeDtypeStruct((2, HALF, WIDTH), BF),
            jax.ShapeDtypeStruct((3, 192, LOCAL), BF),
            jax.ShapeDtypeStruct((192, LOCAL), BF),
            jax.ShapeDtypeStruct((8, WIDTH), F32),
        ],
        in_specs=vmem(4) + anywhere(7),
        out_specs=vmem(4),
        scratch_shapes=[
            pltpu.VMEM((2, HALF, WIDTH), BF),
            pltpu.VMEM((2 * HALF, WIDTH), F32),
            pltpu.VMEM((2, 4, 2 * HALF, HEAD_DIM), F32),
            pltpu.VMEM((1024, LOCAL), BF),
            pltpu.SemaphoreType.DMA((4,)),
            pltpu.VMEM((WIDTH, cols), BF),
            pltpu.SemaphoreType.DMA((3,)),
            pltpu.VMEM((2, 4, 8, 16, cols), BF),
            pltpu.VMEM((2, 4, 2 * HALF, cols), BF),
            pltpu.VMEM((8, WIDTH), F32),
            pltpu.VMEM((8, WIDTH), F32),
            pltpu.VMEM((8, WIDTH), F32),
        ]
        + scatter_scratch(cols)
        + [
            pltpu.VMEM((2, 1024, LOCAL), BF),
            pltpu.VMEM((LOCAL, 1024), BF),
            pltpu.VMEM((8, 2, 192, 4 * LOCAL), BF),
            pltpu.VMEM((8, 192, 4 * LOCAL), BF),
            pltpu.VMEM((2, 2, 96, 4 * LOCAL), BF),
            pltpu.VMEM((2, 2, 2, 96, 4 * LOCAL), BF),
            pltpu.VMEM((192, 4 * LOCAL), BF),
            pltpu.SemaphoreType.DMA((2,)),
            pltpu.SemaphoreType.DMA((8,)),
            pltpu.SemaphoreType.DMA((8,)),
            pltpu.SemaphoreType.DMA((2, 2)),
            pltpu.SemaphoreType.DMA((2, 2)),
            pltpu.SemaphoreType.DMA((2, 2, 2)),
            pltpu.SemaphoreType.DMA((2, 2, 2)),
            pltpu.SemaphoreType.DMA,
            pltpu.SemaphoreType.DMA,
        ]
        + [
            pltpu.VMEM((8, 8, LOCAL), F32),
            pltpu.VMEM((16, 8, LOCAL), F32),
            pltpu.VMEM((8, LOCAL), F32),
            pltpu.SemaphoreType.DMA((8,)),
            pltpu.SemaphoreType.DMA,
            pltpu.SemaphoreType.DMA((16,)),
            pltpu.SemaphoreType.DMA,
            pltpu.SemaphoreType.DMA((8,)),
            pltpu.SemaphoreType.DMA,
        ],
        compiler_params=pltpu.CompilerParams(
            collective_id=1, has_side_effects=True, vmem_limit_bytes=VMEM_BYTES
        ),
        cost_estimate=pl.CostEstimate(
            flops=2 * 1024 * WIDTH * 7 * LOCAL, bytes_accessed=50_000_000, transcendentals=0
        ),
        name="rear",
    )(gate_rows, scale, qkv, grad, hidden, diff, factors, attended, w_qkv, modded, up_all)


def hand_over_kernel(hidden, qkv, out, totals, to_hidden, to_qkv, to_out, *to_rows):
    to_hidden[...] = hidden[...]
    to_qkv[...] = qkv[...]
    to_out[...] = out[...]
    for i, ref in enumerate(to_rows):
        ref[...] = totals[i]


def hand_over(hidden, qkv, out, totals):
    row = jax.ShapeDtypeStruct((WIDTH,), F32)
    return pl.pallas_call(
        hand_over_kernel,
        out_shape=[
            jax.ShapeDtypeStruct(hidden.shape, BF),
            jax.ShapeDtypeStruct(qkv.shape, BF),
            jax.ShapeDtypeStruct(out.shape, BF),
            row,
            row,
            row,
        ],
        in_specs=vmem(4),
        out_specs=vmem(6),
        compiler_params=pltpu.CompilerParams(vmem_limit_bytes=VMEM_BYTES),
        name="hand_over",
    )(hidden, qkv, out, totals)


def shards(hidden_states, teacher, mod_scale, mod_shift, out_gate, w_qkv, w_out):
    scale = mod_scale.reshape(1, WIDTH)
    modded, up_all, qkv, factors, attended, diff, grad_att, gate_rows = front(
        hidden_states,
        teacher,
        scale,
        mod_shift.reshape(1, WIDTH),
        out_gate.reshape(1, WIDTH),
        w_qkv,
        w_out,
    )
    results = rear(
        hidden_states,
        diff,
        gate_rows,
        scale,
        qkv,
        grad_att,
        factors,
        attended.reshape(1024, LOCAL),
        w_qkv,
        modded.reshape(1024, WIDTH),
        up_all.reshape(1024, WIDTH),
    )
    grad_hidden, qkv_grad, out_grad, *sums = hand_over(*results)
    return (grad_hidden, qkv_grad, out_grad.T, *sums)


def solution(mesh):
    in_specs = (
        P("frame", "fsdp", None),
        P("frame", "fsdp", None),
        P(),
        P(),
        P(),
        P(None, None, "fsdp"),
        P("fsdp", None),
    )
    out_specs = (
        P("frame", "fsdp", None),
        P(None, "frame", "fsdp"),
        P("fsdp", "frame"),
        P(),
        P(),
        P(),
    )
    return jax.shard_map(shards, mesh=mesh, in_specs=in_specs, out_specs=out_specs, check_vma=False)
```

```python
import functools
import jax
import jax.numpy as jnp
from jax import lax
from jax.experimental import pallas as pl
from jax.experimental.pallas import tpu as pltpu
from jax.sharding import PartitionSpec as P

HEAD_DIM = 128
HEADS = 3
LOCAL = 384
WIDTH = 3072
HALF = 64
TILE = 512
INV_ROOT = HEAD_DIM ** (-0.5)
MESH = pl.DeviceIdType.MESH
BF = jnp.bfloat16
F32 = jnp.float32
VMEM_BYTES = 60 * 1024 * 1024


class Place:
    def __init__(self):
        fr = lax.axis_index("frame")
        fs = lax.axis_index("fsdp")
        self.fr = fr
        self.fs = fs
        self.x = lax.div(fs, 2)
        self.lo = lax.rem(fs, 2)
        self.core = lax.rem(fr, 2)
        self.group = lax.div(fr, 2)
        other = fs + 1 - 2 * self.lo
        self.hi = lax.rem(self.group, 2)
        self.z = lax.div(self.group, 2)
        self.right = (fr, lax.rem(fs + 2, 8))
        self.left = (fr, lax.rem(fs + 6, 8))
        self.side = tuple((self.frame(self.z, h, self.core), other) for h in range(2))
        self.across = (fr + 2 - 4 * self.hi, other)
        self.beside = (fr, other)

    def frame(self, z, hi, core):
        return 4 * z + 2 * hi + core

    def along(self, off):
        return lax.rem(self.x + off, 4)

    def greet(self, heads):
        barrier = pltpu.get_barrier_semaphore()

        def signal(peer):
            pl.semaphore_signal(barrier, inc=1, device_id=peer, device_id_type=MESH)

        signal(self.across)
        if heads:
            for step in range(1, 8):
                signal((self.fr, lax.rem(self.fs + step, 8)))
        else:
            for peer in (self.right, self.left, self.beside):
                signal(peer)
        loop(15, lambda i: signal((lax.rem(self.fr + i + 1, 16), self.fs)))

    def met(self, heads):
        pl.semaphore_wait(pltpu.get_barrier_semaphore(), 23 if heads else 19)


def remote(src, dst, send_sem, recv_sem, device):
    return pltpu.make_async_remote_copy(
        src_ref=src,
        dst_ref=dst,
        send_sem=send_sem,
        recv_sem=recv_sem,
        device_id=device,
        device_id_type=MESH,
    )


def landed(ref, sem):
    pltpu.make_async_copy(ref, ref, sem).wait()


def loop(count, body):
    def step(i, carry):
        body(i)
        return carry

    lax.fori_loop(0, count, step, 0)


def others_first(p):
    return 2 + p - lax.div(3 * p * (p - 1), 2)


def load_weight(w_hbm, weight, sem):
    if len(w_hbm.shape) == 3:
        copies = [
            pltpu.make_async_copy(w_hbm.at[c], weight.at[:, pl.ds(c * LOCAL, LOCAL)], sem.at[c])
            for c in range(3)
        ]
    else:
        copies = [pltpu.make_async_copy(w_hbm, weight, sem.at[0])]
    for copy in copies:
        copy.start()
    return copies


def gather_phase(at, own, weight, w_copies, kept_all, sent_to, factors, scratch, between=None):
    full, out, x_send, y_send, recv, o_send, o_recv, keep_sem = scratch
    project = factors is not None

    def to_right(slot, src, xi, h, n):
        return remote(src, full.at[slot, xi, h], x_send.at[n], recv.at[slot, xi, h], at.right)

    def to_left(slot, src, xi, h, n):
        return remote(src, full.at[slot, xi, h], x_send.at[n], recv.at[slot, xi, h], at.left)

    def to_side(src, xi, h, n):
        return remote(
            src, full.at[1, xi, at.hi], y_send.at[n], recv.at[1, xi, at.hi], at.side[h]
        )

    xl, xr, xf = at.along(3), at.along(1), at.along(2)
    first = [
        to_right(0, own.at[0], at.x, 0, 0),
        to_left(0, own.at[1], at.x, 1, 1),
        to_side(own.at[0], at.x, 0, 0),
        to_side(own.at[1], at.x, 1, 1),
    ]
    for copy in first:
        copy.start()
    full[0, at.x] = own[...]
    second = [
        to_right(0, full.at[0, xl, 0], xl, 0, 2),
        to_left(0, full.at[0, xr, 1], xr, 1, 3),
    ]
    third = [
        to_right(0, own.at[1], at.x, 1, 4),
        to_side(full.at[0, xf, 0], xf, 0, 4),
        to_left(0, own.at[0], at.x, 0, 5),
        to_side(full.at[0, xf, 1], xf, 1, 5),
    ]
    fourth = [
        to_right(1, full.at[1, at.x, 1], at.x, 1, 6),
        to_left(1, full.at[1, at.x, 0], at.x, 0, 7),
    ]
    if project:
        fourth.append(to_right(1, full.at[1, at.x, 0], at.x, 0, 8))
        fourth.append(to_left(1, full.at[1, at.x, 1], at.x, 1, 9))
    early_sides = [to_side(full.at[0, (xl, xr)[h], h], (xl, xr)[h], h, 2) for h in range(2)]
    late_sides = [to_side(full.at[0, (xl, xr)[h], 1 - h], (xl, xr)[h], 1 - h, 3) for h in range(2)]
    for copy in w_copies:
        copy.wait()

    def arrived(slot, xi, h):
        landed(full.at[slot, xi, h], recv.at[slot, xi, h])

    def early(k):
        @pl.when(k == 1)
        def _():
            arrived(0, xl, 0)
            second[0].start()
            if not project:
                pl.when(at.hi == 0)(lambda: early_sides[0].start())
            arrived(0, xr, 1)
            second[1].start()
            if not project:
                pl.when(at.hi == 1)(lambda: early_sides[1].start())
            arrived(1, at.x, 0)
            arrived(1, at.x, 1)

        work(k, k, at.x)

    def late(i):
        slot = lax.div(i, 3)
        xi = at.along(others_first(lax.rem(i, 3)))

        @pl.when(i == 0)
        def _():
            arrived(0, xf, 0)
            third[0].start()
            third[1].start()
            arrived(0, xf, 1)
            third[2].start()
            third[3].start()

        @pl.when(i == 1)
        def _():
            arrived(0, xl, 1)
            for copy in fourth[0::2]:
                copy.start()
            if not project:
                pl.when(at.hi == 0)(lambda: late_sides[0].start())

        @pl.when(i == 2)
        def _():
            arrived(0, xr, 0)
            for copy in fourth[1::2]:
                copy.start()
            if not project:
                pl.when(at.hi == 1)(lambda: late_sides[1].start())

        if between is not None:
            pl.when(i == 4)(between)

        @pl.when(i >= 3)
        def _():
            arrived(1, xi, 0)
            arrived(1, xi, 1)

        work(i + 2, slot, xi)

    def work(k, slot, xi):
        pltpu.make_async_copy(full.at[slot, xi], kept_all.at[slot, xi], keep_sem).start()
        tokens = full[slot, xi].reshape(2 * HALF, WIDTH)
        if project:
            both = jnp.dot(tokens, weight[...], preferred_element_type=F32)
            lane = lax.broadcasted_iota(jnp.int32, (2 * HALF, HEAD_DIM), 1)
            kept = jnp.zeros((2 * HALF, HEAD_DIM), F32)
            for j in range(3 * HEADS):
                block = both[:, j * HEAD_DIM : (j + 1) * HEAD_DIM]
                if j < 2 * HEADS:
                    factor = lax.rsqrt(jnp.mean(block * block, -1, keepdims=True) + 1e-06)
                    kept = jnp.where(lane == j, factor, kept)
                    block = block * factor
                out[pl.ds(8 * k, 8), :, j * HEAD_DIM : (j + 1) * HEAD_DIM] = block.astype(BF).reshape(
                    8, 16, HEAD_DIM
                )
            factors[slot, xi] = kept
        else:
            both = lax.dot_general(
                tokens, weight[...], (((1,), (1,)), ((), ())), preferred_element_type=F32
            )
            out[pl.ds(8 * k, 8)] = both.astype(BF).reshape(8, 16, LOCAL)
        to_core = lax.rem(xi, 2)
        to_slot = 2 * lax.div(xi, 2) + lax.rem(at.lo + slot, 2)

        def give(b):
            z, upper = lax.rem(b, 4), lax.div(b, 4)
            target = at.frame(z, (1 - slot) * upper + slot * at.hi, to_core)
            origin = at.frame(at.z, (1 - slot) * at.hi + slot * upper, at.core)
            src = out.at[8 * k + b]
            dst = sent_to.at[to_slot, origin]

            @pl.when(target == at.fr)
            def _():
                pltpu.make_async_copy(src, dst, o_recv.at[to_slot]).start()

            @pl.when(target != at.fr)
            def _():
                remote(src, dst, o_send, o_recv.at[to_slot], (target, at.fs)).start()

        loop(8, give)

    loop(2, early)
    loop(6, late)

    def end():
        for copy in first + second + third + fourth:
            copy.wait_send()
        for h in range(0 if project else 2):

            @pl.when(at.hi == h)
            def _(h=h):
                early_sides[h].wait_send()
                late_sides[h].wait_send()

        landed(out.at[pl.ds(0, 58)], o_send)
        pltpu.make_async_copy(full, kept_all, keep_sem).wait()

    return end


def gather_scratch(cols):
    return [
        pltpu.VMEM((2, 4, 2, HALF, WIDTH), BF),
        pltpu.VMEM((64, 16, cols), BF),
        pltpu.SemaphoreType.DMA((10,)),
        pltpu.SemaphoreType.DMA((6,)),
        pltpu.SemaphoreType.DMA((2, 4, 2)),
        pltpu.SemaphoreType.DMA,
        pltpu.SemaphoreType.DMA((4,)),
        pltpu.SemaphoreType.DMA,
    ]


def vmem(count):
    return [pl.BlockSpec(memory_space=pltpu.VMEM)] * count


def anywhere(count):
    return [pl.BlockSpec(memory_space=pl.ANY)] * count


def same_patch():
    rows = lax.broadcasted_iota(jnp.int32, (256, 256), 0)
    cols = lax.broadcasted_iota(jnp.int32, (256, 256), 1)
    return lax.rem(rows, 8) == lax.rem(cols, 8)


def dot_nt(a, b):
    return lax.dot_general(a, b, (((1,), (1,)), ((), ())), preferred_element_type=F32)


def dot_tn(a, b):
    return lax.dot_general(a, b, (((0,), (0,)), ((), ())), preferred_element_type=F32)


def softmax(query, key):
    scores = dot_nt(query, key) * INV_ROOT
    expo = jnp.where(same_patch(), jnp.exp(scores), 0.0)
    return expo / jnp.sum(expo, -1, keepdims=True)


class WeightSums:
    def __init__(self, at, flat, up_all, attended, dproj, result, *scratch):
        self.at = at
        self.flat, self.up_all, self.attended, self.dproj = flat, up_all, attended, dproj
        self.result = result
        (
            self.rows, self.turned, self.part, self.twin, self.far, self.near, self.last,
            self.row_sem, self.t_send, self.t_recv, self.f_send, self.f_recv,
            self.n_send, self.n_recv, self.l_send, self.l_recv,
        ) = scratch
        fr, fs = at.fr, at.fs
        self.hi = lax.rem(at.group, 2)
        self.z = lax.div(at.group, 2)
        self.sibling = (fr + 1 - 2 * at.core, fs)
        self.over = (fr + 2 - 4 * self.hi, fs)
        self.up = (lax.rem(fr + 4, 16), fs)
        self.down = (lax.rem(fr + 12, 16), fs)

    def group(self, off, hi):
        return 2 * lax.rem(self.z + off, 4) + hi

    def flagged(self, flag):
        return flag * self.hi + (1 - flag) * (1 - self.hi)

    def target(self, m):
        q, b = lax.div(m, 2), lax.rem(m, 2)
        inner = lax.div(q * (3 - q), 2)
        base = 2 - q + lax.div(q * (q - 1), 2) - lax.div(q * (q - 1) * (q - 2), 3)
        flag = (1 - inner) * b + inner * (q - 1)
        return self.group(base + 2 * inner * b, self.flagged(flag))

    def load(self, source, j, slot):
        cols = pl.ds(pl.multiple_of(j * LOCAL, LOCAL), LOCAL)
        return pltpu.make_async_copy(
            source.at[:, cols], self.rows.at[slot], self.row_sem.at[slot]
        )

    def fetch(self, source, j, slot):
        self.load(source, j, slot).start()

    def out_rows(self, m):
        slot = lax.rem(m, 2)
        self.load(self.up_all, m, slot).wait()

        @pl.when(m < 7)
        def _():
            self.fetch(self.up_all, m + 1, 1 - slot)

        @pl.when(m == 7)
        def _():
            self.fetch(self.flat, self.target(0), 0)

        self.turned[...] = jnp.transpose(self.rows[slot])
        value = jnp.dot(self.turned[...], self.attended[...], preferred_element_type=F32)
        self.part[m, :, :, 3 * LOCAL :] = value.astype(BF).reshape(2, 192, LOCAL)

    def to_twin(self, j):
        return remote(
            self.part.at[j, 1 - self.at.core],
            self.twin.at[j],
            self.t_send.at[j],
            self.t_recv.at[j],
            self.sibling,
        )

    def rows_of(self, off, flag, half):
        j = self.group(off, self.flagged(flag))
        return self.part.at[j, self.at.core, pl.ds(half * 96, 96)]

    def to_far(self, d, flag):
        return remote(
            self.rows_of(2, flag, d), self.far.at[d, flag], self.f_send.at[d, flag],
            self.f_recv.at[d, flag], (self.up, self.down)[d],
        )

    def to_near(self, d, flag, half):
        return remote(
            self.rows_of((1, 3)[d], flag, half), self.near.at[d, flag, half],
            self.n_send.at[d, flag, half], self.n_recv.at[d, flag, half],
            (self.up, self.down)[d],
        )

    def tile(self, m):
        j = self.target(m)
        slot = lax.rem(m, 2)
        self.load(self.flat, j, slot).wait()

        @pl.when(m < 7)
        def _():
            self.fetch(self.flat, self.target(m + 1), 1 - slot)

        self.turned[...] = jnp.transpose(self.rows[slot])
        for c in range(3):
            cols = slice(c * LOCAL, (c + 1) * LOCAL)
            other = self.dproj[:, :, :, cols].reshape(1024, LOCAL)
            value = jnp.dot(self.turned[...], other, preferred_element_type=F32)
            self.part[j, :, :, cols] = value.astype(BF).reshape(2, 192, LOCAL)
        self.to_twin(j).start()

        @pl.when(m > 0)
        def _():
            self.merge(m - 1)

    def add(self, held, other, count):
        def rows(i):
            some = pl.ds(pl.multiple_of(i * 48, 16), 48)
            held[some, :] = (held[some, :].astype(F32) + other[some, :].astype(F32)).astype(BF)

        loop(count, rows)

    def merge(self, m):
        j = self.target(m)
        landed(self.twin.at[j], self.t_recv.at[j])
        self.add(self.part.at[j, self.at.core], self.twin.at[j], 4)
        for flag in range(2):

            @pl.when(m == flag)
            def _(flag=flag):
                for d in range(2):
                    self.to_far(d, flag).start()

            @pl.when(m == 2 + 2 * flag)
            def _(flag=flag):
                if flag == 1:
                    self.relay(0)
                self.to_near(0, flag, 1).start()

            @pl.when(m == 3 + 2 * flag)
            def _(flag=flag):
                self.to_near(1, flag, 0).start()

    def relay(self, flag):
        for d in range(2):
            landed(self.far.at[d, flag], self.f_recv.at[d, flag])
            self.add(self.rows_of((1, 3)[d], flag, d), self.far.at[d, flag], 2)
            self.to_near(d, flag, d).start()

    def arrived(self, flag):
        for d in range(2):
            for half in range(2):
                landed(self.near.at[d, flag, half], self.n_recv.at[d, flag, half])

    def both(self, flag, half, some):
        value = self.rows_of(0, flag, half)[some, :].astype(F32)
        for d in range(2):
            value = value + self.near[d, flag, half, some, :].astype(F32)
        return value

    def to_last(self):
        source = self.part.at[self.group(0, self.flagged(0)), self.at.core]
        return remote(source, self.last, self.l_send, self.l_recv, self.over)

    def turn(self):
        self.arrived(0)
        for half in range(2):
            held = self.rows_of(0, 0, half)

            def rows(i, half=half, held=held):
                some = pl.ds(pl.multiple_of(i * 48, 16), 48)
                held[some, :] = self.both(0, half, some).astype(BF)

            loop(2, rows)
        self.to_last().start()

    def finish(self):
        self.arrived(1)
        landed(self.last, self.l_recv)
        for half in range(2):

            def end(i, half=half):
                some = pl.ds(pl.multiple_of(i * 48, 16), 48)
                there = pl.ds(pl.multiple_of(half * 96 + i * 48, 16), 48)
                value = self.both(1, half, some) + self.last[there, :].astype(F32)
                value = value.astype(BF)
                for c in range(3):
                    self.result[0][c, there, :] = value[:, c * LOCAL : (c + 1) * LOCAL]
                self.result[1][there, :] = value[:, 3 * LOCAL :]

            loop(2, end)
        for d in range(2):
            for flag in range(2):
                self.to_far(d, flag).wait_send()
                for half in range(2):
                    self.to_near(d, flag, half).wait_send()
        self.to_last().wait_send()
        loop(8, lambda j: self.to_twin(j).wait_send())


def tile_loop(body):
    loop(WIDTH // TILE, lambda j: body(pl.ds(pl.multiple_of(j * TILE, TILE), TILE)))


class Scatter:
    def __init__(self, at, qkv, qkv_sem, grad, weight, tokens, dproj, factors, scratch):
        self.at, self.qkv, self.qkv_sem, self.grad = at, qkv, qkv_sem, grad
        self.weight, self.tokens, self.dproj, self.factors = weight, tokens, dproj, factors
        (
            self.out, self.part, self.own, self.from_side, self.far, self.near, self.passed,
            self.o_send, self.o_recv, self.y_send, self.y_recv, self.f_send, self.f_recv,
            self.n_send, self.n_recv, self.p_send, self.p_recv,
        ) = scratch
        self.back = grad is not None
        self.xl, self.xr, self.xf = at.along(3), at.along(1), at.along(2)

    def put(self, i, block, value):
        cols = slice(block * HEAD_DIM, (block + 1) * HEAD_DIM)
        self.out[i, :, :, cols] = value.astype(BF).reshape(16, 16, HEAD_DIM)

    def attend(self, i):
        at, put = self.at, self.put
        slot = lax.div(i, 2)
        if self.back:
            slot = 1 - slot
        xh = lax.rem(lax.div(at.x, 2) + i, 2)
        t = 2 * xh + lax.rem(at.lo + slot, 2)
        if self.qkv_sem is not None:
            landed(self.qkv.at[t], self.qkv_sem.at[t])

        def columns(ref, block):
            return ref[t, :, :, block * HEAD_DIM : (block + 1) * HEAD_DIM].reshape(256, HEAD_DIM)

        for h in range(HEADS):
            query, key, value = (columns(self.qkv, c * HEADS + h) for c in range(3))
            probs = softmax(query, key)
            low = probs.astype(BF)
            if not self.back:
                put(i, h, jnp.dot(low, value, preferred_element_type=F32))
                continue
            grad_in = columns(self.grad, h)
            dprob = dot_nt(grad_in, value)
            put(i, 2 * HEADS + h, dot_tn(low, grad_in))
            dscore = (probs * (dprob - jnp.sum(probs * dprob, -1, keepdims=True))).astype(BF)
            for c, normed, product in (
                (0, query, jnp.dot(dscore, key, preferred_element_type=F32)),
                (1, key, dot_tn(dscore, query)),
            ):
                step_in = (product * INV_ROOT).astype(BF).astype(F32)
                wide = normed.astype(F32)
                put(
                    i,
                    c * HEADS + h,
                    step_in - wide * jnp.mean(step_in * wide, -1, keepdims=True),
                )
        xi = 2 * xh + at.core

        def give(f):
            upper = lax.rem(lax.div(f, 2), 2)
            target = f + 2 * slot * (at.hi - upper)
            piece = 4 * ((1 - slot) * at.hi + slot * upper) + at.z
            src = self.out.at[i, f]
            dst = self.tokens.at[slot, xi, piece]

            @pl.when(target == at.fr)
            def _():
                pltpu.make_async_copy(src, dst, self.o_recv.at[slot, xi]).start()

            @pl.when(target != at.fr)
            def _():
                remote(
                    src, dst, self.o_send.at[i], self.o_recv.at[slot, xi], (target, at.fs)
                ).start()

        loop(16, give)

    def take(self, slot, xi):
        landed(self.tokens.at[slot, xi], self.o_recv.at[slot, xi])
        if self.back:
            for j in range(3 * HEADS):
                cols = slice(j * HEAD_DIM, (j + 1) * HEAD_DIM)
                block = self.tokens[slot, xi, :, :, cols].reshape(2 * HALF, HEAD_DIM)
                if j < 2 * HEADS:
                    block = (block.astype(F32) * self.factors[slot, xi, :, j : j + 1]).astype(BF)
                self.dproj[slot, xi, :, cols] = block

    def pair(self, p):
        return self.at.along(1 + p), self.at.along(3 - 3 * p)

    def products(self, slot, p, into):
        pair = self.pair(p)
        source = self.dproj if self.back else self.tokens
        rows = jnp.concatenate([source[slot, xi].reshape(2 * HALF, -1) for xi in pair])

        def tiles(tile):
            if self.back:
                value = dot_nt(rows, self.weight[tile, :])
            else:
                value = jnp.dot(rows, self.weight[:, tile], preferred_element_type=F32)
            value = value.astype(BF)
            for n, xi in enumerate(pair):
                some = value[n * 2 * HALF : (n + 1) * 2 * HALF]
                into[xi, :, :, tile] = some.reshape(2, HALF, TILE)

        tile_loop(tiles)

    def add(self, into, xi, h, other):
        def tiles(tile):
            value = into[xi, h, :, tile].astype(F32) + other[:, tile].astype(F32)
            into[xi, h, :, tile] = value.astype(BF)

        tile_loop(tiles)

    def to_side(self, xi, h):
        return remote(
            self.part.at[xi, h], self.from_side.at[xi, self.at.hi], self.y_send.at[xi, h],
            self.y_recv.at[xi, self.at.hi], self.at.side[h],
        )

    def side_arrived(self, xi, h):
        landed(self.from_side.at[xi, h], self.y_recv.at[xi, h])
        self.add(self.own, xi, h, self.from_side.at[xi, h])

    def way(self, d):
        return (self.at.right, self.at.left)[d]

    def pass_on(self, d):
        source = self.part.at[(self.xr, self.xl)[d], d]
        return remote(source, self.passed.at[d], self.p_send.at[d], self.p_recv.at[d], self.way(d))

    def to_far(self, d):
        source = self.own.at[self.xf, d]
        return remote(source, self.far.at[d], self.f_send.at[d], self.f_recv.at[d], self.way(d))

    def to_near(self, d, h):
        source = self.own.at[(self.xr, self.xl)[d], h]
        return remote(
            source, self.near.at[d, h], self.n_send.at[d, h], self.n_recv.at[d, h], self.way(d)
        )

    def add_passed(self):
        for h in range(2):
            landed(self.passed.at[h], self.p_recv.at[h])
            self.add(self.part, self.at.x, h, self.passed.at[h])

    def sides_to_near(self):
        for h in range(2):
            self.side_arrived(self.at.along(3 - 2 * self.at.hi), h)
        self.to_near(0, 1).start()
        self.to_near(1, 0).start()

    def sides_to_far(self):
        for h in range(2):
            self.side_arrived(self.xf, h)
            self.to_far(h).start()

    def far_to_near(self):
        for d, xi in ((0, self.xr), (1, self.xl)):
            landed(self.far.at[d], self.f_recv.at[d])
            self.add(self.own, xi, d, self.far.at[d])
            self.to_near(d, d).start()

    def arrive(self):
        for d, h in ((0, 1), (1, 0), (0, 0), (1, 1)):
            landed(self.near.at[d, h], self.n_recv.at[d, h])

    def total(self, h, some, cols=slice(None)):
        return (
            self.own[self.at.x, h, some, cols].astype(F32)
            + self.near[0, h, some, cols].astype(F32)
            + self.near[1, h, some, cols].astype(F32)
        )

    def forward(self):
        x = self.at.x
        for slot, into in ((1, self.part), (0, self.own)):
            for xi in self.pair(1):
                self.take(slot, xi)
            self.products(slot, 1, into)
            if slot == 1:
                for h in range(2):
                    self.to_side(self.xf, h).start()
        for xi in self.pair(0):
            self.take(1, xi)
        self.products(1, 0, self.part)
        self.pass_on(0).start()
        self.pass_on(1).start()
        for h in range(2):
            self.to_side(self.xf, h).wait_send()
            self.to_side((self.xl, self.xr)[h], h).start()
        self.sides_to_far()
        for xi in self.pair(0):
            self.take(0, xi)
        self.products(0, 0, self.own)
        self.add_passed()
        for h in range(2):
            self.to_side((self.xl, self.xr)[h], h).wait_send()
            self.to_side(x, h).start()
        self.sides_to_near()
        self.far_to_near()
        for h in range(2):
            self.side_arrived(x, h)
        self.arrive()

    def backward(self, sums):
        x = self.at.x

        def first(p):
            for xi in self.pair(p):
                self.take(1, xi)
            self.products(1, p, self.part)

            @pl.when(p == 0)
            def _():
                for d in range(2):
                    self.pass_on(d).start()
                    self.to_side((self.xl, self.xr)[d], d).start()

        loop(2, first)
        loop(4, lambda xi: self.take(0, xi))
        loop(2, sums.tile)

        def second(p):
            self.products(0, p, self.own)

            @pl.when(p == 0)
            def _():
                for h in range(2):
                    self.to_side((self.xl, self.xr)[h], h).wait_send()
                    self.to_side(self.xf, h).start()
                self.add_passed()
                self.sides_to_near()

            loop(2, lambda q: sums.tile(2 + 2 * p + q))

        loop(2, second)
        for h in range(2):
            self.to_side(self.xf, h).wait_send()
            self.to_side(x, h).start()
        self.sides_to_far()
        loop(2, lambda q: sums.tile(6 + q))
        sums.merge(7)
        self.far_to_near()
        sums.relay(1)
        for h in range(2):
            self.side_arrived(x, h)
        sums.turn()
        self.arrive()

    def end(self):
        for d in range(2):
            self.pass_on(d).wait_send()
            self.to_far(d).wait_send()
            for h in range(2):
                self.to_near(d, h).wait_send()
            self.to_side(self.at.x, d).wait_send()
        for i in range(4):
            other = (i < 2) == self.back
            landed(self.out.at[i, pl.ds(0, 14 if other else 15)], self.o_send.at[i])


def scatter_scratch(cols):
    return [
        pltpu.VMEM((4, 16, 16, cols), BF),
        pltpu.VMEM((4, 2, HALF, WIDTH), BF),
        pltpu.VMEM((4, 2, HALF, WIDTH), BF),
        pltpu.VMEM((4, 2, HALF, WIDTH), BF),
        pltpu.VMEM((2, HALF, WIDTH), BF),
        pltpu.VMEM((2, 2, HALF, WIDTH), BF),
        pltpu.VMEM((2, HALF, WIDTH), BF),
        pltpu.SemaphoreType.DMA((4,)),
        pltpu.SemaphoreType.DMA((2, 4)),
        pltpu.SemaphoreType.DMA((4, 2)),
        pltpu.SemaphoreType.DMA((4, 2)),
        pltpu.SemaphoreType.DMA((2,)),
        pltpu.SemaphoreType.DMA((2,)),
        pltpu.SemaphoreType.DMA((2, 2)),
        pltpu.SemaphoreType.DMA((2, 2)),
        pltpu.SemaphoreType.DMA((2,)),
        pltpu.SemaphoreType.DMA((2,)),
    ]


def each_rows(body):
    loop(4, lambda j: body(j))


def pieces(ref, j, cols=slice(None)):
    first, second = (ref[f, pl.ds(pl.multiple_of(16 * j, 16), 16), cols].astype(F32) for f in range(2))
    return [jnp.concatenate([first[i : i + 8], second[i : i + 8]]) for i in (0, 8)]


def place_of(j, n):
    inner = pl.ds(pl.multiple_of(lax.rem(j, 2) * 32 + 16 * n, 16), 16)
    return lax.div(j, 2), inner, pl.ds(pl.multiple_of(j * 32 + 16 * n, 16), 16)


def row_factor(states):
    return lax.rsqrt(jnp.mean(states * states, -1, keepdims=True) + 1e-06)


def front_kernel(
    hidden, teacher, scale, shift, gate, w_qkv, w_out,
    kept_modded, kept_up, qkv_hbm, factors_hbm, tokens_hbm, diff_hbm, grad_att, gate_rows,
    qkv, factors, tokens, diff, out_sem, own, own_up, qkv_weight, out_weight, w_sem, *scratch,
):
    at = Place()
    qkv_copies = load_weight(w_qkv, qkv_weight, w_sem.at[0])
    out_copies = load_weight(w_out, out_weight, w_sem.at[1])
    at.greet(False)

    def modulate(j):
        for n, states in enumerate(pieces(hidden, j)):
            h, inner, _ = place_of(j, n)
            value = states * row_factor(states) * (1.0 + scale[...]) + shift[...]
            own[h, inner, :] = value.astype(BF)

    each_rows(modulate)
    at.met(False)
    ahead, middle, behind = scratch[:8], scratch[8:25], scratch[25:]
    mix = Scatter(at, qkv, ahead[6], None, out_weight, tokens, None, None, middle)
    end_ahead = gather_phase(
        at, own, qkv_weight, qkv_copies, kept_modded, qkv, factors, ahead,
        lambda: loop(2, mix.attend),
    )
    loop(2, lambda i: mix.attend(2 + i))
    for copy in out_copies:
        copy.wait()
    mix.forward()
    gate_rows[...] = jnp.zeros_like(gate_rows)

    def compare(j):
        def tiles(cols):
            rate = gate[:, cols]
            both = zip(pieces(hidden, j, cols), pieces(teacher, j, cols))
            for n, (states, target) in enumerate(both):
                h, inner, some = place_of(j, n)
                mixed = mix.total(h, inner, cols)
                change = states + rate * mixed - target
                diff[some, cols] = change
                own_up[h, inner, cols] = (rate * change).astype(BF)
                product = change * mixed
                gate_rows[:, cols] += product[:8] + product[8:]

        tile_loop(tiles)

    each_rows(compare)
    leaving = [
        pltpu.make_async_copy(here, there, out_sem.at[i])
        for i, (here, there) in enumerate(
            ((qkv, qkv_hbm), (factors, factors_hbm), (tokens, tokens_hbm), (diff, diff_hbm))
        )
    ]
    for copy in leaving:
        copy.start()
    end_behind = gather_phase(at, own_up, out_weight, [], kept_up, grad_att, None, behind)
    for copy in leaving:
        copy.wait()
    end_ahead()
    mix.end()
    end_behind()
    loop(4, lambda t: landed(grad_att.at[t], behind[6].at[t]))


def front(hidden, teacher, scale, shift, gate, w_qkv, w_out):
    kept = jax.ShapeDtypeStruct((2, 4, 2, HALF, WIDTH), BF)
    return pl.pallas_call(
        front_kernel,
        out_shape=[
            kept,
            kept,
            jax.ShapeDtypeStruct((4, 16, 16, 3 * LOCAL), BF),
            jax.ShapeDtypeStruct((2, 4, 2 * HALF, HEAD_DIM), F32),
            jax.ShapeDtypeStruct((2, 4, 8, 16, LOCAL), BF),
            jax.ShapeDtypeStruct((2 * HALF, WIDTH), F32),
            jax.ShapeDtypeStruct((4, 16, 16, LOCAL), BF),
            jax.ShapeDtypeStruct((8, WIDTH), F32),
        ],
        in_specs=vmem(5) + anywhere(2),
        out_specs=anywhere(6) + vmem(2),
        scratch_shapes=[
            pltpu.VMEM((4, 16, 16, 3 * LOCAL), BF),
            pltpu.VMEM((2, 4, 2 * HALF, HEAD_DIM), F32),
            pltpu.VMEM((2, 4, 8, 16, LOCAL), BF),
            pltpu.VMEM((2 * HALF, WIDTH), F32),
            pltpu.SemaphoreType.DMA((4,)),
            pltpu.VMEM((2, HALF, WIDTH), BF),
            pltpu.VMEM((2, HALF, WIDTH), BF),
            pltpu.VMEM((WIDTH, 3 * LOCAL), BF),
            pltpu.VMEM((LOCAL, WIDTH), BF),
            pltpu.SemaphoreType.DMA((2, 3)),
        ]
        + gather_scratch(3 * LOCAL)
        + scatter_scratch(LOCAL)
        + gather_scratch(LOCAL),
        compiler_params=pltpu.CompilerParams(
            collective_id=0, has_side_effects=True, vmem_limit_bytes=VMEM_BYTES
        ),
        cost_estimate=pl.CostEstimate(
            flops=2 * 1024 * WIDTH * 5 * LOCAL, bytes_accessed=50_000_000, transcendentals=0
        ),
        name="front",
    )(hidden, teacher, scale, shift, gate, w_qkv, w_out)


class Totals:
    def __init__(self, at, rows, result, scratch):
        self.at, self.rows, self.result = at, rows, result
        (
            self.by_head, self.by_frame, self.partial,
            self.s1, self.r1, self.s2, self.r2, self.s3, self.r3,
        ) = scratch
        self.started = []

    def piece(self, ref, i):
        return ref.at[:, pl.ds(pl.multiple_of(i * LOCAL, LOCAL), LOCAL)]

    def send(self, copies):
        for copy in copies:
            copy.start()
        self.started += copies

    def head(self, i):
        return (self.at.fr, lax.rem(self.at.fs + i, 8))

    def run(self, between, later):
        fr, fs = self.at.fr, self.at.fs
        self.send(
            [
                remote(
                    self.piece(self.rows, self.head(i)[1]), self.by_head.at[fs], self.s1.at[i],
                    self.r1, self.head(i),
                )
                for i in range(1, 8)
            ]
        )
        self.by_head[fs] = self.piece(self.rows, fs)[...]
        between()
        landed(self.by_head.at[pl.ds(0, 7)], self.r1)
        value = self.by_head[0]
        for i in range(1, 8):
            value = value + self.by_head[i]
        self.partial[...] = value
        self.by_frame[fr] = value
        self.send(
            [
                remote(
                    self.partial, self.by_frame.at[fr], self.s2.at[i], self.r2,
                    (lax.rem(fr + i, 16), fs),
                )
                for i in range(1, 16)
            ]
        )
        later()
        landed(self.by_frame.at[pl.ds(0, 15)], self.r2)
        value = self.by_frame[0]
        for i in range(1, 16):
            value = value + self.by_frame[i]
        here = self.piece(self.result, fs)
        here[...] = value
        self.send(
            [remote(here, here, self.s3.at[i], self.r3, self.head(i)) for i in range(1, 8)]
        )

    def end(self):
        landed(self.result.at[:, pl.ds(0, 7 * LOCAL)], self.r3)
        for copy in self.started:
            copy.wait_send()


def rear_kernel(
    gate_rows, scale, qkv, grad, hidden_hbm, diff_hbm, factors_hbm, attended_hbm, w_qkv, modded,
    up_all, grad_hidden, qkv_grad, out_grad, totals, hidden, diff, factors, attended, in_sem, weight,
    w_sem, tokens, dproj, scale_rows, shift_rows, rows,
    *scratch,
):
    at = Place()
    late = [
        pltpu.make_async_copy(source, here, in_sem.at[i])
        for i, (source, here) in enumerate(
            (
                (attended_hbm, attended),
                (factors_hbm, factors),
                (hidden_hbm, hidden),
                (diff_hbm, diff),
            )
        )
    ]
    w_copies = load_weight(w_qkv, weight, w_sem)
    for copy in late:
        copy.start()
    sums = WeightSums(at, modded, up_all, attended, dproj, (qkv_grad, out_grad), *scratch[17:33])
    sums.fetch(up_all, 0, 0)
    at.greet(True)
    at.met(True)
    back = Scatter(at, qkv, None, grad, weight, tokens, dproj, factors, scratch[:17])
    loop(4, back.attend)
    for copy in late:
        copy.wait()
    loop(8, sums.out_rows)
    for copy in w_copies:
        copy.wait()
    back.backward(sums)
    scale_rows[...] = jnp.zeros_like(scale_rows)
    shift_rows[...] = jnp.zeros_like(shift_rows)

    def add_up(j):
        rates = [row_factor(states) for states in pieces(hidden, j)]

        def tiles(cols):
            for n, states in enumerate(pieces(hidden, j, cols)):
                h, inner, _ = place_of(j, n)
                dmod = back.total(h, inner, cols)
                both = dmod * (states * rates[n])
                scale_rows[:, cols] += both[:8] + both[8:]
                shift_rows[:, cols] += dmod[:8] + dmod[8:]

        tile_loop(tiles)

    def close(j):
        done = []
        for n, states in enumerate(pieces(hidden, j)):
            h, inner, some = place_of(j, n)
            factor = row_factor(states)
            normed = states * factor
            dnorm = back.total(h, inner) * (1.0 + scale[...])
            value = dnorm - normed * jnp.mean(dnorm * normed, -1, keepdims=True)
            done.append(diff[some, :] + factor * value)
        for f in range(2):
            both = jnp.concatenate([value[8 * f : 8 * f + 8] for value in done])
            grad_hidden[f, pl.ds(pl.multiple_of(16 * j, 16), 16), :] = both.astype(BF)

    each_rows(add_up)
    rows[...] = jnp.zeros_like(rows)
    for i, ref in enumerate((scale_rows, shift_rows, gate_rows)):
        rows[i : i + 1, :] = jnp.sum(ref[...], 0, keepdims=True)
    total = Totals(at, rows, totals, scratch[33:])
    total.run(lambda: each_rows(close), sums.finish)
    total.end()
    back.end()


def rear(hidden, diff, gate_rows, scale, qkv, grad, factors, attended, w_qkv, modded, up_all):
    cols = 3 * LOCAL
    return pl.pallas_call(
        rear_kernel,
        out_shape=[
            jax.ShapeDtypeStruct((2, HALF, WIDTH), BF),
            jax.ShapeDtypeStruct((3, 192, LOCAL), BF),
            jax.ShapeDtypeStruct((192, LOCAL), BF),
            jax.ShapeDtypeStruct((8, WIDTH), F32),
        ],
        in_specs=vmem(4) + anywhere(7),
        out_specs=vmem(4),
        scratch_shapes=[
            pltpu.VMEM((2, HALF, WIDTH), BF),
            pltpu.VMEM((2 * HALF, WIDTH), F32),
            pltpu.VMEM((2, 4, 2 * HALF, HEAD_DIM), F32),
            pltpu.VMEM((1024, LOCAL), BF),
            pltpu.SemaphoreType.DMA((4,)),
            pltpu.VMEM((WIDTH, cols), BF),
            pltpu.SemaphoreType.DMA((3,)),
            pltpu.VMEM((2, 4, 8, 16, cols), BF),
            pltpu.VMEM((2, 4, 2 * HALF, cols), BF),
            pltpu.VMEM((8, WIDTH), F32),
            pltpu.VMEM((8, WIDTH), F32),
            pltpu.VMEM((8, WIDTH), F32),
        ]
        + scatter_scratch(cols)
        + [
            pltpu.VMEM((2, 1024, LOCAL), BF),
            pltpu.VMEM((LOCAL, 1024), BF),
            pltpu.VMEM((8, 2, 192, 4 * LOCAL), BF),
            pltpu.VMEM((8, 192, 4 * LOCAL), BF),
            pltpu.VMEM((2, 2, 96, 4 * LOCAL), BF),
            pltpu.VMEM((2, 2, 2, 96, 4 * LOCAL), BF),
            pltpu.VMEM((192, 4 * LOCAL), BF),
            pltpu.SemaphoreType.DMA((2,)),
            pltpu.SemaphoreType.DMA((8,)),
            pltpu.SemaphoreType.DMA((8,)),
            pltpu.SemaphoreType.DMA((2, 2)),
            pltpu.SemaphoreType.DMA((2, 2)),
            pltpu.SemaphoreType.DMA((2, 2, 2)),
            pltpu.SemaphoreType.DMA((2, 2, 2)),
            pltpu.SemaphoreType.DMA,
            pltpu.SemaphoreType.DMA,
        ]
        + [
            pltpu.VMEM((8, 8, LOCAL), F32),
            pltpu.VMEM((16, 8, LOCAL), F32),
            pltpu.VMEM((8, LOCAL), F32),
            pltpu.SemaphoreType.DMA((8,)),
            pltpu.SemaphoreType.DMA,
            pltpu.SemaphoreType.DMA((16,)),
            pltpu.SemaphoreType.DMA,
            pltpu.SemaphoreType.DMA((8,)),
            pltpu.SemaphoreType.DMA,
        ],
        compiler_params=pltpu.CompilerParams(
            collective_id=1, has_side_effects=True, vmem_limit_bytes=VMEM_BYTES
        ),
        cost_estimate=pl.CostEstimate(
            flops=2 * 1024 * WIDTH * 7 * LOCAL, bytes_accessed=50_000_000, transcendentals=0
        ),
        name="rear",
    )(gate_rows, scale, qkv, grad, hidden, diff, factors, attended, w_qkv, modded, up_all)


def hand_over_kernel(hidden, qkv, out, totals, to_hidden, to_qkv, to_out, *to_rows):
    to_hidden[...] = hidden[...]
    to_qkv[...] = qkv[...]
    to_out[...] = out[...]
    for i, ref in enumerate(to_rows):
        ref[...] = totals[i]


def hand_over(hidden, qkv, out, totals):
    row = jax.ShapeDtypeStruct((WIDTH,), F32)
    return pl.pallas_call(
        hand_over_kernel,
        out_shape=[
            jax.ShapeDtypeStruct(hidden.shape, BF),
            jax.ShapeDtypeStruct(qkv.shape, BF),
            jax.ShapeDtypeStruct(out.shape, BF),
            row,
            row,
            row,
        ],
        in_specs=vmem(4),
        out_specs=vmem(6),
        compiler_params=pltpu.CompilerParams(vmem_limit_bytes=VMEM_BYTES),
        name="hand_over",
    )(hidden, qkv, out, totals)


def shards(hidden_states, teacher, mod_scale, mod_shift, out_gate, w_qkv, w_out):
    scale = mod_scale.reshape(1, WIDTH)
    modded, up_all, qkv, factors, attended, diff, grad_att, gate_rows = front(
        hidden_states,
        teacher,
        scale,
        mod_shift.reshape(1, WIDTH),
        out_gate.reshape(1, WIDTH),
        w_qkv,
        w_out,
    )
    results = rear(
        hidden_states,
        diff,
        gate_rows,
        scale,
        qkv,
        grad_att,
        factors,
        attended.reshape(1024, LOCAL),
        w_qkv,
        modded.reshape(1024, WIDTH),
        up_all.reshape(1024, WIDTH),
    )
    grad_hidden, qkv_grad, out_grad, *sums = hand_over(*results)
    return (grad_hidden, qkv_grad, out_grad.T, *sums)


def solution(mesh):
    in_specs = (
        P("frame", "fsdp", None),
        P("frame", "fsdp", None),
        P(),
        P(),
        P(),
        P(None, None, "fsdp"),
        P("fsdp", None),
    )
    out_specs = (
        P("frame", "fsdp", None),
        P(None, "frame", "fsdp"),
        P("fsdp", "frame"),
        P(),
        P(),
        P(),
    )
    return jax.shard_map(shards, mesh=mesh, in_specs=in_specs, out_specs=out_specs, check_vma=False)
```
